32 devices in a mesh: seq: 8 (over y, x, core), wa: 4 (over z).
Axes of the slice: x: 2, y: 2, z: 4, core: 2. Of those that a mesh axis runs over, the one named last changes fastest.
Arguments:
- x_in: float32 [2048, 1024], P('seq'), may hold values from -6 to 6
- d_out: float32 [2048, 1024], P('seq'), may hold values from -6 to 6
- segment_ids: int32 [2048], replicated, may hold values from 0 to 3, never falling along the last dimension, each value on 1 to 1536 neighbouring positions
- norm_gains: float32 [2, 2, 1024], replicated, may hold values from 0.5 to 1.5
- w_zx: bfloat16 [2, 1024, 2, 1536], P(None, None, None, 'wa'), may hold values from -0.1875 to 0.1875
- w_bc: bfloat16 [2, 1024, 256], replicated, may hold values from -0.1875 to 0.1875
- w_dt: bfloat16 [2, 1024, 24], P(None, None, 'wa'), may hold values from -0.1875 to 0.1875
- conv_x: float32 [2, 5, 1536], P(None, None, 'wa'), may hold values from -4 to 4
- conv_bc: float32 [2, 5, 256], replicated, may hold values from -4 to 4
- dt_bias: float32 [2, 24], P(None, 'wa'), may hold values from -5 to 1
- a_log: float32 [2, 24], P(None, 'wa'), may hold values from -9 to 1
- d_skip: float32 [2, 24], P(None, 'wa'), may hold values from 0 to 4
- w_out: bfloat16 [2, 1536, 1024], P(None, 'wa'), may hold values from -0.15625 to 0.15625
- w_q: bfloat16 [2, 1024, 512], P(None, None, 'wa'), may hold values from -0.1875 to 0.1875
- key_value_weight: bfloat16 [2, 1024, 2, 128], replicated, may hold values from -0.1875 to 0.1875
- w_ao: bfloat16 [2, 512, 1024], P(None, 'wa'), may hold values from -1 to 1
- w_gu: bfloat16 [2, 1024, 2, 2048], P(None, None, None, 'wa'), may hold values from -0.1875 to 0.1875
- w_down: bfloat16 [2, 2048, 1024], P(None, 'wa'), may hold values from -0.125 to 0.125
Outputs:
- x_out: float32 [2048, 1024], P('seq')
- d_x: float32 [2048, 1024], P('seq')
- g_norm_first: float32 [2, 1024], replicated
- g_norm_second: float32 [2, 1024], replicated
- g_w_zx: float32 [2, 1024, 2, 1536], P(None, 'seq', None, 'wa')
- g_w_bc: float32 [2, 1024, 256], P(None, 'seq')
- g_w_dt: float32 [2, 1024, 24], P(None, 'seq', 'wa')
- g_conv_x: float32 [2, 5, 1536], P(None, None, 'wa')
- g_conv_bc: float32 [2, 5, 256], replicated
- g_dt_bias: float32 [2, 24], P(None, 'wa')
- g_a_log: float32 [2, 24], P(None, 'wa')
- g_d_skip: float32 [2, 24], P(None, 'wa')
- g_w_out: float32 [2, 1536, 1024], P(None, 'wa', 'seq')
- g_w_q: float32 [2, 1024, 512], P(None, 'seq', 'wa')
- g_w_kv: float32 [2, 1024, 2, 128], P(None, 'seq')
- g_w_ao: float32 [2, 512, 1024], P(None, 'wa', 'seq')
- g_w_gu: float32 [2, 1024, 2, 2048], P(None, 'seq', None, 'wa')
- g_w_down: float32 [2, 2048, 1024], P(None, 'wa', 'seq')
The draws below stay inside these ranges and needn't reach their ends.
Inputs may be any that keep to these rules, and one draw needn't show every extreme that they name: `segment_ids`: segment numbers never fall along the tokens; each of the 4 documents has 1 to 1536 tokens and one has exactly 1536.
All inputs are finite; a program needn't handle non-finite values.
Results may differ from the reference program's by a relative error of at most 0.025.
Values may be sent and summed in bfloat16 or wider, within the bound.
No kernel may reach another device: no remote copies, remote signals or barrier semaphores. Data moves between devices by JAX's collectives and lax.ppermute only.
A program may use at most 192 MiB of HBM per device.

```python
import math
import jax
import jax.numpy as jnp
import numpy as np
from jax import lax

MODEL_WIDTH = 1024
HM = 24
HEAD_SIZE = 64
NS = 128
KC = 4
QUERY_HEADS = 8
KEY_VALUE_HEADS = 2
FF = 2048
LAYER_COUNT = 2
SEGS = 4
TOKENS_PER_SHARD = 256
DI = 1536
TOKEN_TOTAL = 2048
SEG_MOST = 1536
N_SEQ = 8


def draw_dt_bias(key, part):
    spread_values = jax.random.uniform(jax.random.fold_in(key, 411), (LAYER_COUNT, HM), jnp.float32, -1.0, 1.0)
    return spread_values + (math.log(7.0 / math.sqrt(SEG_MOST)) - 0.5)


def draw_a_log(key, part):
    spread_values = jax.random.uniform(jax.random.fold_in(key, 523), (LAYER_COUNT, HM), jnp.float32, -3.5, 2.0)
    return spread_values - 0.5 * math.log(SEG_MOST)


def levels(key, shape, cuts, low, largest):
    loudness = 1.0
    for axis_at, parts in cuts:
        draws = jax.random.uniform(jax.random.fold_in(jax.random.fold_in(key, 6), axis_at), (parts,), jnp.float32, low / len(cuts), largest / len(cuts))
        loudness = loudness * jnp.repeat(jnp.exp(draws), shape[axis_at] // parts).reshape((-1,) + (1,) * (len(shape) - 1 - axis_at))
    return loudness


def split_up(amount, total, bound, lean):
    weights = [(1 << 20) // math.isqrt(standing ** lean) + 1 for standing in range(2, amount + 1)]
    spare, holding = total - bound - (amount - 1), [1] * (amount - 1)
    while spare > 0:
        free = [i for i in range(amount - 1) if holding[i] < bound]
        mass, left = sum([weights[i] for i in free]), spare
        for i in free:
            more = min(bound - holding[i], max(1, left * weights[i] // mass), spare)
            holding[i] = holding[i] + more
            spare = spare - more
    return np.array([bound] + holding)


def ragged(rng, count, total, reach, lean):
    if count == 2:
        one = jax.random.randint(rng, (), max(1, total - reach), min(reach, total - 1) + 1)
        return jnp.stack([one, total - one])
    sizes = jnp.asarray(split_up(count, total, reach, lean), jnp.int32)
    couples = (count - 1) // 2
    donor, sink = sizes[1:1 + 2 * couples:2], sizes[2:2 + 2 * couples:2]
    margin = jnp.minimum(donor - 1, reach - sink)
    shifted = jax.random.randint(jax.random.fold_in(rng, 1), (couples,), 0, 1 << 20) % (margin + 1)
    sizes = sizes.at[1:1 + 2 * couples:2].set(donor - shifted).at[2:2 + 2 * couples:2].set(sink + shifted)
    return sizes[jax.random.permutation(jax.random.fold_in(rng, 2), count)]


def centred(stream_key, shape, deviation, bound, cuts=(), kind=jnp.bfloat16):
    drawn = jax.random.normal(stream_key, shape, jnp.float32) * deviation
    if len(cuts) > 0:
        drawn = levels(stream_key, shape, cuts, -0.22, 0.18) * drawn
    return jnp.clip(drawn, min=-bound, max=bound).astype(kind)


def setup_inputs(seed: int = 0) -> dict:
    arg_keys = jax.random.split(jax.random.key(seed), 19)
    return {
        "x_in": centred(arg_keys[0], (TOKEN_TOTAL, MODEL_WIDTH), 1.0, 6.0, ((0, 8),), jnp.float32),
        "d_out": centred(arg_keys[1], (TOKEN_TOTAL, MODEL_WIDTH), 1.0, 6.0, ((0, 8),), jnp.float32),
        "segment_ids": jnp.searchsorted(jnp.cumsum(ragged(arg_keys[2], SEGS, TOKEN_TOTAL, SEG_MOST, 0)), jnp.arange(TOKEN_TOTAL), side="right").astype(jnp.int32),
        "norm_gains": jnp.clip(1.0 + 0.1 * jax.random.normal(arg_keys[3], (LAYER_COUNT, 2, MODEL_WIDTH), jnp.float32), 0.5, 1.5),
        "w_zx": centred(arg_keys[4], (LAYER_COUNT, MODEL_WIDTH, 2, DI), MODEL_WIDTH ** -0.5, 0.1875, ((3, 4),)),
        "w_bc": centred(arg_keys[5], (LAYER_COUNT, MODEL_WIDTH, 2 * NS), MODEL_WIDTH ** -0.5, 0.1875),
        "w_dt": centred(arg_keys[6], (LAYER_COUNT, MODEL_WIDTH, HM), MODEL_WIDTH ** -0.5, 0.1875, ((2, 4),)),
        "conv_x": centred(arg_keys[7], (LAYER_COUNT, KC + 1, DI), 1.0, 4.0, ((2, 4),), jnp.float32),
        "conv_bc": centred(arg_keys[8], (LAYER_COUNT, KC + 1, 2 * NS), 1.0, 4.0, (), jnp.float32),
        "dt_bias": draw_dt_bias(jax.random.fold_in(arg_keys[18], 71), 0),
        "a_log": draw_a_log(jax.random.fold_in(arg_keys[18], 71), 0),
        "d_skip": jnp.clip(4.0 * jax.random.uniform(arg_keys[11], (LAYER_COUNT, HM), jnp.float32) ** levels(arg_keys[11], (LAYER_COUNT, HM), ((1, 4),), -0.2, 0.2), 0.0, 4.0),
        "w_out": centred(arg_keys[12], (LAYER_COUNT, DI, MODEL_WIDTH), DI ** -0.5, 0.15625, ((1, 4),)),
        "w_q": centred(arg_keys[13], (LAYER_COUNT, MODEL_WIDTH, QUERY_HEADS * HEAD_SIZE), MODEL_WIDTH ** -0.5, 0.1875, ((2, 4),)),
        "key_value_weight": centred(arg_keys[14], (LAYER_COUNT, MODEL_WIDTH, 2, KEY_VALUE_HEADS * HEAD_SIZE), MODEL_WIDTH ** -0.5, 0.1875),
        "w_ao": centred(arg_keys[15], (LAYER_COUNT, QUERY_HEADS * HEAD_SIZE, MODEL_WIDTH), (QUERY_HEADS * HEAD_SIZE // 16) ** -0.5, 1.0, ((1, 4),)),
        "w_gu": centred(arg_keys[16], (LAYER_COUNT, MODEL_WIDTH, 2, FF), MODEL_WIDTH ** -0.5, 0.1875, ((3, 4),)),
        "w_down": centred(arg_keys[17], (LAYER_COUNT, FF, MODEL_WIDTH), FF ** -0.5, 0.125, ((1, 4),)),
    }


eps = 1e-05
theta = 10000.0
neg_big = -1e+30

def norm_apply(values, gain):
    return values * lax.rsqrt(lax.optimization_barrier(jnp.mean(values * values, axis=-1, keepdims=True)) + eps) * gain

def swiglu(gate_part, up_part):
    return jax.nn.silu(gate_part) * up_part

def rotate(tensor, position):
    half_width = tensor.shape[-1] // 2
    frequency = jnp.exp(jnp.arange(half_width, dtype=jnp.float32) * (-math.log(theta) / half_width))
    angles = position[:, None] * frequency[None, :]
    cosine = jnp.cos(angles)[:, None, :]
    sine_part = jnp.sin(angles)[:, None, :]
    first_half = tensor[..., :half_width]
    second = tensor[..., half_width:]
    return jnp.concatenate([first_half * cosine - second * sine_part, second * cosine + first_half * sine_part], axis=-1)

def rotate_back(grad_in, like, position):
    return jax.vjp(lambda tensor: rotate(tensor, position), like)[1](grad_in)[0]

def mixer_front(inputs, edge_rows, conv_w, dt_raw, dt_bias, a_log, d_skip, seg_here, seg_edge, seg_before):
    length = inputs.shape[0]
    head_count = dt_raw.shape[1]
    inner_width = head_count * HEAD_SIZE
    padded = jnp.concatenate([edge_rows, inputs], axis=0)
    seg_full = jnp.concatenate([seg_edge, seg_here])
    conv_sum = jnp.broadcast_to(conv_w[KC], inputs.shape)
    for offset in range(KC):
        usable = (seg_full[offset:offset + length] == seg_here).astype(jnp.float32)
        conv_sum = conv_sum + conv_w[offset] * padded[offset:offset + length] * usable[:, None]
    active = jax.nn.silu(conv_sum)
    x_heads = active[:, :inner_width].reshape(length, head_count, HEAD_SIZE)
    b_mat = active[:, inner_width:inner_width + NS]
    c_mat = active[:, inner_width + NS:]
    dt_val = jax.nn.softplus(dt_raw + dt_bias)
    log_decay = -dt_val * jnp.exp(a_log)
    cumulative = jnp.cumsum(log_decay, axis=0)
    places = jnp.arange(length)
    allowed = (seg_here[:, None] == seg_here[None, :]) & (places[None, :] <= places[:, None])
    differences = cumulative.T[:, :, None] - cumulative.T[:, None, :]
    decay_pair = jnp.exp(jnp.where(allowed[None], differences, neg_big))
    intersection = jnp.dot(c_mat, b_mat.T, precision=lax.Precision.HIGHEST)
    x_scaled = x_heads * dt_val[:, :, None]
    within = jnp.einsum('hts,shp->thp', decay_pair * intersection[None], x_scaled, precision=lax.Precision.HIGHEST)
    y_local = within + d_skip[None, :, None] * x_heads
    inside = (seg_here == seg_before).astype(jnp.float32)
    decay_in = jnp.exp(cumulative) * inside[:, None]
    same_last = (seg_here == seg_here[length - 1])[:, None]
    to_last = jnp.exp(jnp.where(same_last, cumulative[length - 1][None, :] - cumulative, neg_big))
    block_decay = jnp.exp(cumulative[length - 1]) * inside[length - 1]
    local_state = jnp.einsum('shp,sn->hpn', x_scaled * to_last[:, :, None], b_mat, precision=lax.Precision.HIGHEST)
    return (y_local, decay_in, c_mat, block_decay, local_state)

def mixer_back(y_local, decay_in, c_mat, state_in, gate_raw):
    inflow = jnp.einsum('tn,hpn->thp', c_mat, state_in, precision=lax.Precision.HIGHEST) * decay_in[:, :, None]
    mixed_y = (y_local + inflow).reshape(y_local.shape[0], -1)
    return mixed_y * jax.nn.silu(gate_raw)

def mixer_all(inputs, edge_rows, conv_w, dt_raw, dt_bias, a_log, d_skip, gate_raw, state_in, seg_here, seg_edge, seg_before):
    front = mixer_front(inputs, edge_rows, conv_w, dt_raw, dt_bias, a_log, d_skip, seg_here, seg_edge, seg_before)
    return (mixer_back(front[0], front[1], front[2], state_in, gate_raw), front[3], front[4])

def wide(values):
    return lax.optimization_barrier(values.astype(jnp.bfloat16)).astype(jnp.float32)

def reference(x_in, d_out, segment_ids, norm_gains, w_zx, w_bc, w_dt, conv_x, conv_bc, dt_bias, a_log, d_skip, w_out, w_q, key_value_weight, w_ao, w_gu, w_down):
    block_list = N_SEQ
    query_group_width = QUERY_HEADS // KEY_VALUE_HEADS
    score_scale = 1.0 / math.sqrt(HEAD_SIZE)
    width_mix = DI + 2 * NS
    positions = jnp.arange(TOKEN_TOTAL, dtype=jnp.int32)
    pos_float = positions.astype(jnp.float32)
    seg_padded = jnp.concatenate([jnp.full((KC - 1,), -1, jnp.int32), segment_ids])
    edge_index = (jnp.arange(block_list, dtype=jnp.int32) * TOKENS_PER_SHARD)[:, None] + jnp.arange(KC - 1, dtype=jnp.int32)[None, :]
    seg_edges = seg_padded[edge_index]
    seg_blocks = segment_ids.reshape(block_list, TOKENS_PER_SHARD)
    pos_blocks = positions.reshape(block_list, TOKENS_PER_SHARD)

    def grouped_rows(each_token_cost):
        return each_token_cost.reshape(block_list, TOKENS_PER_SHARD, QUERY_HEADS, HEAD_SIZE).transpose(0, 2, 1, 3).reshape(block_list, KEY_VALUE_HEADS, query_group_width * TOKENS_PER_SHARD, HEAD_SIZE)

    def token_rows(grouped):
        return grouped.reshape(block_list, QUERY_HEADS, TOKENS_PER_SHARD, HEAD_SIZE).transpose(0, 2, 1, 3).reshape(TOKEN_TOTAL, QUERY_HEADS, HEAD_SIZE)

    def masks(pos_blk, seg_blk):
        q_pos = jnp.tile(pos_blk, query_group_width)
        q_seg = jnp.tile(seg_blk, query_group_width)
        return (positions[None, :] <= q_pos[:, None]) & (segment_ids[None, :] == q_seg[:, None])
    hidden = x_in
    saved = []
    for layer_number in range(LAYER_COUNT):
        gains = norm_gains[layer_number]
        wzx_flat = w_zx[layer_number].reshape(MODEL_WIDTH, 2 * DI)
        key_value_weight_flat = key_value_weight[layer_number].reshape(MODEL_WIDTH, 2 * KEY_VALUE_HEADS * HEAD_SIZE)
        normalized_input = norm_apply(hidden, gains[0]).astype(jnp.bfloat16)
        zx_raw = jnp.dot(normalized_input, wzx_flat, preferred_element_type=jnp.float32)
        gate_raw = zx_raw[:, :DI]
        bc_raw = jnp.dot(normalized_input, w_bc[layer_number], preferred_element_type=jnp.float32)
        dt_raw = jnp.dot(normalized_input, w_dt[layer_number], preferred_element_type=jnp.float32)
        mix_in = jnp.concatenate([zx_raw[:, DI:], bc_raw], axis=1)
        conv_w = jnp.concatenate([conv_x[layer_number], conv_bc[layer_number]], axis=1)
        dtb = dt_bias[layer_number]
        alg = a_log[layer_number]
        dsk = d_skip[layer_number]

        def mamba_step(carry, slices):
            state_in, edge_rows = carry
            mix_blk, dt_blk, gate_blk, seg_blk, edge_seg = slices
            front = mixer_front(mix_blk, edge_rows, conv_w, dt_blk, dtb, alg, dsk, seg_blk, edge_seg, edge_seg[KC - 2])
            gated_blk = mixer_back(front[0], front[1], front[2], state_in, gate_blk)
            state_out = front[3][:, None, None] * state_in + front[4]
            return ((state_out, mix_blk[TOKENS_PER_SHARD - (KC - 1):]), (gated_blk, state_in, edge_rows))
        start_carry = (jnp.zeros((HM, HEAD_SIZE, NS), jnp.float32), jnp.zeros((KC - 1, width_mix), jnp.float32))
        mamba_xs = (mix_in.reshape(block_list, TOKENS_PER_SHARD, width_mix), dt_raw.reshape(block_list, TOKENS_PER_SHARD, HM), gate_raw.reshape(block_list, TOKENS_PER_SHARD, DI), seg_blocks, seg_edges)
        gated_all, states_in, edges_all = lax.scan(mamba_step, start_carry, mamba_xs)[1]
        gated = gated_all.reshape(TOKEN_TOTAL, DI).astype(jnp.bfloat16)
        q_raw = jnp.dot(normalized_input, w_q[layer_number], preferred_element_type=jnp.float32).reshape(TOKEN_TOTAL, QUERY_HEADS, HEAD_SIZE)
        queries = rotate(q_raw, pos_float).astype(jnp.bfloat16)
        key_value_unrotated = jnp.dot(normalized_input, key_value_weight_flat, preferred_element_type=jnp.float32)
        key_unrotated = key_value_unrotated[:, :KEY_VALUE_HEADS * HEAD_SIZE].reshape(TOKEN_TOTAL, KEY_VALUE_HEADS, HEAD_SIZE)
        key_rows = rotate(key_unrotated, pos_float).astype(jnp.bfloat16)
        value_row_list = key_value_unrotated[:, KEY_VALUE_HEADS * HEAD_SIZE:].reshape(TOKEN_TOTAL, KEY_VALUE_HEADS, HEAD_SIZE).astype(jnp.bfloat16)
        keys_t = key_rows.transpose(1, 0, 2).astype(jnp.float32)
        values_t = value_row_list.transpose(1, 0, 2).astype(jnp.float32)
        q_grouped = grouped_rows(queries)

        def attend_step(carry, slices):
            q_blk, pos_blk, seg_blk = slices
            allowed = masks(pos_blk, seg_blk)[None]
            scores = jnp.einsum('grd,gkd->grk', q_blk.astype(jnp.float32), keys_t, precision=lax.Precision.HIGHEST) * score_scale
            row_max = lax.optimization_barrier(jnp.max(jnp.where(allowed, scores, neg_big), axis=2))
            weights = jnp.where(allowed, jnp.exp(scores - row_max[:, :, None]), 0.0)
            row_total = lax.optimization_barrier(jnp.sum(weights, axis=2))
            attn_blk = jnp.einsum('grk,gkd->grd', weights, values_t, precision=lax.Precision.HIGHEST) / row_total[:, :, None]
            return (carry, (attn_blk, row_max + jnp.log(row_total)))
        attn_g, lse_g = lax.scan(attend_step, jnp.zeros((), jnp.float32), (q_grouped, pos_blocks, seg_blocks))[1]
        attn_flat = token_rows(attn_g).reshape(TOKEN_TOTAL, QUERY_HEADS * HEAD_SIZE).astype(jnp.bfloat16)
        mamba_part = jnp.dot(gated, w_out[layer_number], preferred_element_type=jnp.float32)
        attn_part = jnp.dot(attn_flat, w_ao[layer_number], preferred_element_type=jnp.float32)
        mixed = hidden + (mamba_part + attn_part)
        normed_two = norm_apply(mixed, gains[1]).astype(jnp.bfloat16)
        gate_up = jnp.dot(normed_two, w_gu[layer_number].reshape(MODEL_WIDTH, 2 * FF), preferred_element_type=jnp.float32)
        act_ff = swiglu(gate_up[:, :FF], gate_up[:, FF:]).astype(jnp.bfloat16)
        output = mixed + jnp.dot(act_ff, w_down[layer_number], preferred_element_type=jnp.float32)
        saved.append((hidden, normalized_input, mix_in, gate_raw, dt_raw, states_in, edges_all, gated, q_raw, key_unrotated, q_grouped, keys_t, values_t, attn_g, lse_g, attn_flat, mixed, normed_two, gate_up, act_ff))
        hidden = output
    x_out = hidden
    grad = d_out
    per_layer = [None] * LAYER_COUNT
    for layer_number in reversed(range(LAYER_COUNT)):
        hidden_in, normalized_input, mix_in, gate_raw, dt_raw, states_in, edges_all, gated, q_raw, key_unrotated, q_grouped, keys_t, values_t, attn_g, lse_g, attn_flat, mixed, normed_two, gate_up, act_ff = saved[layer_number]
        gains = norm_gains[layer_number]
        wzx_flat = w_zx[layer_number].reshape(MODEL_WIDTH, 2 * DI)
        key_value_weight_flat = key_value_weight[layer_number].reshape(MODEL_WIDTH, 2 * KEY_VALUE_HEADS * HEAD_SIZE)
        wgu_flat = w_gu[layer_number].reshape(MODEL_WIDTH, 2 * FF)
        conv_w = jnp.concatenate([conv_x[layer_number], conv_bc[layer_number]], axis=1)
        dtb = dt_bias[layer_number]
        alg = a_log[layer_number]
        dsk = d_skip[layer_number]
        grad_b = grad.astype(jnp.bfloat16)
        g_down = jnp.dot(act_ff.T, grad_b, preferred_element_type=jnp.float32)
        d_act = jnp.dot(grad_b, w_down[layer_number].T, preferred_element_type=jnp.float32)
        d_gate, d_up = jax.vjp(swiglu, gate_up[:, :FF], gate_up[:, FF:])[1](d_act)
        d_gu = jnp.concatenate([d_gate, d_up], axis=1).astype(jnp.bfloat16)
        g_gu = jnp.dot(normed_two.T, d_gu, preferred_element_type=jnp.float32).reshape(MODEL_WIDTH, 2, FF)
        d_normed_two = jnp.dot(d_gu, wgu_flat.T, preferred_element_type=jnp.float32)
        d_mixed_n, g_gain_two = jax.vjp(norm_apply, mixed, gains[1])[1](d_normed_two)
        d_mixed = grad + d_mixed_n
        mixed_b = d_mixed.astype(jnp.bfloat16)
        g_out = jnp.dot(gated.T, mixed_b, preferred_element_type=jnp.float32)
        d_gated = jnp.dot(mixed_b, w_out[layer_number].T, preferred_element_type=jnp.float32)
        g_ao = jnp.dot(attn_flat.T, mixed_b, preferred_element_type=jnp.float32)
        d_attn = jnp.dot(mixed_b, w_ao[layer_number].T, preferred_element_type=jnp.float32)
        d_grouped = grouped_rows(d_attn.reshape(TOKEN_TOTAL, QUERY_HEADS, HEAD_SIZE))

        def attend_back(carry, slices):
            key_acc, value_accumulator = carry
            q_blk, d_blk, out_blk, lse_blk, pos_blk, seg_blk = slices
            allowed = masks(pos_blk, seg_blk)[None]
            q_wide = q_blk.astype(jnp.float32)
            delta_rows = lax.optimization_barrier(jnp.sum(d_blk * out_blk, axis=2))
            d_wide = wide(d_blk)
            scores = jnp.einsum('grd,gkd->grk', q_wide, keys_t, precision=lax.Precision.HIGHEST) * score_scale
            probs = jnp.where(allowed, jnp.exp(scores - lse_blk[:, :, None]), 0.0)
            value_accumulator = value_accumulator + jnp.einsum('grk,grd->gkd', wide(probs), d_wide, precision=lax.Precision.HIGHEST)
            d_probs = jnp.einsum('grd,gkd->grk', d_wide, values_t, precision=lax.Precision.HIGHEST)
            d_scores = wide(probs * (d_probs - delta_rows[:, :, None]))
            d_query = jnp.einsum('grk,gkd->grd', d_scores, keys_t, precision=lax.Precision.HIGHEST) * score_scale
            key_acc = key_acc + jnp.einsum('grk,grd->gkd', d_scores, q_wide, precision=lax.Precision.HIGHEST) * score_scale
            return ((key_acc, value_accumulator), d_query)
        empty_key_value = jnp.zeros((KEY_VALUE_HEADS, TOKEN_TOTAL, HEAD_SIZE), jnp.float32)
        (key_acc, value_accumulator), d_query_g = lax.scan(attend_back, (empty_key_value, empty_key_value), (q_grouped, d_grouped, attn_g, lse_g, pos_blocks, seg_blocks))
        d_q_raw = rotate_back(token_rows(d_query_g), q_raw, pos_float)
        grad_key_unrotated = rotate_back(key_acc.transpose(1, 0, 2), key_unrotated, pos_float)
        dq_b = d_q_raw.reshape(TOKEN_TOTAL, QUERY_HEADS * HEAD_SIZE).astype(jnp.bfloat16)
        grad_key_value_block = jnp.concatenate([grad_key_unrotated.reshape(TOKEN_TOTAL, KEY_VALUE_HEADS * HEAD_SIZE), value_accumulator.transpose(1, 0, 2).reshape(TOKEN_TOTAL, KEY_VALUE_HEADS * HEAD_SIZE)], axis=1).astype(jnp.bfloat16)

        def mamba_back(carry, slices):
            later_grad, edge_grad = carry
            mix_blk, dt_blk, gate_blk, seg_blk, edge_seg, state_in, edge_rows, d_gated_blk = slices

            def whole(inputs, edges, conv_part, dt_part, bias_part, log_part, skip_part, gate_part, state_part):
                return mixer_all(inputs, edges, conv_part, dt_part, bias_part, log_part, skip_part, gate_part, state_part, seg_blk, edge_seg, edge_seg[KC - 2])
            primal_out, pull_back = jax.vjp(whole, mix_blk, edge_rows, conv_w, dt_blk, dtb, alg, dsk, gate_blk, state_in)
            d_decay = lax.optimization_barrier(jnp.sum(later_grad * state_in, axis=(1, 2)))
            grad_list = pull_back((d_gated_blk, d_decay, later_grad))
            d_mix = grad_list[0] + jnp.concatenate([jnp.zeros((TOKENS_PER_SHARD - (KC - 1), width_mix), jnp.float32), edge_grad], axis=0)
            new_grad = grad_list[8] + primal_out[1][:, None, None] * later_grad
            return ((new_grad, grad_list[1]), (d_mix, grad_list[3], grad_list[7], grad_list[2], grad_list[4], grad_list[5], grad_list[6]))
        back_carry = (jnp.zeros((HM, HEAD_SIZE, NS), jnp.float32), jnp.zeros((KC - 1, width_mix), jnp.float32))
        back_xs = (mix_in.reshape(block_list, TOKENS_PER_SHARD, width_mix), dt_raw.reshape(block_list, TOKENS_PER_SHARD, HM), gate_raw.reshape(block_list, TOKENS_PER_SHARD, DI), seg_blocks, seg_edges, states_in, edges_all, d_gated.reshape(block_list, TOKENS_PER_SHARD, DI))
        d_mix_all, d_dt_all, d_gate_all, conv_all, dtb_all, alog_all, dsk_all = lax.scan(mamba_back, back_carry, back_xs, reverse=True)[1]
        d_mix_flat = d_mix_all.reshape(TOKEN_TOTAL, width_mix)
        g_conv = lax.optimization_barrier(jnp.sum(conv_all, axis=0))
        dzx_b = jnp.concatenate([d_gate_all.reshape(TOKEN_TOTAL, DI), d_mix_flat[:, :DI]], axis=1).astype(jnp.bfloat16)
        dbc_b = d_mix_flat[:, DI:].astype(jnp.bfloat16)
        ddt_b = d_dt_all.reshape(TOKEN_TOTAL, HM).astype(jnp.bfloat16)
        g_zx = jnp.dot(normalized_input.T, dzx_b, preferred_element_type=jnp.float32).reshape(MODEL_WIDTH, 2, DI)
        g_bc = jnp.dot(normalized_input.T, dbc_b, preferred_element_type=jnp.float32)
        g_dt = jnp.dot(normalized_input.T, ddt_b, preferred_element_type=jnp.float32)
        g_q = jnp.dot(normalized_input.T, dq_b, preferred_element_type=jnp.float32)
        grad_key_value = jnp.dot(normalized_input.T, grad_key_value_block, preferred_element_type=jnp.float32).reshape(MODEL_WIDTH, 2, KEY_VALUE_HEADS * HEAD_SIZE)
        d_normed = jnp.dot(dzx_b, wzx_flat.T, preferred_element_type=jnp.float32)
        d_normed = d_normed + jnp.dot(dbc_b, w_bc[layer_number].T, preferred_element_type=jnp.float32)
        d_normed = d_normed + jnp.dot(ddt_b, w_dt[layer_number].T, preferred_element_type=jnp.float32)
        d_normed = d_normed + jnp.dot(dq_b, w_q[layer_number].T, preferred_element_type=jnp.float32)
        d_normed = d_normed + jnp.dot(grad_key_value_block, key_value_weight_flat.T, preferred_element_type=jnp.float32)
        d_hidden_n, g_gain_one = jax.vjp(norm_apply, hidden_in, gains[0])[1](d_normed)
        grad = d_mixed + d_hidden_n
        per_layer[layer_number] = (jnp.stack([g_gain_one, g_gain_two]), g_zx, g_bc, g_dt, g_conv[:, :DI], g_conv[:, DI:], lax.optimization_barrier(jnp.sum(dtb_all, axis=0)), lax.optimization_barrier(jnp.sum(alog_all, axis=0)), lax.optimization_barrier(jnp.sum(dsk_all, axis=0)), g_out, g_q, grad_key_value, g_ao, g_gu, g_down)
    stacked = [jnp.stack([entry_now[member] for entry_now in per_layer]) for member in range(15)]
    return (x_out, grad, stacked[0][:, 0], stacked[0][:, 1], stacked[1], stacked[2], stacked[3], stacked[4], stacked[5], stacked[6], stacked[7], stacked[8], stacked[9], stacked[10], stacked[11], stacked[12], stacked[13], stacked[14])
```

```python
import math

import jax
import jax.numpy as jnp
from jax import lax
from jax.experimental import pallas as pl
from jax.experimental.pallas import tpu as pltpu
from jax.sharding import PartitionSpec as P

MODEL_WIDTH = 1024
HEAD_SIZE = 64
NS = 128
KC = 4
QUERY_HEADS = 8
KEY_VALUE_HEADS = 2
LAYER_COUNT = 2
DIRECT_MOST = 8

eps = 1e-05
theta = 10000.0
neg_big = -1e30
score_scale = 1.0 / math.sqrt(HEAD_SIZE)

BF = jnp.bfloat16
F32 = jnp.float32
HI = lax.Precision.HIGHEST


def mm(a, b):
    return lax.dot_general(
        a.astype(BF), b.astype(BF), (((1,), (0,)), ((), ())), preferred_element_type=F32
    )


def mm_nt(a, b):
    return lax.dot_general(
        a.astype(BF), b.astype(BF), (((1,), (1,)), ((), ())), preferred_element_type=F32
    )


def mm_tn(a, b):
    return lax.dot_general(
        a.astype(BF), b.astype(BF), (((0,), (0,)), ((), ())), preferred_element_type=F32
    )


def mm_hi(a, b):
    return jnp.dot(a, b, precision=HI, preferred_element_type=F32)


def iota(shape, dim):
    return lax.broadcasted_iota(jnp.int32, shape, dim)


def sigmoid(v):
    return 1.0 / (1.0 + jnp.exp(-v))


def from_earlier(block):
    n = lax.axis_size("seq")
    if n <= DIRECT_MOST:
        return [
            lax.ppermute(block, "seq", [(i, i + d) for i in range(n - d)]) for d in range(1, n)
        ]
    here = lax.axis_index("seq")
    every = lax.all_gather(block, "seq")
    return [
        jnp.where(here >= d, every[(here - d) % n], jnp.zeros_like(block)) for d in range(1, n)
    ]


def from_later(block):
    n = lax.axis_size("seq")
    if n <= DIRECT_MOST:
        return [
            lax.ppermute(block, "seq", [(i + d, i) for i in range(n - d)]) for d in range(1, n)
        ]
    here = lax.axis_index("seq")
    every = lax.all_gather(block, "seq")
    return [
        jnp.where(here + d < n, every[(here + d) % n], jnp.zeros_like(block)) for d in range(1, n)
    ]


def to_earlier(blocks):
    n = lax.axis_size("seq")
    if n <= DIRECT_MOST:
        return [
            lax.ppermute(blocks[d - 1], "seq", [(i + d, i) for i in range(n - d)])
            for d in range(1, n)
        ]
    here = lax.axis_index("seq")
    stacked = jnp.stack([jnp.zeros_like(blocks[0])] + list(blocks))
    places = jnp.arange(n)
    placed = jnp.where((places < here)[:, None, None], stacked[(here - places) % n], 0)
    return [lax.psum_scatter(placed, "seq", scatter_dimension=0, tiled=True)[0]]


def scatter_rows(blocks):
    n = lax.axis_size("seq")
    if n <= DIRECT_MOST:
        got = [
            lax.ppermute(blocks[d], "seq", [(i, (i + d) % n) for i in range(n)])
            for d in range(1, n)
        ]
        total = blocks[0].astype(F32)
        for part in got:
            total = total + part.astype(F32)
        return total
    return lax.psum_scatter(blocks[0], "seq", scatter_dimension=0, tiled=True).astype(F32)


def gather_wa(block):
    n = lax.axis_size("wa")
    return [block] + [
        lax.ppermute(block, "wa", [((i + d) % n, i) for i in range(n)]) for d in range(1, n)
    ]


def scatter_wa(blocks):
    n = lax.axis_size("wa")
    return [blocks[0]] + [
        lax.ppermute(blocks[d], "wa", [(i, (i + d) % n) for i in range(n)]) for d in range(1, n)
    ]


def sum_seq(block):
    n = lax.axis_size("seq")
    if n > DIRECT_MOST:
        return lax.psum(block, "seq")
    total = block
    for d in range(1, n):
        total = total + lax.ppermute(block, "seq", [(i, (i + d) % n) for i in range(n)])
    return total


def layer_of(array, layer):
    return (array, layer)


def kernel_call(name, body, outs, args, scratch=(), flops=0, bytes_accessed=0):
    in_specs, arrays = [], []
    for item in args:
        if isinstance(item, tuple):
            array, layer = item
            rest = array.ndim - 1
            spec = pl.BlockSpec(
                (None,) + array.shape[1:], lambda i, layer=layer, rest=rest: (layer,) + (0,) * rest
            )
        else:
            array = item
            if array.ndim == 1:
                spec = pl.BlockSpec(memory_space=pltpu.SMEM)
            else:
                spec = pl.BlockSpec(array.shape, lambda i, rest=array.ndim: (0,) * rest)
        in_specs.append(spec)
        arrays.append(array)
    out_shape = [jax.ShapeDtypeStruct(shape, kind) for shape, kind in outs]
    out_specs = [
        pl.BlockSpec(shape, lambda i, rest=len(shape): (0,) * rest) for shape, kind in outs
    ]
    if not bytes_accessed:
        bytes_accessed = sum(math.prod(s) * jnp.dtype(k).itemsize for s, k in outs) + sum(
            a.size * a.dtype.itemsize for a in arrays
        )
    return pl.pallas_call(
        body,
        grid=(1,),
        in_specs=in_specs,
        out_specs=out_specs,
        out_shape=out_shape,
        scratch_shapes=list(scratch),
        compiler_params=pltpu.CompilerParams(vmem_limit_bytes=48 * 1024 * 1024),
        cost_estimate=pl.CostEstimate(
            flops=flops, bytes_accessed=bytes_accessed, transcendentals=0
        ),
        name=name,
    )(*arrays)


def ordered(me_ref, parts, nat_ref):
    n = len(parts)
    rows = parts[0].shape[0]
    for d in range(n):
        at = pl.multiple_of(lax.rem(me_ref[0] + d, n) * rows, rows)
        nat_ref[pl.ds(at, rows), :] = parts[d][...]


def rotated(me_ref, nat_ref, blocks):
    n = len(blocks)
    rows = blocks[0].shape[0]
    for d in range(n):
        at = pl.multiple_of(lax.rem(me_ref[0] + d, n) * rows, rows)
        blocks[d][...] = nat_ref[pl.ds(at, rows), :].astype(blocks[d].dtype)


def halves_swapped(v):
    width = v.shape[1]
    half = HEAD_SIZE // 2
    first = iota(v.shape, 1) % HEAD_SIZE < half
    return jnp.where(first, pltpu.roll(v, width - half, 1), pltpu.roll(v, half, 1))


def expand(v, width):
    k = v.shape[1]
    pick = (iota((k, width), 1) // HEAD_SIZE == iota((k, width), 0)).astype(F32)
    return mm_hi(v, pick)


def head_sum(v):
    width = v.shape[1]
    pick = (iota((width, 128), 0) // HEAD_SIZE == iota((width, 128), 1)).astype(F32)
    return mm_hi(v, pick)


def decay_rows(block_decay):
    high = block_decay.astype(BF).astype(F32)
    low = block_decay - high
    row = iota((16, 128), 0)
    return jnp.where(row == 0, high, jnp.where(row == 1, low, 0.0)).astype(BF)


def fold_states(packs, inner):
    heads = inner // HEAD_SIZE
    state = jnp.zeros((inner, NS), F32)
    for pack in reversed(packs):
        tail = pack[inner : inner + 16, :].astype(F32)
        decay = tail[0:1, :] + tail[1:2, :]
        full = jnp.concatenate(
            [jnp.broadcast_to(decay[:, h : h + 1], (HEAD_SIZE, NS)) for h in range(heads)], axis=0
        )
        state = state * full + pack[:inner, :].astype(F32)
    return state


def norm_first(hidden, gain):
    rows, width = hidden.shape

    def body(h_ref, g_ref, n_ref):
        h = h_ref[...]
        scale = lax.rsqrt(jnp.mean(h * h, axis=-1, keepdims=True) + eps)
        n_ref[...] = (h * scale * g_ref[...]).astype(BF)

    return kernel_call("norm_first", body, [((rows, width), BF)], [hidden, gain])[0]


def norm_step(parts, hidden, gain):
    rows, width = hidden.shape
    n = len(parts)

    def body(*refs):
        h_ref, g_ref, out_ref, n_ref = refs[n:]
        total = refs[0][...]
        for part in refs[1:n]:
            total = total + part[...].astype(F32)
        h = h_ref[...] + total
        out_ref[...] = h
        scale = lax.rsqrt(jnp.mean(h * h, axis=-1, keepdims=True) + eps)
        n_ref[...] = (h * scale * g_ref[...]).astype(BF)

    return kernel_call(
        "norm_step", body, [((rows, width), F32), ((rows, width), BF)], [*parts, hidden, gain]
    )


def norm_back(parts, hidden, gain, grad):
    rows, width = hidden.shape
    n = len(parts)

    def body(*refs):
        h_ref, g_ref, grad_ref, out_ref, b_ref, gain_ref = refs[n:]
        total = refs[0][...]
        for part in refs[1:n]:
            total = total + part[...].astype(F32)
        h = h_ref[...]
        scale = lax.rsqrt(jnp.mean(h * h, axis=-1, keepdims=True) + eps)
        unit = h * scale
        through = total * g_ref[...]
        out = grad_ref[...] + scale * (
            through - unit * jnp.mean(through * unit, axis=-1, keepdims=True)
        )
        out_ref[...] = out
        b_ref[...] = out.astype(BF)
        gain_ref[...] = jnp.sum(total * unit, axis=0, keepdims=True)

    return kernel_call(
        "norm_back",
        body,
        [((rows, width), F32), ((rows, width), BF), ((1, width), F32)],
        [*parts, hidden, gain, grad],
    )


def keys_values(me, parts, kvw, cos_kv, sin_kv):
    n = len(parts)
    rows, width = parts[0].shape
    tokens = n * rows

    def body(*refs):
        me_ref = refs[0]
        w_ref, c_ref, s_ref, nat_ref, kv_ref, edge_ref = refs[1 + n :]
        ordered(me_ref, refs[1 : 1 + n], nat_ref)
        raw = mm(nat_ref[...], w_ref[...])
        kv_ref[...] = (raw * c_ref[...] + halves_swapped(raw) * s_ref[...]).astype(BF)
        edge_ref[...] = nat_ref[tokens - 16 :, :]

    return kernel_call(
        "keys_values",
        body,
        [((tokens, width), BF), ((tokens, 128), BF), ((16, width), BF)],
        [me, *parts, kvw, cos_kv, sin_kv],
        flops=2 * tokens * width * 128,
    )


def mixer_front(nat, edge, wzx, wbc, wdt, wq, conv_w, hp, tok, cos_q, sin_q):
    tokens, width = nat.shape
    inner = wzx[0].shape[2] // 2
    mix = inner + 2 * NS

    def body(
        nat_ref, edge_ref, wzx_ref, wbc_ref, wdt_ref, wq_ref, cw_ref, hp_ref, tok_ref, c_ref, s_ref,
        gate_ref, pad_ref, act_ref, slope_ref, hd_ref, q2_ref, pack_ref,
    ):
        x = nat_ref[...]
        e = edge_ref[...]
        gate_ref[...] = mm(x, wzx_ref[:, :inner])
        pad_ref[16:, :inner] = mm(x, wzx_ref[:, inner:])
        pad_ref[16:, inner:] = mm(x, wbc_ref[...])
        pad_ref[:16, :inner] = mm(e, wzx_ref[:, inner:])
        pad_ref[:16, inner:] = mm(e, wbc_ref[...])
        q = mm(x, wq_ref[...])
        q = (q * c_ref[...] + halves_swapped(q) * s_ref[...]).astype(BF).astype(F32)
        lane = iota((tokens, 128), 1)
        q2_ref[:tokens, :] = jnp.where(lane < HEAD_SIZE, q, 0.0).astype(BF)
        q2_ref[tokens:, :] = jnp.where(
            lane < HEAD_SIZE, pltpu.roll(q, HEAD_SIZE, 1), 0.0
        ).astype(BF)
        tk = tok_ref[...]
        conv = jnp.broadcast_to(cw_ref[KC : KC + 1, :], (tokens, mix))
        for j in range(KC):
            shifted = pad_ref[16 - (KC - 1) + j : 16 - (KC - 1) + j + tokens, :]
            conv = conv + cw_ref[j : j + 1, :] * shifted * tk[:, j : j + 1]
        sg = sigmoid(conv)
        act = conv * sg
        act_ref[...] = act
        slope_ref[...] = sg * (1.0 + conv * (1.0 - sg))
        r = mm(x, wdt_ref[...]) + hp_ref[0:1, :]
        dt = jnp.maximum(r, 0.0) + jnp.log1p(jnp.exp(-jnp.abs(r)))
        log_decay = -dt * jnp.exp(hp_ref[1:2, :])
        lower = (iota((tokens, tokens), 0) >= iota((tokens, tokens), 1)).astype(F32)
        cum = mm_hi(lower, log_decay)
        hd_ref[0] = r
        hd_ref[1] = dt
        hd_ref[2] = cum
        last = cum[tokens - 1 :, :]
        to_last = jnp.where(tk[:, 5:6] > 0.5, jnp.exp(last - cum), 0.0)
        scaled = act[:, :inner] * expand(dt * to_last, inner)
        pack_ref[:inner, :] = mm_tn(scaled, act[:, inner : inner + NS]).astype(BF)
        pack_ref[inner:, :] = decay_rows(jnp.exp(last) * tk[tokens - 1 :, 4:5])

    return kernel_call(
        "mixer_front",
        body,
        [
            ((tokens, inner), F32),
            ((tokens + 16, mix), F32),
            ((tokens, mix), F32),
            ((tokens, mix), F32),
            ((3, tokens, 128), F32),
            ((2 * tokens, 128), BF),
            ((inner + 16, NS), BF),
        ],
        [nat, edge, wzx, wbc, wdt, wq, conv_w, hp, tok, cos_q, sin_q],
        flops=2 * tokens * width * 1280,
    )


def allowed_pair(segc, segr, tokens, steps_back):
    heads = segc.shape[0] // tokens
    row = iota((heads * tokens, tokens), 0) % tokens
    column = iota((heads * tokens, tokens), 1)
    return (segc == segr) & (column - tokens * steps_back <= row)


def within_decay(cum, cum_t, h, allowed):
    return jnp.exp(jnp.where(allowed, cum[:, h : h + 1] - cum_t[h : h + 1, :], neg_big))


def attend(kvs, q2, segc, segrel, blocks, act, hd, hp, inner):
    n = len(kvs)
    tokens = kvs[0].shape[0]
    rows = q2.shape[0]

    def body(*refs):
        (q2_ref, segc_ref, segr_ref, nb_ref, act_ref, hd_ref, hp_ref) = refs[n : n + 7]
        o2_ref, lse_ref, flat_ref, y_ref, kv_ref = refs[n + 7 :]
        for d in range(n):
            kv_ref[d] = refs[d][...]
        q = q2_ref[...]
        seg_own = segc_ref[...]
        seg_two = jnp.concatenate([seg_own] * (rows // tokens), axis=0)

        def step(d, carry):
            top, total, out = carry
            kv = kv_ref[d]
            allowed = allowed_pair(seg_two, segr_ref[d], tokens, d)
            scores = jnp.where(allowed, mm_nt(q, kv) * score_scale, neg_big)
            new_top = jnp.maximum(top, jnp.max(scores, axis=1, keepdims=True))
            weights = jnp.where(allowed, jnp.exp(scores - new_top), 0.0)
            shrink = jnp.exp(top - new_top)
            return (
                new_top,
                total * shrink + jnp.sum(weights, axis=1, keepdims=True),
                out * shrink + mm(weights, kv),
            )

        top, total, out = lax.fori_loop(
            0,
            nb_ref[0],
            step,
            (
                jnp.full((rows, 1), neg_big, F32),
                jnp.zeros((rows, 1), F32),
                jnp.zeros((rows, 128), F32),
            ),
        )
        out = out / total
        o2_ref[...] = out
        lse_ref[...] = jnp.broadcast_to(top + jnp.log(total), (rows, 128))
        lane = iota((tokens, 128), 1)
        flat_ref[...] = jnp.where(
            lane < HEAD_SIZE, pltpu.roll(out[:tokens], HEAD_SIZE, 1), out[tokens:]
        ).astype(BF)
        act_all = act_ref[...]
        b_mat = act_all[:, inner : inner + NS]
        c_mat = act_all[:, inner + NS :]
        both = mm_nt(c_mat, b_mat)
        dt, cum = hd_ref[1], hd_ref[2]
        cum_t = cum.T
        allowed = allowed_pair(seg_own, segr_ref[0], tokens, 0)
        scaled = act_all[:, :inner] * expand(dt, inner)
        skip = expand(hp_ref[...], inner)[2:3, :]
        for p in range(inner // 128):
            cols = slice(128 * p, 128 * (p + 1))
            pair = [
                mm(within_decay(cum, cum_t, 2 * p + k, allowed) * both, scaled[:, cols])
                for k in range(2)
            ]
            y_ref[:, cols] = (
                jnp.where(lane < HEAD_SIZE, pair[0], pair[1])
                + skip[:, cols] * act_all[:, cols]
            )

    return kernel_call(
        "attend",
        body,
        [
            ((rows, 128), F32),
            ((rows, 128), F32),
            ((tokens, 128), BF),
            ((tokens, inner), F32),
        ],
        [*kvs, q2, segc, segrel, blocks, act, hd, hp],
        scratch=[pltpu.VMEM((n, tokens, 128), BF)],
        flops=2 * rows * tokens * 128 * 2 * n,
    )


def mixer_out(me, packs, y_local, act, hd, tok, gate, flat, wout, wao, wa_count):
    m = len(packs)
    tokens, inner = y_local.shape
    width = wout[0].shape[2]
    rows = tokens // wa_count

    def body(*refs):
        me_ref = refs[0]
        y_ref, act_ref, hd_ref, tok_ref, gate_ref, flat_ref, wout_ref, wao_ref = refs[
            1 + m : 9 + m
        ]
        state_ref, yy_ref, gated_ref = refs[9 + m : 12 + m]
        blocks = refs[12 + m : 12 + m + wa_count]
        full_ref = refs[-1]
        state = fold_states([r[...] for r in refs[1 : 1 + m]], inner)
        state_ref[...] = state
        decay_in = jnp.exp(hd_ref[2]) * tok_ref[:, 4:5]
        y = y_ref[...] + mm_nt(act_ref[:, inner + NS :], state) * expand(decay_in, inner)
        yy_ref[...] = y
        gate_raw = gate_ref[...]
        gated = (y * gate_raw * sigmoid(gate_raw)).astype(BF)
        gated_ref[...] = gated
        full_ref[...] = mm(gated, wout_ref[...]) + mm(flat_ref[...], wao_ref[...])
        rotated(me_ref, full_ref, blocks)

    return kernel_call(
        "mixer_out",
        body,
        [((inner, NS), F32), ((tokens, inner), F32), ((tokens, inner), BF)]
        + [((rows, width), F32)]
        + [((rows, width), BF)] * (wa_count - 1),
        [me, *packs, y_local, act, hd, tok, gate, flat, wout, wao],
        scratch=[pltpu.VMEM((tokens, width), F32)],
        flops=2 * tokens * width * 512,
    )


def feed_forward(parts, wgu, wdown):
    n = len(parts)
    rows, width = parts[0].shape
    tokens = n * rows
    hidden = wdown[0].shape[1]

    def body(*refs):
        wgu_ref, wdown_ref, n_ref, gu_ref, act_ref = refs[n : n + 5]
        blocks = refs[n + 5 : n + 5 + n]
        for d in range(n):
            n_ref[d * rows : (d + 1) * rows, :] = refs[d][...]
        x = n_ref[...]
        gate = mm(x, wgu_ref[:, :hidden])
        up = mm(x, wgu_ref[:, hidden:])
        gu_ref[:, :hidden] = gate
        gu_ref[:, hidden:] = up
        act = (gate * sigmoid(gate) * up).astype(BF)
        act_ref[...] = act
        for d in range(n):
            blocks[d][...] = mm(act[d * rows : (d + 1) * rows], wdown_ref[...]).astype(
                blocks[d].dtype
            )

    return kernel_call(
        "feed_forward",
        body,
        [((tokens, width), BF), ((tokens, 2 * hidden), F32), ((tokens, hidden), BF)]
        + [((rows, width), F32)]
        + [((rows, width), BF)] * (n - 1),
        [*parts, wgu, wdown],
        flops=2 * tokens * width * 3 * hidden,
    )


def feed_back(parts, gu, wgu, wdown):
    n = len(parts)
    rows, width = parts[0].shape
    tokens = n * rows
    hidden = wdown[0].shape[1]

    def body(*refs):
        gu_ref, wgu_ref, wdown_ref, gb_ref, dgu_ref = refs[n : n + 5]
        blocks = refs[n + 5 : n + 5 + n]
        for d in range(n):
            gb_ref[d * rows : (d + 1) * rows, :] = refs[d][...]
        d_act = mm_nt(gb_ref[...], wdown_ref[...])
        gate = gu_ref[:, :hidden]
        up = gu_ref[:, hidden:]
        sg = sigmoid(gate)
        dgu_ref[:, :hidden] = (d_act * up * sg * (1.0 + gate * (1.0 - sg))).astype(BF)
        dgu_ref[:, hidden:] = (d_act * gate * sg).astype(BF)
        for d in range(n):
            blocks[d][...] = mm_nt(dgu_ref[d * rows : (d + 1) * rows, :], wgu_ref[...]).astype(
                blocks[d].dtype
            )

    return kernel_call(
        "feed_back",
        body,
        [((tokens, width), BF), ((tokens, 2 * hidden), BF)]
        + [((rows, width), F32)]
        + [((rows, width), BF)] * (n - 1),
        [*parts, gu, wgu, wdown],
        flops=2 * tokens * width * 3 * hidden,
    )


def weight_grads(here, pairs, n):
    width = pairs[0][0].shape[1]
    columns = sum(right.shape[1] for left, right in pairs)
    flat = [a for pair in pairs for a in pair]
    direct = n <= DIRECT_MOST
    blocks = n if direct else 1
    rows = width // blocks

    def body(*refs):
        here_ref = refs[0]
        outs = refs[1 + len(flat) :]
        for d in range(blocks):
            start = 0
            for k in range(len(pairs)):
                left, right = refs[1 + 2 * k], refs[2 + 2 * k]
                wide = right.shape[1]
                if direct:
                    at = pl.multiple_of(lax.rem(here_ref[0] + d, n) * rows, rows)
                    piece = left[:, pl.ds(at, rows)]
                else:
                    piece = left[...]
                outs[d][:, start : start + wide] = mm_tn(piece, right[...]).astype(outs[d].dtype)
                start += wide

    return kernel_call(
        "weight_grads",
        body,
        [((rows, columns), F32 if direct and d == 0 else BF) for d in range(blocks)],
        [here, *flat],
        flops=2 * pairs[0][0].shape[0] * width * columns,
    )


def mixer_grad_in(me, parts, wout, wao, gate, y, act, hd, tok, o2):
    n = len(parts)
    rows, width = parts[0].shape
    tokens, inner = y.shape

    def body(*refs):
        me_ref = refs[0]
        wout_ref, wao_ref, gate_ref, y_ref, act_ref, hd_ref, tok_ref, o2_ref = refs[1 + n : 9 + n]
        nat_ref, dy_ref, dgate_ref, pack_ref, da2_ref, delta_ref = refs[9 + n :]
        ordered(me_ref, refs[1 : 1 + n], nat_ref)
        mb = nat_ref[...]
        d_gated = mm_nt(mb, wout_ref[...])
        gate_raw = gate_ref[...]
        sg = sigmoid(gate_raw)
        dy = d_gated * gate_raw * sg
        dy_ref[...] = dy
        dgate_ref[...] = (
            d_gated * y_ref[...] * sg * (1.0 + gate_raw * (1.0 - sg))
        ).astype(BF)
        cum = hd_ref[2]
        decay_in = jnp.exp(cum) * tok_ref[:, 4:5]
        pack_ref[:inner, :] = mm_tn(
            dy * expand(decay_in, inner), act_ref[:, inner + NS :]
        ).astype(BF)
        pack_ref[inner:, :] = decay_rows(decay_in[tokens - 1 :, :])
        d_attn = mm_nt(mb, wao_ref[...])
        lane = iota((tokens, 128), 1)
        da2 = jnp.concatenate(
            [
                jnp.where(lane >= HEAD_SIZE, pltpu.roll(d_attn, HEAD_SIZE, 1), 0.0),
                jnp.where(lane >= HEAD_SIZE, d_attn, 0.0),
            ],
            axis=0,
        )
        da2_ref[...] = da2.astype(BF)
        delta_ref[...] = jnp.broadcast_to(
            jnp.sum(da2 * o2_ref[...], axis=1, keepdims=True), da2.shape
        )

    return kernel_call(
        "mixer_grad_in",
        body,
        [
            ((tokens, width), BF),
            ((tokens, inner), F32),
            ((tokens, inner), BF),
            ((inner + 16, NS), BF),
            ((2 * tokens, 128), BF),
            ((2 * tokens, 128), F32),
        ],
        [me, *parts, wout, wao, gate, y, act, hd, tok, o2],
        flops=2 * tokens * width * 512,
    )


def attend_back(kvs, q2, da2, delta, lse, segc, segrel, blocks, cos_q, sin_q):
    n = len(kvs)
    tokens = kvs[0].shape[0]
    rows = q2.shape[0]

    def body(*refs):
        (q2_ref, da_ref, delta_ref, lse_ref, segc_ref, segr_ref, nb_ref, c_ref, s_ref) = refs[
            n : n + 9
        ]
        dq_ref = refs[n + 9]
        outs = refs[n + 10 : n + 10 + n]
        kv_ref, dkv_ref = refs[n + 10 + n :]
        for d in range(n):
            kv_ref[d] = refs[d][...]
        for d in range(1, n):
            dkv_ref[d] = jnp.zeros((tokens, 128), F32)
        q = q2_ref[...]
        da = da_ref[...]
        lse_col = lse_ref[:, 0:1]
        delta_col = delta_ref[:, 0:1]
        seg_two = jnp.concatenate([segc_ref[...]] * (rows // tokens), axis=0)

        def step(d, dq):
            kv = kv_ref[d]
            allowed = allowed_pair(seg_two, segr_ref[d], tokens, d)
            scores = mm_nt(q, kv) * score_scale
            probs = jnp.exp(jnp.where(allowed, scores - lse_col, neg_big))
            d_scores = (probs * (mm_nt(da, kv) - delta_col)).astype(BF)
            dkv_ref[d] = mm_tn(d_scores, q) * score_scale + mm_tn(probs, da)
            return dq + mm(d_scores, kv)

        dq = lax.fori_loop(0, nb_ref[0], step, jnp.zeros((rows, 128), F32)) * score_scale
        lane = iota((tokens, 128), 1)
        flat = jnp.where(lane < HEAD_SIZE, dq[:tokens], pltpu.roll(dq[tokens:], HEAD_SIZE, 1))
        dq_ref[...] = (flat * c_ref[...] - halves_swapped(flat) * s_ref[...]).astype(BF)
        for d in range(n):
            outs[d][...] = dkv_ref[d].astype(outs[d].dtype)

    return kernel_call(
        "attend_back",
        body,
        [((tokens, 128), BF), ((tokens, 128), F32)] + [((tokens, 128), BF)] * (n - 1),
        [*kvs, q2, da2, delta, lse, segc, segrel, blocks, cos_q, sin_q],
        scratch=[pltpu.VMEM((n, tokens, 128), BF), pltpu.VMEM((n, tokens, 128), F32)],
        flops=2 * rows * tokens * 128 * 5 * n,
    )


def mixer_grad(packs, state_in, dy, act, slope, pad, hd, tok, segc, segrel, hp, conv_w):
    m = len(packs)
    tokens, inner = dy.shape
    mix = act.shape[1]

    def body(*refs):
        (
            state_ref, dy_ref, act_ref, slope_ref, pad_ref, hd_ref, tok_ref, segc_ref, segr_ref,
            hp_ref, cw_ref, dmix_ref, tail_ref, edge_ref, ddt_ref, gconv_ref, ghead_ref,
            dconv_ref, dpad_ref, dxs_ref,
        ) = refs[m:]
        later = fold_states([r[...] for r in refs[:m]], inner)
        state = state_ref[...]
        tk = tok_ref[...]
        act_all = act_ref[...]
        x = act_all[:, :inner]
        b_mat = act_all[:, inner : inner + NS]
        c_mat = act_all[:, inner + NS :]
        dy_all = dy_ref[...]
        r, dt, cum = hd_ref[0], hd_ref[1], hd_ref[2]
        cum_t = cum.T
        last = cum[tokens - 1 :, :]
        to_last = jnp.where(tk[:, 5:6] > 0.5, jnp.exp(last - cum), 0.0)
        decay_in = jnp.exp(cum) * tk[:, 4:5]
        dt_wide = expand(dt, inner)
        last_wide = expand(to_last, inner)
        in_wide = expand(decay_in, inner)
        xs = x * dt_wide
        allowed = allowed_pair(segc_ref[...], segr_ref[0], tokens, 0)
        both = mm_nt(c_mat, b_mat)
        lane = iota((tokens, 128), 1)
        lane_row = iota((128, tokens), 0)
        d_both = jnp.zeros((tokens, tokens), F32)
        d_cum = jnp.zeros((tokens, 128), F32)
        d_cum_t = jnp.zeros((128, tokens), F32)
        for p in range(inner // 128):
            cols = slice(128 * p, 128 * (p + 1))
            xs_pair = xs[:, cols].astype(BF)
            dy_pair = dy_all[:, cols]
            pieces = []
            for k in range(2):
                h = 2 * p + k
                decay = within_decay(cum, cum_t, h, allowed)
                weight = decay * both
                mine = (lane >= HEAD_SIZE) if k else (lane < HEAD_SIZE)
                d_weight = mm_nt(jnp.where(mine, dy_pair, 0.0), xs_pair)
                d_both = d_both + d_weight * decay
                flow = d_weight * weight
                d_cum = d_cum + jnp.where(lane == h, jnp.sum(flow, axis=1, keepdims=True), 0.0)
                d_cum_t = d_cum_t + jnp.where(
                    lane_row == h, jnp.sum(flow, axis=0, keepdims=True), 0.0
                )
                pieces.append(mm_tn(weight, dy_pair))
            dxs_ref[:, cols] = jnp.where(lane < HEAD_SIZE, pieces[0], pieces[1])
        from_state = mm_nt(b_mat, later)
        d_xs = dxs_ref[...] + from_state * last_wide
        dy_in = dy_all * in_wide
        inflow = mm_nt(c_mat, state)
        d_c = mm(d_both, b_mat) + mm(dy_in, state)
        d_b = mm_tn(d_both, c_mat) + mm(xs * last_wide, later)
        carried = head_sum(from_state * xs * last_wide)
        d_cum = d_cum - d_cum_t.T + head_sum(dy_in * inflow) - carried
        row_sum = jnp.sum(later * state, axis=1, keepdims=True)
        pick = (iota((inner, 128), 0) // HEAD_SIZE == iota((inner, 128), 1)).astype(F32)
        d_decay = jnp.sum(row_sum * pick, axis=0, keepdims=True)
        d_last = jnp.sum(carried, axis=0, keepdims=True) + decay_in[tokens - 1 :, :] * d_decay
        d_cum = d_cum + jnp.where(iota((tokens, 128), 0) == tokens - 1, d_last, 0.0)
        upper = (iota((tokens, tokens), 0) <= iota((tokens, tokens), 1)).astype(F32)
        d_log = mm_hi(upper, d_cum)
        rate = jnp.exp(hp_ref[1:2, :])
        d_dt = head_sum(d_xs * x) - rate * d_log
        d_r = d_dt * sigmoid(r)
        ddt_ref[...] = d_r.astype(BF)
        g_bias = jnp.sum(d_r, axis=0, keepdims=True)
        g_log = -jnp.sum(d_log * dt, axis=0, keepdims=True) * rate
        g_skip = jnp.sum(head_sum(dy_all * x), axis=0, keepdims=True)
        row8 = iota((8, 128), 0)
        ghead_ref[...] = jnp.where(
            row8 == 0, g_bias, jnp.where(row8 == 1, g_log, jnp.where(row8 == 2, g_skip, 0.0))
        )
        skip = expand(hp_ref[...], inner)[2:3, :]
        dconv_ref[:, :inner] = (dy_all * skip + d_xs * dt_wide) * slope_ref[:, :inner]
        dconv_ref[:, inner : inner + NS] = d_b * slope_ref[:, inner : inner + NS]
        dconv_ref[:, inner + NS :] = d_c * slope_ref[:, inner + NS :]
        dpad_ref[...] = jnp.zeros((tokens + 16, mix), F32)
        gconv_ref[...] = jnp.zeros((8, mix), F32)
        dconv = dconv_ref[...]
        gconv_ref[KC : KC + 1, :] = jnp.sum(dconv, axis=0, keepdims=True)
        for j in range(KC):
            at = 16 - (KC - 1) + j
            used = dconv * tk[:, j : j + 1]
            gconv_ref[j : j + 1, :] = jnp.sum(
                used * pad_ref[at : at + tokens, :], axis=0, keepdims=True
            )
            dpad_ref[at : at + tokens, :] = (
                dpad_ref[at : at + tokens, :] + used * cw_ref[j : j + 1, :]
            )
        dmix_ref[...] = dpad_ref[16:, :].astype(BF)
        tail_ref[...] = dpad_ref[tokens:, :]
        edge_ref[...] = dpad_ref[8:16, :]

    return kernel_call(
        "mixer_grad",
        body,
        [
            ((tokens, mix), BF),
            ((16, mix), F32),
            ((8, mix), F32),
            ((tokens, 128), BF),
            ((8, mix), F32),
            ((8, 128), F32),
        ],
        [*packs, state_in, dy, act, slope, pad, hd, tok, segc, segrel, hp, conv_w],
        scratch=[
            pltpu.VMEM((tokens, mix), F32),
            pltpu.VMEM((tokens + 16, mix), F32),
            pltpu.VMEM((tokens, inner), F32),
        ],
        flops=2 * tokens * tokens * 128 * 24,
    )


def grads_out(
    me, dgate, dmix, tail, next_edge, ddt, dq, dkv_own, dkv_got, cos_kv, sin_kv,
    wzx, wbc, wdt, wq, kvw, wa_count,
):
    m = len(dkv_got)
    tokens, inner = dgate.shape
    mix = dmix.shape[1]
    width = wzx[0].shape[1]
    rows = tokens // wa_count
    wide = inner + mix + 3 * 128

    def body(*refs):
        me_ref = refs[0]
        got = refs[1 : 1 + m]
        (
            dgate_ref, dmix_ref, tail_ref, edge_ref, ddt_ref, dq_ref, own_ref, c_ref, s_ref,
            wzx_ref, wbc_ref, wdt_ref, wq_ref, kvw_ref, right_ref,
        ) = refs[1 + m : 16 + m]
        blocks = refs[16 + m : 16 + m + wa_count]
        full_ref = refs[-1]
        right_ref[:, :inner] = dgate_ref[...]
        right_ref[: tokens - 16, inner : inner + mix] = dmix_ref[: tokens - 16, :]
        right_ref[tokens - 16 :, inner : inner + mix] = (
            tail_ref[...]
            + jnp.concatenate([jnp.zeros((8, mix), F32), edge_ref[...]], axis=0)
        ).astype(BF)
        at = inner + mix
        right_ref[:, at : at + 128] = dq_ref[...]
        dkv = own_ref[...]
        for part in got:
            dkv = dkv + part[...].astype(F32)
        right_ref[:, at + 128 : at + 256] = (
            dkv * c_ref[...] - halves_swapped(dkv) * s_ref[...]
        ).astype(BF)
        right_ref[:, at + 256 :] = ddt_ref[...]
        full_ref[...] = (
            mm_nt(right_ref[:, : 2 * inner], wzx_ref[...])
            + mm_nt(right_ref[:, 2 * inner : at], wbc_ref[...])
            + mm_nt(right_ref[:, at : at + 128], wq_ref[...])
            + mm_nt(right_ref[:, at + 128 : at + 256], kvw_ref[...])
            + mm_nt(right_ref[:, at + 256 :], wdt_ref[...])
        )
        rotated(me_ref, full_ref, blocks)

    return kernel_call(
        "grads_out",
        body,
        [((tokens, wide), BF), ((rows, width), F32)] + [((rows, width), BF)] * (wa_count - 1),
        [
            me, *dkv_got, dgate, dmix, tail, next_edge, ddt, dq, dkv_own, cos_kv, sin_kv,
            wzx, wbc, wdt, wq, kvw,
        ],
        scratch=[pltpu.VMEM((tokens, width), F32)],
        flops=2 * tokens * width * wide,
    )


def per_device(
    x_in,
    d_out,
    segment_ids,
    norm_gains,
    w_zx,
    w_bc,
    w_dt,
    conv_x,
    conv_bc,
    dt_bias,
    a_log,
    d_skip,
    w_out,
    w_q,
    key_value_weight,
    w_ao,
    w_gu,
    w_down,
):
    seq_count = lax.axis_size("seq")
    wa_count = lax.axis_size("wa")
    tokens, width = x_in.shape
    rows = tokens // wa_count
    seq_here = lax.axis_index("seq")
    wa_here = lax.axis_index("wa")
    start_row = seq_here * tokens
    inner = w_zx.shape[3]
    heads = w_dt.shape[2]
    hidden = w_gu.shape[3]
    query_local = w_q.shape[2] // HEAD_SIZE
    group = QUERY_HEADS // KEY_VALUE_HEADS
    kv_head = wa_here * query_local // group
    me = wa_here.astype(jnp.int32).reshape(1)
    here = seq_here.astype(jnp.int32).reshape(1)

    seg_blocks = segment_ids.reshape(seq_count, tokens)
    seg_here = lax.dynamic_slice_in_dim(segment_ids, start_row, tokens)
    seg_padded = jnp.concatenate([jnp.full((KC - 1,), -1, jnp.int32), segment_ids])
    seg_edge = lax.dynamic_slice_in_dim(seg_padded, start_row, KC - 1)
    seg_full = jnp.concatenate([seg_edge, seg_here])
    steps = jnp.arange(seq_count, dtype=jnp.int32)
    segrel = jnp.where(
        (steps <= seq_here)[:, None], seg_blocks[(seq_here - steps) % seq_count], -1
    )
    blocks_used = (
        1 + jnp.sum((segrel[1:, tokens - 1] == seg_here[0]).astype(jnp.int32))
    ).astype(jnp.int32).reshape(1)
    segrel = segrel[:, None, :]
    segc = seg_here[:, None]
    columns = [(seg_full[j : j + tokens] == seg_here).astype(F32) for j in range(KC)]
    columns.append((seg_here == seg_edge[KC - 2]).astype(F32))
    columns.append((seg_here == seg_here[tokens - 1]).astype(F32))
    tok = jnp.pad(jnp.stack(columns, axis=1), ((0, 0), (0, 128 - len(columns))))
    half = HEAD_SIZE // 2
    frequency = jnp.exp(jnp.arange(half, dtype=F32) * (-math.log(theta) / half))
    positions = (start_row + jnp.arange(tokens, dtype=jnp.int32)).astype(F32)
    angles = positions[:, None] * frequency[None, :]
    cosine, sine = jnp.cos(angles), jnp.sin(angles)
    cos_q = jnp.concatenate([cosine] * 4, axis=1)
    sin_q = jnp.concatenate([-sine, sine, -sine, sine], axis=1)
    ones = jnp.ones((tokens, HEAD_SIZE), F32)
    cos_kv = jnp.concatenate([cosine, cosine, ones], axis=1)
    sin_kv = jnp.concatenate([-sine, sine, 0.0 * ones], axis=1)

    wzx_all = w_zx.reshape(LAYER_COUNT, width, 2 * inner)
    wgu_all = w_gu.reshape(LAYER_COUNT, width, 2 * hidden)
    wdt_all = jnp.pad(w_dt, ((0, 0), (0, 0), (0, 128 - heads)))
    kvw_all = lax.dynamic_slice_in_dim(
        key_value_weight, kv_head * HEAD_SIZE, HEAD_SIZE, axis=3
    ).reshape(LAYER_COUNT, width, 2 * HEAD_SIZE)
    conv_all = jnp.pad(
        jnp.concatenate([conv_x, conv_bc], axis=2), ((0, 0), (0, 8 - (KC + 1)), (0, 0))
    )
    hp_all = jnp.pad(
        jnp.stack([dt_bias, a_log, d_skip], axis=1), ((0, 0), (0, 5), (0, 128 - heads))
    )

    def own_rows(array):
        return lax.dynamic_slice_in_dim(array, wa_here * rows, rows)

    h = own_rows(x_in)
    normed = norm_first(h, norm_gains[0, 0][None, :])
    saved = []
    for layer in range(LAYER_COUNT):
        wzx, wbc, wdt, wq = [(a, layer) for a in (wzx_all, w_bc, wdt_all, w_q)]
        kvw, conv_w, hp = [(a, layer) for a in (kvw_all, conv_all, hp_all)]
        wout, wao, wgu, wdown = [(a, layer) for a in (w_out, w_ao, wgu_all, w_down)]
        nat, kv, edge = keys_values(me, gather_wa(normed), kvw, cos_kv, sin_kv)
        n = seq_count
        edge = lax.ppermute(edge, "seq", [(i, i + 1) for i in range(n - 1)])
        kvs = [kv] + from_earlier(kv)
        gate, pad, act, slope, hd, q2, pack = mixer_front(
            nat, edge, wzx, wbc, wdt, wq, conv_w, hp, tok, cos_q, sin_q
        )
        packs = from_earlier(pack)
        o2, lse, flat, y_local = attend(
            kvs, q2, segc, segrel, blocks_used, act, hd, hp, inner
        )
        state_in, y, gated, *parts = mixer_out(
            me, packs, y_local, act, hd, tok, gate, flat, wout, wao, wa_count
        )
        mixed, normed_two = norm_step(scatter_wa(parts), h, norm_gains[layer, 1][None, :])
        n2, gu, act_ff, *parts = feed_forward(gather_wa(normed_two), wgu, wdown)
        saved.append(
            (h, nat, kvs, gate, pad, act, slope, hd, q2, o2, lse, flat, state_in, y, gated,
             mixed, n2, gu, act_ff)
        )
        following = norm_gains[min(layer + 1, LAYER_COUNT - 1), 0][None, :]
        h, normed = norm_step(scatter_wa(parts), mixed, following)

    def whole_rows(parts):
        full = jnp.zeros((tokens, width), F32)
        for d, part in enumerate(parts):
            at = (wa_here + d) % wa_count * rows
            full = lax.dynamic_update_slice_in_dim(full, part.astype(F32), at, axis=0)
        return full

    x_out = whole_rows(gather_wa(h.astype(BF)))

    grad = own_rows(d_out)
    grad_parts = [
        lax.dynamic_slice_in_dim(d_out, (wa_here + d) % wa_count * rows, rows).astype(BF)
        for d in range(wa_count)
    ]
    sums = [None] * LAYER_COUNT
    small = [None] * LAYER_COUNT
    for layer in reversed(range(LAYER_COUNT)):
        wzx, wbc, wdt, wq = [(a, layer) for a in (wzx_all, w_bc, wdt_all, w_q)]
        kvw, conv_w, hp = [(a, layer) for a in (kvw_all, conv_all, hp_all)]
        wout, wao, wgu, wdown = [(a, layer) for a in (w_out, w_ao, wgu_all, w_down)]
        (h_in, nat, kvs, gate, pad, act, slope, hd, q2, o2, lse, flat, state_in, y, gated,
         mixed, n2, gu, act_ff) = saved[layer]
        gb, dgu, *parts = feed_back(grad_parts, gu, wgu, wdown)
        parts = scatter_wa(parts)
        sum_ff = scatter_rows(weight_grads(here, [(gb, act_ff), (n2, dgu)], seq_count))
        d_mixed, mixed_b, gain_two = norm_back(
            parts, mixed, norm_gains[layer, 1][None, :], grad
        )
        mb, dy, dgate, pack, da2, delta = mixer_grad_in(
            me, gather_wa(mixed_b), wout, wao, gate, y, act, hd, tok, o2
        )
        packs = from_later(pack)
        dq, dkv_own, *dkv_rest = attend_back(
            kvs, q2, da2, delta, lse, segc, segrel, blocks_used, cos_q, sin_q
        )
        dkv_got = to_earlier(dkv_rest)
        sum_mix = scatter_rows(weight_grads(here, [(mb, gated), (mb, flat)], seq_count))
        dmix, tail, edge_grad, ddt, gconv, ghead = mixer_grad(
            packs, state_in, dy, act, slope, pad, hd, tok, segc, segrel, hp, conv_w
        )
        next_edge = lax.ppermute(
            edge_grad, "seq", [(i + 1, i) for i in range(seq_count - 1)]
        )
        right, *parts = grads_out(
            me, dgate, dmix, tail, next_edge, ddt, dq, dkv_own, dkv_got, cos_kv, sin_kv,
            wzx, wbc, wdt, wq, kvw, wa_count,
        )
        parts = scatter_wa(parts)
        sum_in = scatter_rows(weight_grads(here, [(nat, right)], seq_count))
        grad, grad_b, gain_one = norm_back(
            parts, h_in, norm_gains[layer, 0][None, :], d_mixed
        )
        grad_parts = gather_wa(grad_b)
        sums[layer] = (sum_ff, sum_mix, sum_in)
        small[layer] = (gain_one, gain_two, gconv, ghead)
    d_x = whole_rows(grad_parts)

    gains = [small[layer][k].reshape(width // 128, 128) for layer in range(LAYER_COUNT) for k in (0, 1)]
    convs = [
        jnp.concatenate([small[layer][2][j].reshape(-1, 128) for j in range(KC + 1)])
        for layer in range(LAYER_COUNT)
    ]
    packed = jnp.concatenate(gains + convs + [small[layer][3] for layer in range(LAYER_COUNT)])
    packed = sum_seq(packed)
    gain_rows = 4 * width // 128
    gain_sum = packed[:gain_rows]
    mix = inner + 2 * NS
    conv_sum = packed[gain_rows : gain_rows + LAYER_COUNT * (KC + 1) * (mix // 128)].reshape(
        LAYER_COUNT, KC + 1, mix
    )
    head_part = packed[gain_rows + LAYER_COUNT * (KC + 1) * (mix // 128) :].reshape(
        LAYER_COUNT, 8, 128
    )
    shared = jnp.concatenate(
        [gain_sum, conv_sum[:, :, inner:].reshape(-1, 128)], axis=0
    )
    shared_parts = gather_wa(shared)
    shared = shared_parts[0]
    for part in shared_parts[1:]:
        shared = shared + part
    gain_sum = shared[:gain_rows].reshape(LAYER_COUNT, 2, width)
    g_conv_bc = shared[gain_rows:].reshape(LAYER_COUNT, KC + 1, 2 * NS)

    at = 2 * inner
    after = at + 2 * NS
    every = jnp.stack(
        [
            jnp.concatenate([s[2][:, at:after], s[2][:, after + 128 : after + 256]], axis=1)
            for s in sums
        ]
    ).astype(BF)
    every_parts = gather_wa(every)
    g_bc = sum(part[:, :, : 2 * NS].astype(F32) for part in every_parts)
    kv_columns = []
    for head in range(KEY_VALUE_HEADS):
        total = 0.0
        for d, part in enumerate(every_parts):
            source = (wa_here + d) % wa_count * query_local // group
            total = total + jnp.where(source == head, part[:, :, 2 * NS :].astype(F32), 0.0)
        kv_columns.append(total.reshape(total.shape[0], total.shape[1], 2, HEAD_SIZE))
    g_kv = jnp.concatenate(kv_columns, axis=3)

    block = sums[0][0].shape[0]

    def stacked(pick):
        return jnp.stack([pick(s) for s in sums])

    g_down = stacked(lambda s: s[0][:, :hidden].T)
    g_gu = stacked(lambda s: s[0][:, hidden:].reshape(block, 2, hidden))
    g_out = stacked(lambda s: s[1][:, :inner].T)
    g_ao = stacked(lambda s: s[1][:, inner:].T)
    g_zx = stacked(lambda s: s[2][:, : 2 * inner].reshape(block, 2, inner))
    g_q = stacked(lambda s: s[2][:, after : after + 128])
    g_dt = stacked(lambda s: s[2][:, after + 256 : after + 256 + heads])
    return (
        x_out,
        d_x,
        gain_sum[:, 0],
        gain_sum[:, 1],
        g_zx,
        g_bc,
        g_dt,
        conv_sum[:, :, :inner],
        g_conv_bc,
        head_part[:, 0, :heads],
        head_part[:, 1, :heads],
        head_part[:, 2, :heads],
        g_out,
        g_q,
        g_kv,
        g_ao,
        g_gu,
        g_down,
    )


def solution(mesh):
    return jax.shard_map(
        per_device,
        mesh=mesh,
        in_specs=(
            P("seq", None),
            P("seq", None),
            P(),
            P(),
            P(None, None, None, "wa"),
            P(),
            P(None, None, "wa"),
            P(None, None, "wa"),
            P(),
            P(None, "wa"),
            P(None, "wa"),
            P(None, "wa"),
            P(None, "wa", None),
            P(None, None, "wa"),
            P(),
            P(None, "wa", None),
            P(None, None, None, "wa"),
            P(None, "wa", None),
        ),
        out_specs=(
            P("seq", None),
            P("seq", None),
            P(),
            P(),
            P(None, "seq", None, "wa"),
            P(None, "seq", None),
            P(None, "seq", "wa"),
            P(None, None, "wa"),
            P(),
            P(None, "wa"),
            P(None, "wa"),
            P(None, "wa"),
            P(None, "wa", "seq"),
            P(None, "seq", "wa"),
            P(None, "seq", None, None),
            P(None, "wa", "seq"),
            P(None, "seq", None, "wa"),
            P(None, "wa", "seq"),
        ),
        check_vma=False,
    )
```

```python
import math

import jax
import jax.numpy as jnp
from jax import lax
from jax.experimental import pallas as pl
from jax.experimental.pallas import tpu as pltpu
from jax.sharding import PartitionSpec as P

MODEL_WIDTH = 1024
HEAD_SIZE = 64
NS = 128
KC = 4
QUERY_HEADS = 8
KEY_VALUE_HEADS = 2
LAYER_COUNT = 2
DIRECT_MOST = 8
VMEM_MIB = 48

eps = 1e-05
theta = 10000.0
neg_big = -1e30
score_scale = 1.0 / math.sqrt(HEAD_SIZE)

BF = jnp.bfloat16
F32 = jnp.float32
HI = lax.Precision.HIGHEST


def mm(a, b):
    return lax.dot_general(
        a.astype(BF), b.astype(BF), (((1,), (0,)), ((), ())), preferred_element_type=F32
    )


def mm_nt(a, b):
    return lax.dot_general(
        a.astype(BF), b.astype(BF), (((1,), (1,)), ((), ())), preferred_element_type=F32
    )


def mm_tn(a, b):
    return lax.dot_general(
        a.astype(BF), b.astype(BF), (((0,), (0,)), ((), ())), preferred_element_type=F32
    )


def mm_hi(a, b):
    return jnp.dot(a, b, precision=HI, preferred_element_type=F32)


def iota(shape, dim):
    return lax.broadcasted_iota(jnp.int32, shape, dim)


def sigmoid(v):
    return 1.0 / (1.0 + jnp.exp(-v))


def gather_seq(block):
    return lax.all_gather(block, "seq")


def scatter_rows(blocks):
    n = lax.axis_size("seq")
    if len(blocks) > 1:
        got = [
            lax.ppermute(blocks[d], "seq", [(i, (i + d) % n) for i in range(n)])
            for d in range(1, n)
        ]
        total = blocks[0].astype(F32)
        for part in got:
            total = total + part.astype(F32)
        return total
    return lax.psum_scatter(blocks[0], "seq", scatter_dimension=0, tiled=True).astype(F32)


def gather_wa(block):
    n = lax.axis_size("wa")
    return [block] + [
        lax.ppermute(block, "wa", [(i, (i + d) % n) for i in range(n)]) for d in range(1, n)
    ]


def scatter_wa(blocks):
    n = lax.axis_size("wa")
    return [blocks[0]] + [
        lax.ppermute(blocks[n - d], "wa", [(i, (i + d) % n) for i in range(n)])
        for d in range(1, n)
    ]


def arrive(*refs):
    pass


def kernel_call(name, body, outs, args, scratch=(), flops=0, ties=()):
    in_specs, arrays = [], []
    bytes_accessed = sum(math.prod(s) * jnp.dtype(k).itemsize for s, k in outs)
    for item in args:
        array, layer = item if isinstance(item, tuple) else (item, None)
        arrays.append(array)
        if layer is not None:
            rest = array.ndim - 1
            spec = pl.BlockSpec(
                (None,) + array.shape[1:], lambda i, layer=layer, rest=rest: (layer,) + (0,) * rest
            )
        elif array.ndim == 1:
            spec = pl.BlockSpec(memory_space=pltpu.SMEM)
        else:
            spec = pl.BlockSpec(array.shape, lambda i, rest=array.ndim: (0,) * rest)
        in_specs.append(spec)
        bytes_accessed += array.size * array.dtype.itemsize // (1 if layer is None else array.shape[0])
    count, gap = len(arrays), len(arrays) + len(ties)
    in_specs += [pl.BlockSpec(memory_space=pl.ANY)] * len(ties)

    def whole(*refs):
        body(*refs[:count], *refs[gap:])

    return pl.pallas_call(
        whole,
        grid=(1,),
        in_specs=in_specs,
        out_specs=[
            pl.BlockSpec(shape, lambda i, rest=len(shape): (0,) * rest) for shape, kind in outs
        ],
        out_shape=[jax.ShapeDtypeStruct(shape, kind) for shape, kind in outs],
        scratch_shapes=list(scratch),
        compiler_params=pltpu.CompilerParams(vmem_limit_bytes=VMEM_MIB * 1024 * 1024),
        cost_estimate=pl.CostEstimate(
            flops=flops, bytes_accessed=bytes_accessed, transcendentals=0
        ),
        name=name,
    )(*arrays, *ties)


def ordered(me_ref, parts, nat_ref):
    n = len(parts)
    rows = parts[0].shape[0]
    for d in range(n):
        at = pl.multiple_of(lax.rem(me_ref[0] + n - d, n) * rows, rows)
        nat_ref[pl.ds(at, rows), :] = parts[d][...]


def rotated(me_ref, nat_ref, blocks):
    n = len(blocks)
    rows = blocks[0].shape[0]
    for d in range(n):
        at = pl.multiple_of(lax.rem(me_ref[0] + n - d, n) * rows, rows)
        blocks[d][...] = nat_ref[pl.ds(at, rows), :].astype(blocks[d].dtype)


def halves_swapped(v):
    width = v.shape[1]
    half = HEAD_SIZE // 2
    first = iota(v.shape, 1) % HEAD_SIZE < half
    return jnp.where(first, pltpu.roll(v, width - half, 1), pltpu.roll(v, half, 1))


def expand(v, width):
    k = v.shape[1]
    pick = (iota((k, width), 1) // HEAD_SIZE == iota((k, width), 0)).astype(F32)
    return mm_hi(v, pick)


def head_sum(v):
    width = v.shape[1]
    pick = (iota((width, 128), 0) // HEAD_SIZE == iota((width, 128), 1)).astype(F32)
    return mm_hi(v, pick)


def decay_rows(block_decay):
    high = block_decay.astype(BF).astype(F32)
    low = block_decay - high
    row = iota((16, 128), 0)
    return jnp.where(row == 0, high, jnp.where(row == 1, low, 0.0)).astype(BF)


def fold_states(packs_ref, inner, here, later):
    arrive(packs_ref)
    heads = inner // HEAD_SIZE
    n = packs_ref.shape[0]

    def step(k, state):
        j = n - 1 - k if later else k
        tail = packs_ref[j, inner : inner + 16, :].astype(F32)
        decay = tail[0:1, :] + tail[1:2, :]
        full = jnp.concatenate(
            [jnp.broadcast_to(decay[:, h : h + 1], (HEAD_SIZE, NS)) for h in range(heads)], axis=0
        )
        return state * full + packs_ref[j, :inner, :].astype(F32)

    count = n - 1 - here if later else here
    return lax.fori_loop(0, count, step, jnp.zeros((inner, NS), F32))


def norm_first(hidden, gain):
    rows, width = hidden.shape

    def body(h_ref, g_ref, n_ref):
        h = h_ref[...]
        scale = lax.rsqrt(jnp.mean(h * h, axis=-1, keepdims=True) + eps)
        n_ref[...] = (h * scale * g_ref[...]).astype(BF)

    return kernel_call("norm_first", body, [((rows, width), BF)], [hidden, gain])[0]


def norm_step(parts, hidden, gain, ties=()):
    rows, width = hidden.shape
    n = len(parts)

    def body(*refs):
        h_ref, g_ref, out_ref, n_ref = refs[n:]
        total = refs[0][...]
        for part in refs[1:n]:
            total = total + part[...].astype(F32)
        h = h_ref[...] + total
        out_ref[...] = h
        scale = lax.rsqrt(jnp.mean(h * h, axis=-1, keepdims=True) + eps)
        n_ref[...] = (h * scale * g_ref[...]).astype(BF)

    return kernel_call(
        "norm_step",
        body,
        [((rows, width), F32), ((rows, width), BF)],
        [*parts, hidden, gain],
        ties=ties,
    )


def norm_back(parts, hidden, gain, grad):
    rows, width = hidden.shape
    n = len(parts)

    def body(*refs):
        h_ref, g_ref, grad_ref, out_ref, b_ref, gain_ref = refs[n:]
        total = refs[0][...]
        for part in refs[1:n]:
            total = total + part[...].astype(F32)
        h = h_ref[...]
        scale = lax.rsqrt(jnp.mean(h * h, axis=-1, keepdims=True) + eps)
        unit = h * scale
        through = total * g_ref[...]
        out = grad_ref[...] + scale * (
            through - unit * jnp.mean(through * unit, axis=-1, keepdims=True)
        )
        out_ref[...] = out
        b_ref[...] = out.astype(BF)
        gain_ref[...] = jnp.sum(total * unit, axis=0, keepdims=True)

    return kernel_call(
        "norm_back",
        body,
        [((rows, width), F32), ((rows, width), BF), ((1, width), F32)],
        [*parts, hidden, gain, grad],
    )


def project(me, parts, wzx, wbc, wdt, wq, kvw, cos_q, sin_q, cos_kv, sin_kv):
    n = len(parts)
    rows, width = parts[0].shape
    tokens = n * rows
    inner = wzx[0].shape[2] // 2
    mix = inner + 2 * NS

    def body(*refs):
        me_ref = refs[0]
        (
            kvw_ref, wq_ref, wdt_ref, wbc_ref, wzx_ref, cq_ref, sq_ref, ck_ref, sk_ref,
            nat_ref, gate_ref, u_ref, r_ref, kv_ref, q_ref,
        ) = refs[1 + n :]
        ordered(me_ref, refs[1 : 1 + n], nat_ref)
        x = nat_ref[...]
        kv = mm(x, kvw_ref[...])
        kv_ref[...] = (kv * ck_ref[...] + halves_swapped(kv) * sk_ref[...]).astype(BF)
        q = mm(x, wq_ref[...])
        q_ref[...] = (q * cq_ref[...] + halves_swapped(q) * sq_ref[...]).astype(BF)
        r_ref[...] = mm(x, wdt_ref[...])
        u_ref[:, inner:] = mm(x, wbc_ref[...])
        gate_ref[...] = mm(x, wzx_ref[:, :inner])
        u_ref[:, :inner] = mm(x, wzx_ref[:, inner:])

    return kernel_call(
        "project",
        body,
        [
            ((tokens, width), BF),
            ((tokens, inner), F32),
            ((tokens, mix), F32),
            ((tokens, 128), F32),
            ((tokens, 128), BF),
            ((tokens, 128), BF),
        ],
        [me, *parts, kvw, wq, wdt, wbc, wzx, cos_q, sin_q, cos_kv, sin_kv],
        flops=2 * tokens * width * 1408,
    )


def mixer_front(edge, u, r_raw, wzx, wbc, conv_w, hp, tok):
    tokens, mix = u.shape
    inner = mix - 2 * NS

    def body(
        edge_ref, u_ref, r_ref, wzx_ref, wbc_ref, cw_ref, hp_ref, tok_ref,
        pad_ref, act_ref, slope_ref, hd_ref, pack_ref,
    ):
        e = edge_ref[...]
        pad_ref[:16, :inner] = mm(e, wzx_ref[:, inner:])
        pad_ref[:16, inner:] = mm(e, wbc_ref[...])
        pad_ref[16:, :] = u_ref[...]
        tk = tok_ref[...]
        conv = jnp.broadcast_to(cw_ref[KC : KC + 1, :], (tokens, mix))
        for j in range(KC):
            shifted = pad_ref[16 - (KC - 1) + j : 16 - (KC - 1) + j + tokens, :]
            conv = conv + cw_ref[j : j + 1, :] * shifted * tk[:, j : j + 1]
        sg = sigmoid(conv)
        act = conv * sg
        act_ref[...] = act
        slope_ref[...] = sg * (1.0 + conv * (1.0 - sg))
        r = r_ref[...] + hp_ref[0:1, :]
        dt = jnp.maximum(r, 0.0) + jnp.log1p(jnp.exp(-jnp.abs(r)))
        log_decay = -dt * jnp.exp(hp_ref[1:2, :])
        lower = (iota((tokens, tokens), 0) >= iota((tokens, tokens), 1)).astype(F32)
        cum = mm_hi(lower, log_decay)
        hd_ref[0] = r
        hd_ref[1] = dt
        hd_ref[2] = cum
        last = cum[tokens - 1 :, :]
        to_last = jnp.where(tk[:, 5:6] > 0.5, jnp.exp(last - cum), 0.0)
        scaled = act[:, :inner] * expand(dt * to_last, inner)
        pack_ref[:inner, :] = mm_tn(scaled, act[:, inner : inner + NS]).astype(BF)
        pack_ref[inner:, :] = decay_rows(jnp.exp(last) * tk[tokens - 1 :, 4:5])

    return kernel_call(
        "mixer_front",
        body,
        [
            ((tokens + 16, mix), F32),
            ((tokens, mix), F32),
            ((tokens, mix), F32),
            ((3, tokens, 128), F32),
            ((inner + 16, NS), BF),
        ],
        [edge, u, r_raw, wzx, wbc, conv_w, hp, tok],
        flops=2 * tokens * tokens * 512,
    )


def query_rows(q):
    lane = iota(q.shape, 1)
    wide = q.astype(F32)
    return jnp.concatenate(
        [
            jnp.where(lane < HEAD_SIZE, wide, 0.0),
            jnp.where(lane < HEAD_SIZE, pltpu.roll(wide, HEAD_SIZE, 1), 0.0),
        ],
        axis=0,
    ).astype(BF)


def value_rows(v):
    lane = iota(v.shape, 1)
    wide = v.astype(F32)
    return jnp.concatenate(
        [
            jnp.where(lane >= HEAD_SIZE, pltpu.roll(wide, HEAD_SIZE, 1), 0.0),
            jnp.where(lane >= HEAD_SIZE, wide, 0.0),
        ],
        axis=0,
    )


def allowed_pair(segc, segr, tokens, steps_back):
    heads = segc.shape[0] // tokens
    row = iota((heads * tokens, tokens), 0) % tokens
    column = iota((heads * tokens, tokens), 1)
    return (segc == segr) & (column - tokens * steps_back <= row)


def within_decay(cum, cum_t, h, allowed):
    return jnp.exp(jnp.where(allowed, cum[:, h : h + 1] - cum_t[h : h + 1, :], neg_big))


def mixer_within(act, hd, segc, segrel, hp, inner):
    tokens = act.shape[0]

    def body(act_ref, hd_ref, segc_ref, segr_ref, hp_ref, y_ref):
        lane = iota((tokens, 128), 1)
        act_all = act_ref[...]
        b_mat = act_all[:, inner : inner + NS]
        c_mat = act_all[:, inner + NS :]
        both = mm_nt(c_mat, b_mat)
        dt, cum = hd_ref[1], hd_ref[2]
        cum_t = cum.T
        allowed = allowed_pair(segc_ref[...], segr_ref[0], tokens, 0)
        scaled = act_all[:, :inner] * expand(dt, inner)
        skip = expand(hp_ref[...], inner)[2:3, :]
        for p in range(inner // 128):
            cols = slice(128 * p, 128 * (p + 1))
            pair = [
                mm(within_decay(cum, cum_t, 2 * p + k, allowed) * both, scaled[:, cols])
                for k in range(2)
            ]
            y_ref[:, cols] = (
                jnp.where(lane < HEAD_SIZE, pair[0], pair[1])
                + skip[:, cols] * act_all[:, cols]
            )

    return kernel_call(
        "mixer_within",
        body,
        [((tokens, inner), F32)],
        [act, hd, segc, segrel, hp],
        flops=2 * tokens * tokens * 128 * 8,
    )[0]


def attend(here, every, q_own, segc, segrel, blocks):
    n = every.shape[0]
    tokens = segc.shape[0]
    rows = 2 * tokens

    def body(*refs):
        here_ref, all_ref, q_ref, segc_ref, segr_ref, nb_ref, o2_ref, flat_ref = refs
        arrive(all_ref, segr_ref)
        here_at = here_ref[0]
        q = query_rows(q_ref[...])
        seg_own = segc_ref[...]
        seg_two = jnp.concatenate([seg_own] * (rows // tokens), axis=0)

        def step(d, carry):
            top, total, out = carry
            kv = all_ref[here_at - d]
            allowed = allowed_pair(seg_two, segr_ref[d], tokens, d)
            scores = jnp.where(allowed, mm_nt(q, kv) * score_scale, neg_big)
            new_top = jnp.maximum(top, jnp.max(scores, axis=1, keepdims=True))
            weights = jnp.where(allowed, jnp.exp(scores - new_top), 0.0)
            shrink = jnp.exp(top - new_top)
            return (
                new_top,
                total * shrink + jnp.sum(weights, axis=1, keepdims=True),
                out * shrink + mm(weights, kv),
            )

        top, total, out = lax.fori_loop(
            0,
            nb_ref[0],
            step,
            (
                jnp.full((rows, 1), neg_big, F32),
                jnp.zeros((rows, 1), F32),
                jnp.zeros((rows, 128), F32),
            ),
        )
        out = out / total
        o2_ref[...] = jnp.where(iota((rows, 128), 1) == 0, top + jnp.log(total), out)
        lane = iota((tokens, 128), 1)
        flat_ref[...] = jnp.where(
            lane < HEAD_SIZE, pltpu.roll(out[:tokens], HEAD_SIZE, 1), out[tokens:]
        ).astype(BF)

    return kernel_call(
        "attend",
        body,
        [
            ((rows, 128), F32),
            ((tokens, 128), BF),
        ],
        [here, every, q_own, segc, segrel, blocks],
        flops=2 * rows * tokens * 128 * 2 * n,
    )


def mixer_out(me, here, states, y_local, act, hd, tok, gate, flat, wout, wao, wa_count):
    tokens, inner = y_local.shape
    width = wout[0].shape[2]
    rows = tokens // wa_count

    def body(*refs):
        me_ref, here_ref, all_ref = refs[:3]
        y_ref, act_ref, hd_ref, tok_ref, gate_ref, flat_ref, wout_ref, wao_ref = refs[3:11]
        state_ref, yy_ref, gated_ref = refs[11:14]
        blocks = refs[14 : 14 + wa_count]
        full_ref = refs[-1]
        state = fold_states(all_ref, inner, here_ref[0], False)
        state_ref[...] = state
        decay_in = jnp.exp(hd_ref[2]) * tok_ref[:, 4:5]
        y = y_ref[...] + mm_nt(act_ref[:, inner + NS :], state) * expand(decay_in, inner)
        yy_ref[...] = y
        gate_raw = gate_ref[...]
        gated = (y * gate_raw * sigmoid(gate_raw)).astype(BF)
        gated_ref[...] = gated
        full_ref[...] = mm(gated, wout_ref[...]) + mm(flat_ref[...], wao_ref[...])
        rotated(me_ref, full_ref, blocks)

    return kernel_call(
        "mixer_out",
        body,
        [((inner, NS), F32), ((tokens, inner), F32), ((tokens, inner), BF)]
        + [((rows, width), F32)]
        + [((rows, width), BF)] * (wa_count - 1),
        [me, here, states, y_local, act, hd, tok, gate, flat, wout, wao],
        scratch=[pltpu.VMEM((tokens, width), F32)],
        flops=2 * tokens * width * 512,
    )


def feed_forward(parts, wgu, wdown):
    n = len(parts)
    rows, width = parts[0].shape
    tokens = n * rows
    hidden = wdown[0].shape[1]

    def body(*refs):
        wgu_ref, wdown_ref, n_ref, gu_ref, act_ref = refs[n : n + 5]
        blocks = refs[n + 5 : n + 5 + n]
        for d in range(n):
            n_ref[d * rows : (d + 1) * rows, :] = refs[d][...]
        x = n_ref[...]
        gate = mm(x, wgu_ref[:, :hidden])
        up = mm(x, wgu_ref[:, hidden:])
        gu_ref[:, :hidden] = gate
        gu_ref[:, hidden:] = up
        act = (gate * sigmoid(gate) * up).astype(BF)
        act_ref[...] = act
        for d in range(n):
            blocks[d][...] = mm(act[d * rows : (d + 1) * rows], wdown_ref[...]).astype(
                blocks[d].dtype
            )

    return kernel_call(
        "feed_forward",
        body,
        [((tokens, width), BF), ((tokens, 2 * hidden), F32), ((tokens, hidden), BF)]
        + [((rows, width), F32)]
        + [((rows, width), BF)] * (n - 1),
        [*parts, wgu, wdown],
        flops=2 * tokens * width * 3 * hidden,
    )


def feed_back(parts, gu, wgu, wdown):
    n = len(parts)
    rows, width = parts[0].shape
    tokens = n * rows
    hidden = wdown[0].shape[1]

    def body(*refs):
        gu_ref, wgu_ref, wdown_ref, gb_ref, dgu_ref = refs[n : n + 5]
        blocks = refs[n + 5 : n + 5 + n]
        for d in range(n):
            gb_ref[d * rows : (d + 1) * rows, :] = refs[d][...]
        d_act = mm_nt(gb_ref[...], wdown_ref[...])
        gate = gu_ref[:, :hidden]
        up = gu_ref[:, hidden:]
        sg = sigmoid(gate)
        dgu_ref[:, :hidden] = (d_act * up * sg * (1.0 + gate * (1.0 - sg))).astype(BF)
        dgu_ref[:, hidden:] = (d_act * gate * sg).astype(BF)
        for d in range(n):
            blocks[d][...] = mm_nt(dgu_ref[d * rows : (d + 1) * rows, :], wgu_ref[...]).astype(
                blocks[d].dtype
            )

    return kernel_call(
        "feed_back",
        body,
        [((tokens, width), BF), ((tokens, 2 * hidden), BF)]
        + [((rows, width), F32)]
        + [((rows, width), BF)] * (n - 1),
        [*parts, gu, wgu, wdown],
        flops=2 * tokens * width * 3 * hidden,
    )


def weight_grads(here, pairs, n, direct, ties=()):
    width = pairs[0][0].shape[1]
    columns = sum(right.shape[1] for left, right in pairs)
    flat = [a for pair in pairs for a in pair]
    direct = direct and n <= DIRECT_MOST
    blocks = n if direct else 1
    rows = width // blocks

    def body(*refs):
        here_ref = refs[0]
        outs = refs[1 + len(flat) :]
        for d in range(blocks):
            start = 0
            for k in range(len(pairs)):
                left, right = refs[1 + 2 * k], refs[2 + 2 * k]
                wide = right.shape[1]
                if direct:
                    at = pl.multiple_of(lax.rem(here_ref[0] + d, n) * rows, rows)
                    piece = left[:, pl.ds(at, rows)]
                else:
                    piece = left[...]
                outs[d][:, start : start + wide] = mm_tn(piece, right[...]).astype(outs[d].dtype)
                start += wide

    return kernel_call(
        "weight_grads",
        body,
        [((rows, columns), F32 if direct and d == 0 else BF) for d in range(blocks)],
        [here, *flat],
        flops=2 * pairs[0][0].shape[0] * width * columns,
        ties=ties,
    )


def mixer_grad_in(me, parts, wout, wao, gate, y, act, hd, tok, o2, q_own):
    n = len(parts)
    rows, width = parts[0].shape
    tokens, inner = y.shape
    early = 96

    def body(*refs):
        me_ref = refs[0]
        wout_ref, wao_ref, gate_ref, y_ref, act_ref, hd_ref, tok_ref, o2_ref = refs[1 + n : 9 + n]
        q_ref, nat_ref, dy_ref, dgate_ref, pack_ref, da_ref, delta_ref = refs[9 + n :]
        ordered(me_ref, refs[1 : 1 + n], nat_ref)
        mb = nat_ref[...]
        d_gated = mm_nt(mb, wout_ref[...])
        gate_raw = gate_ref[...]
        sg = sigmoid(gate_raw)
        dy = d_gated * gate_raw * sg
        dy_ref[...] = dy
        dgate_ref[...] = (
            d_gated * y_ref[...] * sg * (1.0 + gate_raw * (1.0 - sg))
        ).astype(BF)
        cum = hd_ref[2]
        decay_in = jnp.exp(cum) * tok_ref[:, 4:5]
        pack_ref[:inner, :] = mm_tn(
            dy * expand(decay_in, inner), act_ref[:, inner + NS :]
        ).astype(BF)
        pack_ref[inner : inner + 16, :] = decay_rows(decay_in[tokens - 1 :, :])
        pack_ref[inner + 16 :, :] = q_ref[:early, :]
        da_ref[tokens + 16 :, :] = q_ref[early:, :]
        d_attn = mm_nt(mb, wao_ref[...])
        da_ref[:tokens, :] = d_attn.astype(BF)
        delta = jnp.sum(value_rows(d_attn) * o2_ref[...], axis=1, keepdims=True)
        delta_ref[...] = jnp.broadcast_to(delta, (2 * tokens, 128))
        lane = iota((tokens, 128), 1)
        table = jnp.zeros((tokens, 128), F32)
        columns = [
            o2_ref[:tokens, 0:1], o2_ref[tokens:, 0:1], delta[:tokens], delta[tokens:]
        ]
        for k in range(4):
            table = jnp.where((lane == k) | (lane == k + 4), columns[k], table)
        table = table.T[:8]
        high = table.astype(BF).astype(F32)
        table = jnp.where(iota(table.shape, 0) < 4, high, table - high)
        da_ref[tokens : tokens + 16, :] = jnp.concatenate(
            [table[:, 128 * k : 128 * (k + 1)] for k in range(tokens // 128)], axis=0
        ).astype(BF)

    return kernel_call(
        "mixer_grad_in",
        body,
        [
            ((tokens, width), BF),
            ((tokens, inner), F32),
            ((tokens, inner), BF),
            ((inner + 16 + early, NS), BF),
            ((tokens + 16 + tokens - early, 128), BF),
            ((2 * tokens, 128), F32),
        ],
        [me, *parts, wout, wao, gate, y, act, hd, tok, o2, q_own],
        flops=2 * tokens * width * 512,
    )


def attend_back(
    here, every, states_back, every_back, delta, o2, q_own, segc, segrel, seglater, blocks,
    cos_q, sin_q, cos_kv, sin_kv, inner,
):
    n = every.shape[0]
    tokens = segc.shape[0]
    rows = 2 * tokens

    def body(
        here_ref, all_ref, state_ref, back_ref, delta_ref, lse_ref, q_ref, segc_ref, segr_ref, segl_ref, nb_ref,
        cq_ref, sq_ref, ck_ref, sk_ref, dq_ref, dkv_ref,
    ):
        arrive(all_ref, state_ref, back_ref, segr_ref, segl_ref)
        here_at = here_ref[0]
        q = query_rows(q_ref[...])
        da = value_rows(back_ref[here_at, :tokens, :]).astype(BF)
        lse_col = lse_ref[:, 0:1]
        delta_col = delta_ref[:, 0:1]
        seg_own = segc_ref[...]
        seg_two = jnp.concatenate([seg_own] * 2, axis=0)

        def step(d, dq):
            kv = all_ref[here_at - d]
            allowed = allowed_pair(seg_two, segr_ref[d], tokens, d)
            scores = mm_nt(q, kv) * score_scale
            probs = jnp.exp(jnp.where(allowed, scores - lse_col, neg_big))
            d_scores = probs * (mm_nt(da, kv) - delta_col)
            return dq + mm(d_scores, kv)

        dq = lax.fori_loop(0, nb_ref[0], step, jnp.zeros((rows, 128), F32)) * score_scale
        lane = iota((tokens, 128), 1)
        flat = jnp.where(lane < HEAD_SIZE, dq[:tokens], pltpu.roll(dq[tokens:], HEAD_SIZE, 1))
        dq_ref[...] = (flat * cq_ref[...] - halves_swapped(flat) * sq_ref[...]).astype(BF)
        kv_own = all_ref[here_at]

        def back_step(d, dkv):
            j = here_at + d
            q_there = query_rows(
                jnp.concatenate(
                    [state_ref[j, inner + 16 :, :], back_ref[j, tokens + 16 :, :]], axis=0
                )
            )
            da_there = value_rows(back_ref[j, :tokens, :]).astype(BF)
            table = back_ref[j, tokens : tokens + 16, :].astype(F32)
            row = iota((tokens, tokens), 0)
            column = iota((tokens, tokens), 1)
            allowed = (seg_own == segl_ref[d]) & (row <= column + tokens * d)
            d_key = jnp.zeros((tokens, 128), F32)
            d_value = jnp.zeros((tokens, 128), F32)
            for k in range(2):

                def line(r):
                    return jnp.concatenate(
                        [
                            table[8 * i + r : 8 * i + r + 1] + table[8 * i + r + 4 : 8 * i + r + 5]
                            for i in range(tokens // 128)
                        ],
                        axis=1,
                    )

                mine = slice(k * tokens, (k + 1) * tokens)
                scores = mm_nt(kv_own, q_there[mine]) * score_scale
                probs = jnp.exp(jnp.where(allowed, scores - line(k), neg_big))
                d_scores = probs * (mm_nt(kv_own, da_there[mine]) - line(2 + k))
                d_key = d_key + mm(d_scores, q_there[mine])
                d_value = d_value + mm(probs, da_there[mine])
            return dkv + (d_key * score_scale + d_value)

        dkv = lax.fori_loop(0, nb_ref[1], back_step, jnp.zeros((tokens, 128), F32))
        dkv_ref[...] = (dkv * ck_ref[...] - halves_swapped(dkv) * sk_ref[...]).astype(BF)

    return kernel_call(
        "attend_back",
        body,
        [((tokens, 128), BF), ((tokens, 128), BF)],
        [
            here, every, states_back, every_back, delta, o2, q_own, segc, segrel, seglater, blocks,
            cos_q, sin_q, cos_kv, sin_kv,
        ],
        flops=2 * rows * tokens * 128 * 7 * n,
    )


def mixer_grad(here, every_back, state_in, dy, act, slope, pad, hd, tok, segc, segrel, hp, conv_w):
    tokens, inner = dy.shape
    mix = act.shape[1]

    def body(*refs):
        (
            here_ref, back_ref, state_ref, dy_ref, act_ref, slope_ref, pad_ref, hd_ref, tok_ref, segc_ref, segr_ref,
            hp_ref, cw_ref, dmix_ref, tail_ref, edge_ref, ddt_ref, gconv_ref, ghead_ref,
            dconv_ref, dpad_ref, dxs_ref,
        ) = refs
        later = fold_states(back_ref, inner, here_ref[0], True)
        state = state_ref[...]
        tk = tok_ref[...]
        act_all = act_ref[...]
        x = act_all[:, :inner]
        b_mat = act_all[:, inner : inner + NS]
        c_mat = act_all[:, inner + NS :]
        dy_all = dy_ref[...]
        r, dt, cum = hd_ref[0], hd_ref[1], hd_ref[2]
        cum_t = cum.T
        last = cum[tokens - 1 :, :]
        to_last = jnp.where(tk[:, 5:6] > 0.5, jnp.exp(last - cum), 0.0)
        decay_in = jnp.exp(cum) * tk[:, 4:5]
        dt_wide = expand(dt, inner)
        last_wide = expand(to_last, inner)
        in_wide = expand(decay_in, inner)
        xs = x * dt_wide
        allowed = allowed_pair(segc_ref[...], segr_ref[0], tokens, 0)
        both = mm_nt(c_mat, b_mat)
        lane = iota((tokens, 128), 1)
        lane_row = iota((128, tokens), 0)
        d_both = jnp.zeros((tokens, tokens), F32)
        d_cum = jnp.zeros((tokens, 128), F32)
        d_cum_t = jnp.zeros((128, tokens), F32)
        for p in range(inner // 128):
            cols = slice(128 * p, 128 * (p + 1))
            xs_pair = xs[:, cols].astype(BF)
            dy_pair = dy_all[:, cols]
            pieces = []
            for k in range(2):
                h = 2 * p + k
                decay = within_decay(cum, cum_t, h, allowed)
                weight = decay * both
                mine = (lane >= HEAD_SIZE) if k else (lane < HEAD_SIZE)
                d_weight = mm_nt(jnp.where(mine, dy_pair, 0.0), xs_pair)
                d_both = d_both + d_weight * decay
                flow = d_weight * weight
                d_cum = d_cum + jnp.where(lane == h, jnp.sum(flow, axis=1, keepdims=True), 0.0)
                d_cum_t = d_cum_t + jnp.where(
                    lane_row == h, jnp.sum(flow, axis=0, keepdims=True), 0.0
                )
                pieces.append(mm_tn(weight, dy_pair))
            dxs_ref[:, cols] = jnp.where(lane < HEAD_SIZE, pieces[0], pieces[1])
        from_state = mm_nt(b_mat, later)
        d_xs = dxs_ref[...] + from_state * last_wide
        dy_in = dy_all * in_wide
        inflow = mm_nt(c_mat, state)
        d_c = mm(d_both, b_mat) + mm(dy_in, state)
        d_b = mm_tn(d_both, c_mat) + mm(xs * last_wide, later)
        carried = head_sum(from_state * xs * last_wide)
        d_cum = d_cum - d_cum_t.T + head_sum(dy_in * inflow) - carried
        row_sum = jnp.sum(later * state, axis=1, keepdims=True)
        pick = (iota((inner, 128), 0) // HEAD_SIZE == iota((inner, 128), 1)).astype(F32)
        d_decay = jnp.sum(row_sum * pick, axis=0, keepdims=True)
        d_last = jnp.sum(carried, axis=0, keepdims=True) + decay_in[tokens - 1 :, :] * d_decay
        d_cum = d_cum + jnp.where(iota((tokens, 128), 0) == tokens - 1, d_last, 0.0)
        upper = (iota((tokens, tokens), 0) <= iota((tokens, tokens), 1)).astype(F32)
        d_log = mm_hi(upper, d_cum)
        rate = jnp.exp(hp_ref[1:2, :])
        d_dt = head_sum(d_xs * x) - rate * d_log
        d_r = d_dt * sigmoid(r)
        ddt_ref[...] = d_r.astype(BF)
        g_bias = jnp.sum(d_r, axis=0, keepdims=True)
        g_log = -jnp.sum(d_log * dt, axis=0, keepdims=True) * rate
        g_skip = jnp.sum(head_sum(dy_all * x), axis=0, keepdims=True)
        row8 = iota((8, 128), 0)
        ghead_ref[...] = jnp.where(
            row8 == 0, g_bias, jnp.where(row8 == 1, g_log, jnp.where(row8 == 2, g_skip, 0.0))
        )
        skip = expand(hp_ref[...], inner)[2:3, :]
        dconv_ref[:, :inner] = (dy_all * skip + d_xs * dt_wide) * slope_ref[:, :inner]
        dconv_ref[:, inner : inner + NS] = d_b * slope_ref[:, inner : inner + NS]
        dconv_ref[:, inner + NS :] = d_c * slope_ref[:, inner + NS :]
        dpad_ref[...] = jnp.zeros((tokens + 16, mix), F32)
        gconv_ref[...] = jnp.zeros((8, mix), F32)
        dconv = dconv_ref[...]
        gconv_ref[KC : KC + 1, :] = jnp.sum(dconv, axis=0, keepdims=True)
        for j in range(KC):
            at = 16 - (KC - 1) + j
            used = dconv * tk[:, j : j + 1]
            gconv_ref[j : j + 1, :] = jnp.sum(
                used * pad_ref[at : at + tokens, :], axis=0, keepdims=True
            )
            dpad_ref[at : at + tokens, :] = (
                dpad_ref[at : at + tokens, :] + used * cw_ref[j : j + 1, :]
            )
        dmix_ref[...] = dpad_ref[16:, :].astype(BF)
        tail_ref[...] = dpad_ref[tokens:, :]
        edge_ref[...] = dpad_ref[8:16, :]

    return kernel_call(
        "mixer_grad",
        body,
        [
            ((tokens, mix), BF),
            ((16, mix), F32),
            ((8, mix), F32),
            ((tokens, 128), BF),
            ((8, mix), F32),
            ((8, 128), F32),
        ],
        [here, every_back, state_in, dy, act, slope, pad, hd, tok, segc, segrel, hp, conv_w],
        scratch=[
            pltpu.VMEM((tokens, mix), F32),
            pltpu.VMEM((tokens + 16, mix), F32),
            pltpu.VMEM((tokens, inner), F32),
        ],
        flops=2 * tokens * tokens * 128 * 24,
    )


def grads_out(
    me, dgate, dmix, tail, next_edge, ddt, dq, dkv, wzx, wbc, wdt, wq, kvw, wa_count
):
    tokens, inner = dgate.shape
    mix = dmix.shape[1]
    width = wzx[0].shape[1]
    rows = tokens // wa_count

    def body(
        me_ref, dgate_ref, dmix_ref, tail_ref, edge_ref, ddt_ref, dq_ref, dkv_ref,
        wzx_ref, wbc_ref, wdt_ref, wq_ref, kvw_ref, dx_ref, dbc_ref, *rest,
    ):
        blocks, full_ref = rest[:-1], rest[-1]
        ends = tail_ref[...] + jnp.concatenate([jnp.zeros((8, mix), F32), edge_ref[...]], axis=0)
        for ref, cols in ((dx_ref, slice(0, inner)), (dbc_ref, slice(inner, mix))):
            ref[: tokens - 16, :] = dmix_ref[: tokens - 16, cols]
            ref[tokens - 16 :, :] = ends[:, cols].astype(BF)
        full_ref[...] = (
            mm_nt(ddt_ref[...], wdt_ref[...])
            + mm_nt(dq_ref[...], wq_ref[...])
            + mm_nt(dkv_ref[...], kvw_ref[...])
            + mm_nt(dbc_ref[...], wbc_ref[...])
            + mm_nt(dgate_ref[...], wzx_ref[:, :inner])
            + mm_nt(dx_ref[...], wzx_ref[:, inner:])
        )
        rotated(me_ref, full_ref, blocks)

    return kernel_call(
        "grads_out",
        body,
        [((tokens, inner), BF), ((tokens, 2 * NS), BF), ((rows, width), F32)]
        + [((rows, width), BF)] * (wa_count - 1),
        [me, dgate, dmix, tail, next_edge, ddt, dq, dkv, wzx, wbc, wdt, wq, kvw],
        scratch=[pltpu.VMEM((tokens, width), F32)],
        flops=2 * tokens * width * (mix + 768),
    )


def all_rows(me, parts):
    n = len(parts)
    rows, width = parts[0].shape

    def body(*refs):
        for d in range(n):
            at = pl.multiple_of(lax.rem(refs[0][0] + n - d, n) * rows, rows)
            refs[-1][pl.ds(at, rows), :] = refs[1 + d][...].astype(F32)

    return kernel_call("all_rows", body, [((n * rows, width), F32)], [me, *parts])[0]


def held_back(arrays, ties):
    count = len(arrays)

    def body(*refs):
        pass

    return pl.pallas_call(
        body,
        in_specs=[pl.BlockSpec(memory_space=pl.ANY)] * (count + len(ties)),
        out_specs=[pl.BlockSpec(memory_space=pl.ANY)] * count,
        out_shape=[jax.ShapeDtypeStruct(a.shape, a.dtype) for a in arrays],
        input_output_aliases={i: i for i in range(count)},
        name="held_back",
    )(*arrays, *ties)


def pack_small(gains, convs, heads, inner, ties):
    width = gains[0].shape[1]
    mix = convs[0].shape[1]
    pieces = [(g, 0, 0, width) for g in range(len(gains))]
    at = len(gains)
    pieces += [(at + k, j, inner, mix) for k in range(len(convs)) for j in range(KC + 1)]
    pieces += [(at + k, j, 0, inner) for k in range(len(convs)) for j in range(KC + 1)]
    at += len(convs)
    pieces += [(at + k, j, 0, 128) for k in range(len(heads)) for j in range(8)]
    total = sum((end - start) // 128 for _, _, start, end in pieces)

    def body(*refs):
        row = 0
        for source, line, start, end in pieces:
            for c in range(start, end, 128):
                refs[-1][row : row + 1, :] = refs[source][line : line + 1, c : c + 128]
                row += 1

    return kernel_call(
        "pack_small", body, [((total, 128), F32)], [*gains, *convs, *heads], ties=ties
    )[0]


def per_device(
    x_in,
    d_out,
    segment_ids,
    norm_gains,
    w_zx,
    w_bc,
    w_dt,
    conv_x,
    conv_bc,
    dt_bias,
    a_log,
    d_skip,
    w_out,
    w_q,
    key_value_weight,
    w_ao,
    w_gu,
    w_down,
):
    seq_count = lax.axis_size("seq")
    wa_count = lax.axis_size("wa")
    tokens, width = x_in.shape
    rows = tokens // wa_count
    seq_here = lax.axis_index("seq")
    wa_here = lax.axis_index("wa")
    start_row = seq_here * tokens
    inner = w_zx.shape[3]
    heads = w_dt.shape[2]
    hidden = w_gu.shape[3]
    query_local = w_q.shape[2] // HEAD_SIZE
    group = QUERY_HEADS // KEY_VALUE_HEADS
    kv_head = wa_here * query_local // group
    me = wa_here.astype(jnp.int32).reshape(1)
    here = seq_here.astype(jnp.int32).reshape(1)

    seg_blocks = segment_ids.reshape(seq_count, tokens)
    seg_here = lax.dynamic_slice_in_dim(segment_ids, start_row, tokens)
    seg_padded = jnp.concatenate([jnp.full((KC - 1,), -1, jnp.int32), segment_ids])
    seg_edge = lax.dynamic_slice_in_dim(seg_padded, start_row, KC - 1)
    seg_full = jnp.concatenate([seg_edge, seg_here])
    steps = jnp.arange(seq_count, dtype=jnp.int32)
    segrel = jnp.where(
        (steps <= seq_here)[:, None], seg_blocks[(seq_here - steps) % seq_count], -1
    )
    seglater = jnp.where(
        (steps + seq_here < seq_count)[:, None], seg_blocks[(seq_here + steps) % seq_count], -1
    )
    blocks_used = jnp.stack(
        [
            1 + jnp.sum((segrel[1:, tokens - 1] == seg_here[0]).astype(jnp.int32)),
            1 + jnp.sum((seglater[1:, 0] == seg_here[tokens - 1]).astype(jnp.int32)),
        ]
    ).astype(jnp.int32)
    segrel = segrel[:, None, :]
    seglater = seglater[:, None, :]
    segc = seg_here[:, None]
    columns = [(seg_full[j : j + tokens] == seg_here).astype(F32) for j in range(KC)]
    columns.append((seg_here == seg_edge[KC - 2]).astype(F32))
    columns.append((seg_here == seg_here[tokens - 1]).astype(F32))
    tok = jnp.pad(jnp.stack(columns, axis=1), ((0, 0), (0, 128 - len(columns))))
    half = HEAD_SIZE // 2
    frequency = jnp.exp(jnp.arange(half, dtype=F32) * (-math.log(theta) / half))
    positions = (start_row + jnp.arange(tokens, dtype=jnp.int32)).astype(F32)
    angles = positions[:, None] * frequency[None, :]
    cosine, sine = jnp.cos(angles), jnp.sin(angles)
    cos_q = jnp.concatenate([cosine] * 4, axis=1)
    sin_q = jnp.concatenate([-sine, sine, -sine, sine], axis=1)
    ones = jnp.ones((tokens, HEAD_SIZE), F32)
    cos_kv = jnp.concatenate([cosine, cosine, ones], axis=1)
    sin_kv = jnp.concatenate([-sine, sine, 0.0 * ones], axis=1)

    wzx_all = w_zx.reshape(LAYER_COUNT, width, 2 * inner)
    wgu_all = w_gu.reshape(LAYER_COUNT, width, 2 * hidden)
    wdt_all = jnp.pad(w_dt, ((0, 0), (0, 0), (0, 128 - heads)))
    kvw_all = lax.dynamic_slice_in_dim(
        key_value_weight, kv_head * HEAD_SIZE, HEAD_SIZE, axis=3
    ).reshape(LAYER_COUNT, width, 2 * HEAD_SIZE)
    conv_all = jnp.pad(
        jnp.concatenate([conv_x, conv_bc], axis=2), ((0, 0), (0, 8 - (KC + 1)), (0, 0))
    )
    hp_all = jnp.pad(
        jnp.stack([dt_bias, a_log, d_skip], axis=1), ((0, 0), (0, 5), (0, 128 - heads))
    )

    def own_rows(array):
        return lax.dynamic_slice_in_dim(array, wa_here * rows, rows)

    h = own_rows(x_in)
    normed = norm_first(h, norm_gains[0, 0][None, :])
    saved = []
    for layer in range(LAYER_COUNT):
        wzx, wbc, wdt, wq = [(a, layer) for a in (wzx_all, w_bc, wdt_all, w_q)]
        kvw, conv_w, hp = [(a, layer) for a in (kvw_all, conv_all, hp_all)]
        wout, wao, wgu, wdown = [(a, layer) for a in (w_out, w_ao, wgu_all, w_down)]
        normed_parts = gather_wa(normed)
        edge = jnp.zeros((16, width), BF)
        for d, part in enumerate(normed_parts):
            edge = jnp.where((wa_here + wa_count - d) % wa_count == wa_count - 1, part[rows - 16 :], edge)
        edge = lax.ppermute(edge, "seq", [(i, i + 1) for i in range(seq_count - 1)])
        nat, gate, u, r_raw, kv, q_own = project(
            me, normed_parts, wzx, wbc, wdt, wq, kvw, cos_q, sin_q, cos_kv, sin_kv
        )
        every = gather_seq(kv)
        pad, act, slope, hd, pack = mixer_front(
            edge, u, r_raw, wzx, wbc, conv_w, hp, tok
        )
        states = gather_seq(pack)
        y_local = mixer_within(act, hd, segc, segrel, hp, inner)
        o2, flat = attend(here, every, q_own, segc, segrel, blocks_used)
        state_in, y, gated, *parts = mixer_out(
            me, here, states, y_local, act, hd, tok, gate, flat, wout, wao, wa_count
        )
        mixed, normed_two = norm_step(scatter_wa(parts), h, norm_gains[layer, 1][None, :])
        n2, gu, act_ff, *parts = feed_forward(gather_wa(normed_two), wgu, wdown)
        saved.append(
            (h, nat, every, q_own, gate, pad, act, slope, hd, o2, flat, state_in, y, gated,
             mixed, n2, gu, act_ff)
        )
        if layer + 1 < LAYER_COUNT:
            h, normed = norm_step(scatter_wa(parts), mixed, norm_gains[layer + 1, 0][None, :])

    last_parts = parts
    last_mixed = mixed

    grad = own_rows(d_out)
    grad_parts = [
        lax.dynamic_slice_in_dim(d_out, (wa_here + wa_count - d) % wa_count * rows, rows).astype(BF)
        for d in range(wa_count)
    ]
    sums = [None] * LAYER_COUNT
    small = [None] * LAYER_COUNT
    for layer in reversed(range(LAYER_COUNT)):
        wzx, wbc, wdt, wq = [(a, layer) for a in (wzx_all, w_bc, wdt_all, w_q)]
        kvw, conv_w, hp = [(a, layer) for a in (kvw_all, conv_all, hp_all)]
        wout, wao, wgu, wdown = [(a, layer) for a in (w_out, w_ao, wgu_all, w_down)]
        (h_in, nat, every, q_own, gate, pad, act, slope, hd, o2, flat, state_in, y, gated,
         mixed, n2, gu, act_ff) = saved[layer]
        gb, dgu, *parts = feed_back(grad_parts, gu, wgu, wdown)
        parts = scatter_wa(parts)
        sum_ff = scatter_rows(
            weight_grads(here, [(gb, act_ff), (n2, dgu)], seq_count, False, [parts[1]])
        )
        d_mixed, mixed_b, gain_two = norm_back(
            parts, mixed, norm_gains[layer, 1][None, :], grad
        )
        mixed_parts = gather_wa(mixed_b)
        mb, dy, dgate, pack, da, delta = mixer_grad_in(
            me, mixed_parts, wout, wao, gate, y, act, hd, tok, o2, q_own
        )
        states_back = gather_seq(pack)
        every_back = gather_seq(da)
        dq, dkv = attend_back(
            here, every, states_back, every_back, delta, o2, q_own, segc, segrel, seglater,
            blocks_used, cos_q, sin_q, cos_kv, sin_kv, inner,
        )
        if layer == LAYER_COUNT - 1:
            out_parts = scatter_wa(held_back(last_parts, [delta]))
            h = norm_step(out_parts, last_mixed, norm_gains[layer, 0][None, :], [dq])[0]
        dmix, tail, edge_grad, ddt, gconv, ghead = mixer_grad(
            here, states_back, state_in, dy, act, slope, pad, hd, tok, segc, segrel, hp, conv_w
        )
        next_edge = lax.ppermute(
            edge_grad, "seq", [(i + 1, i) for i in range(seq_count - 1)]
        )
        dx, dbc, *parts = grads_out(
            me, dgate, dmix, tail, next_edge, ddt, dq, dkv, wzx, wbc, wdt, wq, kvw, wa_count
        )
        parts = scatter_wa(parts)
        mix_pairs = [(mb, gated), (mb, flat), (nat, dgate), (nat, dq)]
        if layer:
            sum_mix = scatter_rows(
                weight_grads(here, mix_pairs, seq_count, False, [parts[1]])
            )
        else:
            sum_mix = scatter_rows(weight_grads(here, mix_pairs, seq_count, False))
            sum_every = scatter_rows(
                weight_grads(here, [(nat, dbc), (nat, dkv)], seq_count, True)
            )
            sum_in = scatter_rows(weight_grads(here, [(nat, dx), (nat, ddt)], seq_count, True))
        grad, grad_b, gain_one = norm_back(
            parts, h_in, norm_gains[layer, 0][None, :], d_mixed
        )
        grad_parts = gather_wa(grad_b)
        if layer:
            joint = scatter_rows(
                weight_grads(
                    here, [(nat, dbc), (nat, dkv), (nat, dx), (nat, ddt)], seq_count, False,
                    [grad_parts[1]],
                )
            )
            ends = 2 * NS + 128
            sum_every, sum_in = joint[:, :ends], joint[:, ends:]
            x_parts = gather_wa(held_back([h.astype(BF)], [grad_parts[-1]])[0])
        sums[layer] = (sum_ff, sum_mix, sum_in, sum_every)
        small[layer] = (gain_one, gain_two, gconv, ghead)
    x_out = all_rows(me, x_parts)
    d_x = all_rows(me, grad_parts)

    mix = inner + 2 * NS
    local = pack_small(
        [small[layer][k] for layer in range(LAYER_COUNT) for k in (0, 1)],
        [small[layer][2] for layer in range(LAYER_COUNT)],
        [small[layer][3] for layer in range(LAYER_COUNT)],
        inner,
        [grad_parts[1]],
    )
    local = jnp.sum(gather_seq(local), axis=0)
    gain_rows = 2 * LAYER_COUNT * width // 128
    shared_rows = gain_rows + LAYER_COUNT * (KC + 1) * 2 * NS // 128
    shared = sum(gather_wa(local[:shared_rows]))
    gain_sum = shared[:gain_rows].reshape(LAYER_COUNT, 2, width)
    g_conv_bc = shared[gain_rows:].reshape(LAYER_COUNT, KC + 1, 2 * NS)
    local = local[shared_rows:]
    conv_rows = LAYER_COUNT * (KC + 1) * (inner // 128)
    g_conv_x = local[:conv_rows].reshape(LAYER_COUNT, KC + 1, inner)
    head_part = local[conv_rows:].reshape(LAYER_COUNT, 8, 128)

    every = jnp.stack([s[3] for s in sums]).astype(BF)
    every_parts = gather_wa(every)
    g_bc = sum(part[:, :, : 2 * NS].astype(F32) for part in every_parts)
    kv_columns = []
    for head in range(KEY_VALUE_HEADS):
        total = 0.0
        for d, part in enumerate(every_parts):
            source = (wa_here + wa_count - d) % wa_count * query_local // group
            total = total + jnp.where(source == head, part[:, :, 2 * NS :].astype(F32), 0.0)
        kv_columns.append(total.reshape(total.shape[0], total.shape[1], 2, HEAD_SIZE))
    g_kv = jnp.concatenate(kv_columns, axis=3)

    block = sums[0][0].shape[0]

    def stacked(pick):
        return jnp.stack([pick(s) for s in sums])

    g_down = stacked(lambda s: s[0][:, :hidden].T)
    g_gu = stacked(lambda s: s[0][:, hidden:].reshape(block, 2, hidden))
    ends = inner + 128
    g_out = stacked(lambda s: s[1][:, :inner].T)
    g_ao = stacked(lambda s: s[1][:, inner:ends].T)
    g_zx = stacked(
        lambda s: jnp.stack([s[1][:, ends : ends + inner], s[2][:, :inner]], axis=1)
    )
    g_q = stacked(lambda s: s[1][:, ends + inner :])
    g_dt = stacked(lambda s: s[2][:, inner : inner + heads])
    return (
        x_out,
        d_x,
        gain_sum[:, 0],
        gain_sum[:, 1],
        g_zx,
        g_bc,
        g_dt,
        g_conv_x,
        g_conv_bc,
        head_part[:, 0, :heads],
        head_part[:, 1, :heads],
        head_part[:, 2, :heads],
        g_out,
        g_q,
        g_kv,
        g_ao,
        g_gu,
        g_down,
    )


def solution(mesh):
    return jax.shard_map(
        per_device,
        mesh=mesh,
        in_specs=(
            P("seq", None),
            P("seq", None),
            P(),
            P(),
            P(None, None, None, "wa"),
            P(),
            P(None, None, "wa"),
            P(None, None, "wa"),
            P(),
            P(None, "wa"),
            P(None, "wa"),
            P(None, "wa"),
            P(None, "wa", None),
            P(None, None, "wa"),
            P(),
            P(None, "wa", None),
            P(None, None, None, "wa"),
            P(None, "wa", None),
        ),
        out_specs=(
            P("seq", None),
            P("seq", None),
            P(),
            P(),
            P(None, "seq", None, "wa"),
            P(None, "seq", None),
            P(None, "seq", "wa"),
            P(None, None, "wa"),
            P(),
            P(None, "wa"),
            P(None, "wa"),
            P(None, "wa"),
            P(None, "wa", "seq"),
            P(None, "seq", "wa"),
            P(None, "seq", None, None),
            P(None, "wa", "seq"),
            P(None, "seq", None, "wa"),
            P(None, "wa", "seq"),
        ),
        check_vma=False,
    )
```

```python
import math

import jax
import jax.numpy as jnp
from jax import lax
from jax.experimental import pallas as pl
from jax.experimental.pallas import tpu as pltpu
from jax.sharding import PartitionSpec as P

MODEL_WIDTH = 1024
HEAD_SIZE = 64
NS = 128
KC = 4
QUERY_HEADS = 8
KEY_VALUE_HEADS = 2
LAYER_COUNT = 2
DIRECT_MOST = 8
VMEM_MIB = 48

eps = 1e-05
theta = 10000.0
neg_big = -1e30
score_scale = 1.0 / math.sqrt(HEAD_SIZE)

BF = jnp.bfloat16
F32 = jnp.float32
HI = lax.Precision.HIGHEST


def mm(a, b):
    return lax.dot_general(
        a.astype(BF), b.astype(BF), (((1,), (0,)), ((), ())), preferred_element_type=F32
    )


def mm_nt(a, b):
    return lax.dot_general(
        a.astype(BF), b.astype(BF), (((1,), (1,)), ((), ())), preferred_element_type=F32
    )


def mm_tn(a, b):
    return lax.dot_general(
        a.astype(BF), b.astype(BF), (((0,), (0,)), ((), ())), preferred_element_type=F32
    )


def mm_hi(a, b):
    return jnp.dot(a, b, precision=HI, preferred_element_type=F32)


def iota(shape, dim):
    return lax.broadcasted_iota(jnp.int32, shape, dim)


def sigmoid(v):
    return 1.0 / (1.0 + jnp.exp(-v))


def gather_seq(block):
    return lax.all_gather(block, "seq")


def scatter_rows(blocks):
    n = lax.axis_size("seq")
    if len(blocks) > 1:
        got = [
            lax.ppermute(blocks[d], "seq", [(i, (i + d) % n) for i in range(n)])
            for d in range(1, n)
        ]
        total = blocks[0].astype(F32)
        for part in got:
            total = total + part.astype(F32)
        return total
    return lax.psum_scatter(blocks[0], "seq", scatter_dimension=0, tiled=True)


def gather_wa(block):
    n = lax.axis_size("wa")
    return [block] + [
        lax.ppermute(block, "wa", [(i, (i + d) % n) for i in range(n)]) for d in range(1, n)
    ]


def scatter_wa(blocks):
    n = lax.axis_size("wa")
    return [blocks[0]] + [
        lax.ppermute(blocks[n - d], "wa", [(i, (i + d) % n) for i in range(n)])
        for d in range(1, n)
    ]


def arrive(*refs):
    pass


def kernel_call(name, body, outs, args, scratch=(), flops=0, ties=()):
    in_specs, arrays = [], []
    bytes_accessed = sum(math.prod(s) * jnp.dtype(k).itemsize for s, k in outs)
    for item in args:
        array, layer = item if isinstance(item, tuple) else (item, None)
        arrays.append(array)
        if layer is not None:
            rest = array.ndim - 1
            spec = pl.BlockSpec(
                (None,) + array.shape[1:], lambda i, layer=layer, rest=rest: (layer,) + (0,) * rest
            )
        elif array.ndim == 1:
            spec = pl.BlockSpec(memory_space=pltpu.SMEM)
        else:
            spec = pl.BlockSpec(array.shape, lambda i, rest=array.ndim: (0,) * rest)
        in_specs.append(spec)
        bytes_accessed += array.size * array.dtype.itemsize // (1 if layer is None else array.shape[0])
    count, gap = len(arrays), len(arrays) + len(ties)
    in_specs += [pl.BlockSpec(memory_space=pl.ANY)] * len(ties)

    def whole(*refs):
        body(*refs[:count], *refs[gap:])

    return pl.pallas_call(
        whole,
        grid=(1,),
        in_specs=in_specs,
        out_specs=[
            pl.BlockSpec(shape, lambda i, rest=len(shape): (0,) * rest) for shape, kind in outs
        ],
        out_shape=[jax.ShapeDtypeStruct(shape, kind) for shape, kind in outs],
        scratch_shapes=list(scratch),
        compiler_params=pltpu.CompilerParams(vmem_limit_bytes=VMEM_MIB * 1024 * 1024),
        cost_estimate=pl.CostEstimate(
            flops=flops, bytes_accessed=bytes_accessed, transcendentals=0
        ),
        name=name,
    )(*arrays, *ties)


def ordered(me_ref, parts, nat_ref):
    n = len(parts)
    rows = parts[0].shape[0]
    for d in range(n):
        at = pl.multiple_of(lax.rem(me_ref[0] + n - d, n) * rows, rows)
        nat_ref[pl.ds(at, rows), :] = parts[d][...]


def rotated(me_ref, nat_ref, blocks):
    n = len(blocks)
    rows = blocks[0].shape[0]
    for d in range(n):
        at = pl.multiple_of(lax.rem(me_ref[0] + n - d, n) * rows, rows)
        blocks[d][...] = nat_ref[pl.ds(at, rows), :].astype(blocks[d].dtype)


def halves_swapped(v):
    width = v.shape[1]
    half = HEAD_SIZE // 2
    first = iota(v.shape, 1) % HEAD_SIZE < half
    return jnp.where(first, pltpu.roll(v, width - half, 1), pltpu.roll(v, half, 1))


def expand(v, width):
    k = v.shape[1]
    pick = (iota((k, width), 1) // HEAD_SIZE == iota((k, width), 0)).astype(F32)
    return mm_hi(v, pick)


def head_sum(v):
    width = v.shape[1]
    pick = (iota((width, 128), 0) // HEAD_SIZE == iota((width, 128), 1)).astype(F32)
    return mm_hi(v, pick)


def decay_rows(block_decay):
    high = block_decay.astype(BF).astype(F32)
    low = block_decay - high
    row = iota((16, 128), 0)
    return jnp.where(row == 0, high, jnp.where(row == 1, low, 0.0)).astype(BF)


def fold_states(packs_ref, inner, here, later):
    arrive(packs_ref)
    heads = inner // HEAD_SIZE
    n = packs_ref.shape[0]

    def step(k, state):
        j = n - 1 - k if later else k
        tail = packs_ref[j, inner : inner + 16, :].astype(F32)
        decay = tail[0:1, :] + tail[1:2, :]
        full = jnp.concatenate(
            [jnp.broadcast_to(decay[:, h : h + 1], (HEAD_SIZE, NS)) for h in range(heads)], axis=0
        )
        return state * full + packs_ref[j, :inner, :].astype(F32)

    count = n - 1 - here if later else here
    return lax.fori_loop(0, count, step, jnp.zeros((inner, NS), F32))


def norm_first(hidden, gain):
    rows, width = hidden.shape

    def body(h_ref, g_ref, n_ref):
        h = h_ref[...]
        scale = lax.rsqrt(jnp.mean(h * h, axis=-1, keepdims=True) + eps)
        n_ref[...] = (h * scale * g_ref[...]).astype(BF)

    return kernel_call("norm_first", body, [((rows, width), BF)], [hidden, gain])[0]


def norm_step(parts, hidden, gain, ties=()):
    rows, width = hidden.shape
    n = len(parts)

    def body(*refs):
        h_ref, g_ref, out_ref, n_ref = refs[n:]
        total = refs[0][...]
        for part in refs[1:n]:
            total = total + part[...].astype(F32)
        h = h_ref[...] + total
        out_ref[...] = h
        scale = lax.rsqrt(jnp.mean(h * h, axis=-1, keepdims=True) + eps)
        n_ref[...] = (h * scale * g_ref[...]).astype(BF)

    return kernel_call(
        "norm_step",
        body,
        [((rows, width), F32), ((rows, width), BF)],
        [*parts, hidden, gain],
        ties=ties,
    )


def norm_back(parts, hidden, gain, grad, ties):
    rows, width = hidden.shape
    n = len(parts)

    def body(*refs):
        h_ref, g_ref, grad_ref, out_ref, b_ref, gain_ref = refs[n:]
        total = refs[0][...]
        for part in refs[1:n]:
            total = total + part[...].astype(F32)
        h = h_ref[...]
        scale = lax.rsqrt(jnp.mean(h * h, axis=-1, keepdims=True) + eps)
        unit = h * scale
        through = total * g_ref[...]
        out = grad_ref[...] + scale * (
            through - unit * jnp.mean(through * unit, axis=-1, keepdims=True)
        )
        out_ref[...] = out
        b_ref[...] = out.astype(BF)
        gain_ref[...] = jnp.sum(total * unit, axis=0, keepdims=True)

    return kernel_call(
        "norm_back",
        body,
        [((rows, width), F32), ((rows, width), BF), ((1, width), F32)],
        [*parts, hidden, gain, grad],
        ties=ties,
    )


def project(me, parts, wzx, wbc, wdt, wq, kvw, cos_q, sin_q, cos_kv, sin_kv):
    n = len(parts)
    rows, width = parts[0].shape
    tokens = n * rows
    inner = wzx[0].shape[2] // 2
    mix = inner + 2 * NS

    def body(*refs):
        me_ref = refs[0]
        (
            kvw_ref, wq_ref, wdt_ref, wbc_ref, wzx_ref, cq_ref, sq_ref, ck_ref, sk_ref,
            nat_ref, gate_ref, u_ref, r_ref, kv_ref, q_ref,
        ) = refs[1 + n :]
        ordered(me_ref, refs[1 : 1 + n], nat_ref)
        x = nat_ref[...]
        kv = mm(x, kvw_ref[...])
        kv_ref[...] = (kv * ck_ref[...] + halves_swapped(kv) * sk_ref[...]).astype(BF)
        q = mm(x, wq_ref[...])
        q_ref[...] = (q * cq_ref[...] + halves_swapped(q) * sq_ref[...]).astype(BF)
        r_ref[...] = mm(x, wdt_ref[...])
        u_ref[:, inner:] = mm(x, wbc_ref[...])
        gate_ref[...] = mm(x, wzx_ref[:, :inner]).astype(BF)
        u_ref[:, :inner] = mm(x, wzx_ref[:, inner:])

    return kernel_call(
        "project",
        body,
        [
            ((tokens, width), BF),
            ((tokens, inner), BF),
            ((tokens, mix), F32),
            ((tokens, 128), F32),
            ((tokens, 128), BF),
            ((tokens, 128), BF),
        ],
        [me, *parts, kvw, wq, wdt, wbc, wzx, cos_q, sin_q, cos_kv, sin_kv],
        flops=2 * tokens * width * 1408,
    )


def convolved(pad_ref, cw_ref, tk, tokens):
    mix = pad_ref.shape[1]
    conv = jnp.broadcast_to(cw_ref[KC : KC + 1, :], (tokens, mix))
    for j in range(KC):
        at = 16 - (KC - 1) + j
        conv = conv + cw_ref[j : j + 1, :] * pad_ref[at : at + tokens, :] * tk[:, j : j + 1]
    return conv


def mixer_front(edge, u, r_raw, wzx, wbc, conv_w, hp, tok):
    tokens, mix = u.shape
    inner = mix - 2 * NS

    def body(
        edge_ref, u_ref, r_ref, wzx_ref, wbc_ref, cw_ref, hp_ref, tok_ref,
        pad_ref, act_ref, hd_ref, pack_ref,
    ):
        e = edge_ref[...]
        pad_ref[:16, :inner] = mm(e, wzx_ref[:, inner:])
        pad_ref[:16, inner:] = mm(e, wbc_ref[...])
        pad_ref[16:, :] = u_ref[...]
        tk = tok_ref[...]
        conv = convolved(pad_ref, cw_ref, tk, tokens)
        act = conv * sigmoid(conv)
        act_ref[...] = act.astype(BF)
        r = r_ref[...] + hp_ref[0:1, :]
        dt = jnp.maximum(r, 0.0) + jnp.log1p(jnp.exp(-jnp.abs(r)))
        log_decay = -dt * jnp.exp(hp_ref[1:2, :])
        lower = (iota((tokens, tokens), 0) >= iota((tokens, tokens), 1)).astype(F32)
        cum = mm_hi(lower, log_decay)
        hd_ref[0] = r
        hd_ref[1] = dt
        hd_ref[2] = cum
        last = cum[tokens - 1 :, :]
        to_last = jnp.where(tk[:, 5:6] > 0.5, jnp.exp(last - cum), 0.0)
        scaled = act[:, :inner] * expand(dt * to_last, inner)
        pack_ref[:inner, :] = mm_tn(scaled, act[:, inner : inner + NS]).astype(BF)
        pack_ref[inner:, :] = decay_rows(jnp.exp(last) * tk[tokens - 1 :, 4:5])

    return kernel_call(
        "mixer_front",
        body,
        [
            ((tokens + 16, mix), F32),
            ((tokens, mix), BF),
            ((3, tokens, 128), F32),
            ((inner + 16, NS), BF),
        ],
        [edge, u, r_raw, wzx, wbc, conv_w, hp, tok],
        flops=2 * tokens * tokens * 512,
    )


def query_rows(q):
    lane = iota(q.shape, 1)
    wide = q.astype(F32)
    return jnp.concatenate(
        [
            jnp.where(lane < HEAD_SIZE, wide, 0.0),
            jnp.where(lane < HEAD_SIZE, pltpu.roll(wide, HEAD_SIZE, 1), 0.0),
        ],
        axis=0,
    ).astype(BF)


def value_rows(v):
    lane = iota(v.shape, 1)
    wide = v.astype(F32)
    return jnp.concatenate(
        [
            jnp.where(lane >= HEAD_SIZE, pltpu.roll(wide, HEAD_SIZE, 1), 0.0),
            jnp.where(lane >= HEAD_SIZE, wide, 0.0),
        ],
        axis=0,
    )


def allowed_pair(segc, segr, tokens, steps_back):
    heads = segc.shape[0] // tokens
    row = iota((heads * tokens, tokens), 0) % tokens
    column = iota((heads * tokens, tokens), 1)
    return (segc == segr) & (column - tokens * steps_back <= row)


def within_decay(cum, cum_t, h, allowed):
    return jnp.exp(jnp.where(allowed, cum[:, h : h + 1] - cum_t[h : h + 1, :], neg_big))


def mixer_within(act, hd, segc, segrel, hp, inner):
    tokens = act.shape[0]

    def body(act_ref, hd_ref, segc_ref, segr_ref, hp_ref, y_ref):
        lane = iota((tokens, 128), 1)
        act_all = act_ref[...].astype(F32)
        b_mat = act_all[:, inner : inner + NS]
        c_mat = act_all[:, inner + NS :]
        both = mm_nt(c_mat, b_mat)
        dt, cum = hd_ref[1], hd_ref[2]
        cum_t = cum.T
        allowed = allowed_pair(segc_ref[...], segr_ref[0], tokens, 0)
        scaled = act_all[:, :inner] * expand(dt, inner)
        skip = expand(hp_ref[...], inner)[2:3, :]
        for p in range(inner // 128):
            cols = slice(128 * p, 128 * (p + 1))
            pair = [
                mm(within_decay(cum, cum_t, 2 * p + k, allowed) * both, scaled[:, cols])
                for k in range(2)
            ]
            y_ref[:, cols] = (
                jnp.where(lane < HEAD_SIZE, pair[0], pair[1])
                + skip[:, cols] * act_all[:, cols]
            )

    return kernel_call(
        "mixer_within",
        body,
        [((tokens, inner), F32)],
        [act, hd, segc, segrel, hp],
        flops=2 * tokens * tokens * 128 * 8,
    )[0]


def attend(here, every, q_own, segc, segrel, blocks):
    n = every.shape[0]
    tokens = segc.shape[0]
    rows = 2 * tokens

    def body(*refs):
        here_ref, all_ref, q_ref, segc_ref, segr_ref, nb_ref, o2_ref, flat_ref = refs
        arrive(all_ref, segr_ref)
        here_at = here_ref[0]
        q = query_rows(q_ref[...])
        seg_own = segc_ref[...]
        seg_two = jnp.concatenate([seg_own] * (rows // tokens), axis=0)

        def step(d, carry):
            top, total, out = carry
            kv = all_ref[here_at - d]
            allowed = allowed_pair(seg_two, segr_ref[d], tokens, d)
            scores = jnp.where(allowed, mm_nt(q, kv) * score_scale, neg_big)
            new_top = jnp.maximum(top, jnp.max(scores, axis=1, keepdims=True))
            weights = jnp.where(allowed, jnp.exp(scores - new_top), 0.0)
            shrink = jnp.exp(top - new_top)
            return (
                new_top,
                total * shrink + jnp.sum(weights, axis=1, keepdims=True),
                out * shrink + mm(weights, kv),
            )

        top, total, out = lax.fori_loop(
            0,
            nb_ref[0],
            step,
            (
                jnp.full((rows, 1), neg_big, F32),
                jnp.zeros((rows, 1), F32),
                jnp.zeros((rows, 128), F32),
            ),
        )
        out = out / total
        o2_ref[...] = jnp.where(iota((rows, 128), 1) == 0, top + jnp.log(total), out)
        lane = iota((tokens, 128), 1)
        flat_ref[...] = jnp.where(
            lane < HEAD_SIZE, pltpu.roll(out[:tokens], HEAD_SIZE, 1), out[tokens:]
        ).astype(BF)

    return kernel_call(
        "attend",
        body,
        [
            ((rows, 128), F32),
            ((tokens, 128), BF),
        ],
        [here, every, q_own, segc, segrel, blocks],
        flops=2 * rows * tokens * 128 * 2 * n,
    )


def mixer_out(me, here, states, y_local, act, hd, tok, gate, flat, wout, wao, wa_count):
    tokens, inner = y_local.shape
    width = wout[0].shape[2]
    rows = tokens // wa_count

    def body(*refs):
        me_ref, here_ref, all_ref = refs[:3]
        y_ref, act_ref, hd_ref, tok_ref, gate_ref, flat_ref, wout_ref, wao_ref = refs[3:11]
        state_ref, yy_ref, gated_ref = refs[11:14]
        blocks = refs[14 : 14 + wa_count]
        full_ref = refs[-1]
        state = fold_states(all_ref, inner, here_ref[0], False)
        state_ref[...] = state
        decay_in = jnp.exp(hd_ref[2]) * tok_ref[:, 4:5]
        y = y_ref[...] + mm_nt(act_ref[:, inner + NS :], state) * expand(decay_in, inner)
        yy_ref[...] = y.astype(BF)
        gate_raw = gate_ref[...].astype(F32)
        gated = (y * gate_raw * sigmoid(gate_raw)).astype(BF)
        gated_ref[...] = gated
        full_ref[...] = mm(gated, wout_ref[...]) + mm(flat_ref[...], wao_ref[...])
        rotated(me_ref, full_ref, blocks)

    return kernel_call(
        "mixer_out",
        body,
        [((inner, NS), F32), ((tokens, inner), BF), ((tokens, inner), BF)]
        + [((rows, width), F32)]
        + [((rows, width), BF)] * (wa_count - 1),
        [me, here, states, y_local, act, hd, tok, gate, flat, wout, wao],
        scratch=[pltpu.VMEM((tokens, width), F32)],
        flops=2 * tokens * width * 512,
    )


def feed_forward(parts, wgu, wdown):
    n = len(parts)
    rows, width = parts[0].shape
    tokens = n * rows
    hidden = wdown[0].shape[1]

    def body(*refs):
        wgu_ref, wdown_ref, n_ref, gu_ref, act_ref = refs[n : n + 5]
        blocks = refs[n + 5 : n + 5 + n]
        for d in range(n):
            n_ref[d * rows : (d + 1) * rows, :] = refs[d][...]
        x = n_ref[...]
        gate = mm(x, wgu_ref[:, :hidden])
        up = mm(x, wgu_ref[:, hidden:])
        gu_ref[:, :hidden] = gate.astype(BF)
        gu_ref[:, hidden:] = up.astype(BF)
        act = (gate * sigmoid(gate) * up).astype(BF)
        act_ref[...] = act
        for d in range(n):
            blocks[d][...] = mm(act[d * rows : (d + 1) * rows], wdown_ref[...]).astype(
                blocks[d].dtype
            )

    return kernel_call(
        "feed_forward",
        body,
        [((tokens, width), BF), ((tokens, 2 * hidden), BF), ((tokens, hidden), BF)]
        + [((rows, width), F32)]
        + [((rows, width), BF)] * (n - 1),
        [*parts, wgu, wdown],
        flops=2 * tokens * width * 3 * hidden,
    )


def feed_back(parts, gu, wgu, wdown):
    n = len(parts)
    rows, width = parts[0].shape
    tokens = n * rows
    hidden = wdown[0].shape[1]

    def body(*refs):
        gu_ref, wgu_ref, wdown_ref, gb_ref, dgu_ref = refs[n : n + 5]
        blocks = refs[n + 5 : n + 5 + n]
        for d in range(n):
            gb_ref[d * rows : (d + 1) * rows, :] = refs[d][...]
        d_act = mm_nt(gb_ref[...], wdown_ref[...])
        gate = gu_ref[:, :hidden].astype(F32)
        up = gu_ref[:, hidden:].astype(F32)
        sg = sigmoid(gate)
        dgu_ref[:, :hidden] = (d_act * up * sg * (1.0 + gate * (1.0 - sg))).astype(BF)
        dgu_ref[:, hidden:] = (d_act * gate * sg).astype(BF)
        for d in range(n):
            blocks[d][...] = mm_nt(dgu_ref[d * rows : (d + 1) * rows, :], wgu_ref[...]).astype(
                blocks[d].dtype
            )

    return kernel_call(
        "feed_back",
        body,
        [((tokens, width), BF), ((tokens, 2 * hidden), BF)]
        + [((rows, width), F32)]
        + [((rows, width), BF)] * (n - 1),
        [*parts, gu, wgu, wdown],
        flops=2 * tokens * width * 3 * hidden,
    )


def weight_grads(here, groups, n, ties=()):
    width = groups[0][0][0][0].shape[1]
    flat = [a for pairs, _ in groups for pair in pairs for a in pair]
    plan, shapes = [], []
    for pairs, direct in groups:
        blocks = n if direct and n <= DIRECT_MOST else 1
        columns = sum(right.shape[1] for _, right in pairs)
        plan.append((len(pairs), blocks))
        shapes += [
            ((width // blocks, columns), F32 if blocks > 1 and d == 0 else BF)
            for d in range(blocks)
        ]

    def body(*refs):
        here_ref = refs[0]
        source, out = 1, 1 + len(flat)
        for count, blocks in plan:
            for d in range(blocks):
                rows = width // blocks
                start = 0
                for k in range(count):
                    left, right = refs[source + 2 * k], refs[source + 2 * k + 1]
                    if blocks > 1:
                        at = pl.multiple_of(lax.rem(here_ref[0] + d, n) * rows, rows)
                        piece = left[:, pl.ds(at, rows)]
                    else:
                        piece = left[...]
                    wide = right.shape[1]
                    target = refs[out + d]
                    target[:, start : start + wide] = mm_tn(piece, right[...]).astype(target.dtype)
                    start += wide
            source += 2 * count
            out += blocks

    got = kernel_call(
        "weight_grads",
        body,
        shapes,
        [here, *flat],
        flops=2 * flat[0].shape[0] * width * sum(a.shape[1] for a in flat[1::2]),
        ties=ties,
    )
    out = []
    for _, blocks in plan:
        out.append(got[:blocks])
        got = got[blocks:]
    return out


def mixer_grad_in(me, parts, wout, wao, gate, y, act, hd, tok, o2, q_own):
    n = len(parts)
    rows, width = parts[0].shape
    tokens, inner = y.shape
    early = 96

    def body(*refs):
        me_ref = refs[0]
        wout_ref, wao_ref, gate_ref, y_ref, act_ref, hd_ref, tok_ref, o2_ref = refs[1 + n : 9 + n]
        q_ref, nat_ref, dy_ref, dgate_ref, pack_ref, da_ref, delta_ref = refs[9 + n :]
        ordered(me_ref, refs[1 : 1 + n], nat_ref)
        mb = nat_ref[...]
        d_gated = mm_nt(mb, wout_ref[...])
        gate_raw = gate_ref[...].astype(F32)
        sg = sigmoid(gate_raw)
        dy = d_gated * gate_raw * sg
        dy_ref[...] = dy.astype(BF)
        dgate_ref[...] = (
            d_gated * y_ref[...].astype(F32) * sg * (1.0 + gate_raw * (1.0 - sg))
        ).astype(BF)
        cum = hd_ref[2]
        decay_in = jnp.exp(cum) * tok_ref[:, 4:5]
        pack_ref[:inner, :] = mm_tn(
            dy * expand(decay_in, inner), act_ref[:, inner + NS :]
        ).astype(BF)
        pack_ref[inner : inner + 16, :] = decay_rows(decay_in[tokens - 1 :, :])
        pack_ref[inner + 16 :, :] = q_ref[:early, :]
        da_ref[tokens + 16 :, :] = q_ref[early:, :]
        d_attn = mm_nt(mb, wao_ref[...])
        da_ref[:tokens, :] = d_attn.astype(BF)
        delta = jnp.sum(value_rows(d_attn) * o2_ref[...], axis=1, keepdims=True)
        delta_ref[...] = jnp.broadcast_to(delta, (2 * tokens, 128))
        lane = iota((tokens, 128), 1)
        table = jnp.zeros((tokens, 128), F32)
        columns = [
            o2_ref[:tokens, 0:1], o2_ref[tokens:, 0:1], delta[:tokens], delta[tokens:]
        ]
        for k in range(4):
            table = jnp.where((lane == k) | (lane == k + 4), columns[k], table)
        table = table.T[:8]
        high = table.astype(BF).astype(F32)
        table = jnp.where(iota(table.shape, 0) < 4, high, table - high)
        da_ref[tokens : tokens + 16, :] = jnp.concatenate(
            [table[:, 128 * k : 128 * (k + 1)] for k in range(tokens // 128)], axis=0
        ).astype(BF)

    return kernel_call(
        "mixer_grad_in",
        body,
        [
            ((tokens, width), BF),
            ((tokens, inner), BF),
            ((tokens, inner), BF),
            ((inner + 16 + early, NS), BF),
            ((tokens + 16 + tokens - early, 128), BF),
            ((2 * tokens, 128), F32),
        ],
        [me, *parts, wout, wao, gate, y, act, hd, tok, o2, q_own],
        flops=2 * tokens * width * 512,
    )


def attend_back(
    here, every, states_back, every_back, delta, o2, q_own, segc, segrel, seglater, blocks,
    cos_q, sin_q, cos_kv, sin_kv, inner, ties,
):
    n = every.shape[0]
    tokens = segc.shape[0]
    rows = 2 * tokens

    def body(
        here_ref, all_ref, state_ref, back_ref, delta_ref, lse_ref, q_ref, segc_ref, segr_ref, segl_ref, nb_ref,
        cq_ref, sq_ref, ck_ref, sk_ref, dq_ref, dkv_ref,
    ):
        arrive(all_ref, state_ref, back_ref, segr_ref, segl_ref)
        here_at = here_ref[0]
        q = query_rows(q_ref[...])
        da = value_rows(back_ref[here_at, :tokens, :]).astype(BF)
        lse_col = lse_ref[:, 0:1]
        delta_col = delta_ref[:, 0:1]
        seg_own = segc_ref[...]
        seg_two = jnp.concatenate([seg_own] * 2, axis=0)

        def step(d, dq):
            kv = all_ref[here_at - d]
            allowed = allowed_pair(seg_two, segr_ref[d], tokens, d)
            scores = mm_nt(q, kv) * score_scale
            probs = jnp.exp(jnp.where(allowed, scores - lse_col, neg_big))
            d_scores = probs * (mm_nt(da, kv) - delta_col)
            return dq + mm(d_scores, kv)

        dq = lax.fori_loop(0, nb_ref[0], step, jnp.zeros((rows, 128), F32)) * score_scale
        lane = iota((tokens, 128), 1)
        flat = jnp.where(lane < HEAD_SIZE, dq[:tokens], pltpu.roll(dq[tokens:], HEAD_SIZE, 1))
        dq_ref[...] = (flat * cq_ref[...] - halves_swapped(flat) * sq_ref[...]).astype(BF)
        kv_own = all_ref[here_at]

        def back_step(d, dkv):
            j = here_at + d
            q_there = query_rows(
                jnp.concatenate(
                    [state_ref[j, inner + 16 :, :], back_ref[j, tokens + 16 :, :]], axis=0
                )
            )
            da_there = value_rows(back_ref[j, :tokens, :]).astype(BF)
            table = back_ref[j, tokens : tokens + 16, :].astype(F32)
            row = iota((tokens, tokens), 0)
            column = iota((tokens, tokens), 1)
            allowed = (seg_own == segl_ref[d]) & (row <= column + tokens * d)
            d_key = jnp.zeros((tokens, 128), F32)
            d_value = jnp.zeros((tokens, 128), F32)
            for k in range(2):

                def line(r):
                    return jnp.concatenate(
                        [
                            table[8 * i + r : 8 * i + r + 1] + table[8 * i + r + 4 : 8 * i + r + 5]
                            for i in range(tokens // 128)
                        ],
                        axis=1,
                    )

                mine = slice(k * tokens, (k + 1) * tokens)
                scores = mm_nt(kv_own, q_there[mine]) * score_scale
                probs = jnp.exp(jnp.where(allowed, scores - line(k), neg_big))
                d_scores = probs * (mm_nt(kv_own, da_there[mine]) - line(2 + k))
                d_key = d_key + mm(d_scores, q_there[mine])
                d_value = d_value + mm(probs, da_there[mine])
            return dkv + (d_key * score_scale + d_value)

        dkv = lax.fori_loop(0, nb_ref[1], back_step, jnp.zeros((tokens, 128), F32))
        dkv_ref[...] = (dkv * ck_ref[...] - halves_swapped(dkv) * sk_ref[...]).astype(BF)

    return kernel_call(
        "attend_back",
        body,
        [((tokens, 128), BF), ((tokens, 128), BF)],
        [
            here, every, states_back, every_back, delta, o2, q_own, segc, segrel, seglater, blocks,
            cos_q, sin_q, cos_kv, sin_kv,
        ],
        flops=2 * rows * tokens * 128 * 7 * n,
        ties=ties,
    )


def mixer_grad(here, every_back, state_in, dy, pad, hd, tok, segc, segrel, hp, conv_w):
    tokens, inner = dy.shape
    mix = pad.shape[1]

    def body(*refs):
        (
            here_ref, back_ref, state_ref, dy_ref, pad_ref, hd_ref, tok_ref, segc_ref, segr_ref,
            hp_ref, cw_ref, dmix_ref, tail_ref, edge_ref, ddt_ref, gconv_ref, ghead_ref,
            dconv_ref, dpad_ref, dxs_ref, slope_ref,
        ) = refs
        later = fold_states(back_ref, inner, here_ref[0], True)
        state = state_ref[...]
        tk = tok_ref[...]
        conv = convolved(pad_ref, cw_ref, tk, tokens)
        sg = sigmoid(conv)
        slope_ref[...] = sg * (1.0 + conv * (1.0 - sg))
        act_all = conv * sg
        x = act_all[:, :inner]
        b_mat = act_all[:, inner : inner + NS]
        c_mat = act_all[:, inner + NS :]
        dy_all = dy_ref[...].astype(F32)
        r, dt, cum = hd_ref[0], hd_ref[1], hd_ref[2]
        cum_t = cum.T
        last = cum[tokens - 1 :, :]
        to_last = jnp.where(tk[:, 5:6] > 0.5, jnp.exp(last - cum), 0.0)
        decay_in = jnp.exp(cum) * tk[:, 4:5]
        dt_wide = expand(dt, inner)
        last_wide = expand(to_last, inner)
        in_wide = expand(decay_in, inner)
        xs = x * dt_wide
        allowed = allowed_pair(segc_ref[...], segr_ref[0], tokens, 0)
        both = mm_nt(c_mat, b_mat)
        lane = iota((tokens, 128), 1)
        lane_row = iota((128, tokens), 0)
        d_both = jnp.zeros((tokens, tokens), F32)
        d_cum = jnp.zeros((tokens, 128), F32)
        d_cum_t = jnp.zeros((128, tokens), F32)
        for p in range(inner // 128):
            cols = slice(128 * p, 128 * (p + 1))
            xs_pair = xs[:, cols].astype(BF)
            dy_pair = dy_all[:, cols]
            pieces = []
            for k in range(2):
                h = 2 * p + k
                decay = within_decay(cum, cum_t, h, allowed)
                weight = decay * both
                mine = (lane >= HEAD_SIZE) if k else (lane < HEAD_SIZE)
                d_weight = mm_nt(jnp.where(mine, dy_pair, 0.0), xs_pair)
                d_both = d_both + d_weight * decay
                flow = d_weight * weight
                d_cum = d_cum + jnp.where(lane == h, jnp.sum(flow, axis=1, keepdims=True), 0.0)
                d_cum_t = d_cum_t + jnp.where(
                    lane_row == h, jnp.sum(flow, axis=0, keepdims=True), 0.0
                )
                pieces.append(mm_tn(weight, dy_pair))
            dxs_ref[:, cols] = jnp.where(lane < HEAD_SIZE, pieces[0], pieces[1])
        from_state = mm_nt(b_mat, later)
        d_xs = dxs_ref[...] + from_state * last_wide
        dy_in = dy_all * in_wide
        inflow = mm_nt(c_mat, state)
        d_c = mm(d_both, b_mat) + mm(dy_in, state)
        d_b = mm_tn(d_both, c_mat) + mm(xs * last_wide, later)
        carried = head_sum(from_state * xs * last_wide)
        d_cum = d_cum - d_cum_t.T + head_sum(dy_in * inflow) - carried
        row_sum = jnp.sum(later * state, axis=1, keepdims=True)
        pick = (iota((inner, 128), 0) // HEAD_SIZE == iota((inner, 128), 1)).astype(F32)
        d_decay = jnp.sum(row_sum * pick, axis=0, keepdims=True)
        d_last = jnp.sum(carried, axis=0, keepdims=True) + decay_in[tokens - 1 :, :] * d_decay
        d_cum = d_cum + jnp.where(iota((tokens, 128), 0) == tokens - 1, d_last, 0.0)
        upper = (iota((tokens, tokens), 0) <= iota((tokens, tokens), 1)).astype(F32)
        d_log = mm_hi(upper, d_cum)
        rate = jnp.exp(hp_ref[1:2, :])
        d_dt = head_sum(d_xs * x) - rate * d_log
        d_r = d_dt * sigmoid(r)
        ddt_ref[...] = d_r.astype(BF)
        g_bias = jnp.sum(d_r, axis=0, keepdims=True)
        g_log = -jnp.sum(d_log * dt, axis=0, keepdims=True) * rate
        g_skip = jnp.sum(head_sum(dy_all * x), axis=0, keepdims=True)
        row8 = iota((8, 128), 0)
        ghead_ref[...] = jnp.where(
            row8 == 0, g_bias, jnp.where(row8 == 1, g_log, jnp.where(row8 == 2, g_skip, 0.0))
        )
        skip = expand(hp_ref[...], inner)[2:3, :]
        dconv_ref[:, :inner] = (dy_all * skip + d_xs * dt_wide) * slope_ref[:, :inner]
        dconv_ref[:, inner : inner + NS] = d_b * slope_ref[:, inner : inner + NS]
        dconv_ref[:, inner + NS :] = d_c * slope_ref[:, inner + NS :]
        dpad_ref[...] = jnp.zeros((tokens + 16, mix), F32)
        gconv_ref[...] = jnp.zeros((8, mix), F32)
        dconv = dconv_ref[...]
        gconv_ref[KC : KC + 1, :] = jnp.sum(dconv, axis=0, keepdims=True)
        for j in range(KC):
            at = 16 - (KC - 1) + j
            used = dconv * tk[:, j : j + 1]
            gconv_ref[j : j + 1, :] = jnp.sum(
                used * pad_ref[at : at + tokens, :], axis=0, keepdims=True
            )
            dpad_ref[at : at + tokens, :] = (
                dpad_ref[at : at + tokens, :] + used * cw_ref[j : j + 1, :]
            )
        dmix_ref[...] = dpad_ref[16:, :].astype(BF)
        tail_ref[...] = dpad_ref[tokens:, :]
        edge_ref[...] = dpad_ref[8:16, :]

    return kernel_call(
        "mixer_grad",
        body,
        [
            ((tokens, mix), BF),
            ((16, mix), F32),
            ((8, mix), F32),
            ((tokens, 128), BF),
            ((8, mix), F32),
            ((8, 128), F32),
        ],
        [here, every_back, state_in, dy, pad, hd, tok, segc, segrel, hp, conv_w],
        scratch=[
            pltpu.VMEM((tokens, mix), F32),
            pltpu.VMEM((tokens + 16, mix), F32),
            pltpu.VMEM((tokens, inner), F32),
            pltpu.VMEM((tokens, mix), F32),
        ],
        flops=2 * tokens * tokens * 128 * 24,
    )


def grads_out(
    me, dgate, dmix, tail, next_edge, ddt, dq, dkv, wzx, wbc, wdt, wq, kvw, wa_count, ties
):
    tokens, inner = dgate.shape
    mix = dmix.shape[1]
    width = wzx[0].shape[1]
    rows = tokens // wa_count

    def body(
        me_ref, dgate_ref, dmix_ref, tail_ref, edge_ref, ddt_ref, dq_ref, dkv_ref,
        wzx_ref, wbc_ref, wdt_ref, wq_ref, kvw_ref, dx_ref, dbc_ref, *rest,
    ):
        blocks, full_ref = rest[:-1], rest[-1]
        ends = tail_ref[...] + jnp.concatenate([jnp.zeros((8, mix), F32), edge_ref[...]], axis=0)
        for ref, cols in ((dx_ref, slice(0, inner)), (dbc_ref, slice(inner, mix))):
            ref[: tokens - 16, :] = dmix_ref[: tokens - 16, cols]
            ref[tokens - 16 :, :] = ends[:, cols].astype(BF)
        full_ref[...] = (
            mm_nt(ddt_ref[...], wdt_ref[...])
            + mm_nt(dq_ref[...], wq_ref[...])
            + mm_nt(dkv_ref[...], kvw_ref[...])
            + mm_nt(dbc_ref[...], wbc_ref[...])
            + mm_nt(dgate_ref[...], wzx_ref[:, :inner])
            + mm_nt(dx_ref[...], wzx_ref[:, inner:])
        )
        rotated(me_ref, full_ref, blocks)

    return kernel_call(
        "grads_out",
        body,
        [((tokens, inner), BF), ((tokens, 2 * NS), BF), ((rows, width), F32)]
        + [((rows, width), BF)] * (wa_count - 1),
        [me, dgate, dmix, tail, next_edge, ddt, dq, dkv, wzx, wbc, wdt, wq, kvw],
        scratch=[pltpu.VMEM((tokens, width), F32)],
        flops=2 * tokens * width * (mix + 768),
        ties=ties,
    )


def all_rows(me, parts):
    n = len(parts)
    rows, width = parts[0].shape

    def body(*refs):
        for d in range(n):
            at = pl.multiple_of(lax.rem(refs[0][0] + n - d, n) * rows, rows)
            refs[-1][pl.ds(at, rows), :] = refs[1 + d][...].astype(F32)

    return kernel_call("all_rows", body, [((n * rows, width), F32)], [me, *parts])[0]


def held_back(arrays, ties):
    count = len(arrays)

    def body(*refs):
        pass

    return pl.pallas_call(
        body,
        in_specs=[pl.BlockSpec(memory_space=pl.ANY)] * (count + len(ties)),
        out_specs=[pl.BlockSpec(memory_space=pl.ANY)] * count,
        out_shape=[jax.ShapeDtypeStruct(a.shape, a.dtype) for a in arrays],
        input_output_aliases={i: i for i in range(count)},
        name="held_back",
    )(*arrays, *ties)


def pack_small(gains, convs, heads, inner, ties):
    width = gains[0].shape[1]
    mix = convs[0].shape[1]
    pieces = [(g, 0, 0, width) for g in range(len(gains))]
    at = len(gains)
    pieces += [(at + k, j, inner, mix) for k in range(len(convs)) for j in range(KC + 1)]
    pieces += [(at + k, j, 0, inner) for k in range(len(convs)) for j in range(KC + 1)]
    at += len(convs)
    pieces += [(at + k, j, 0, 128) for k in range(len(heads)) for j in range(8)]
    total = sum((end - start) // 128 for _, _, start, end in pieces)

    def body(*refs):
        row = 0
        for source, line, start, end in pieces:
            for c in range(start, end, 128):
                refs[-1][row : row + 1, :] = refs[source][line : line + 1, c : c + 128]
                row += 1

    return kernel_call(
        "pack_small", body, [((total, 128), F32)], [*gains, *convs, *heads], ties=ties
    )[0]


def per_device(
    x_in,
    d_out,
    segment_ids,
    norm_gains,
    w_zx,
    w_bc,
    w_dt,
    conv_x,
    conv_bc,
    dt_bias,
    a_log,
    d_skip,
    w_out,
    w_q,
    key_value_weight,
    w_ao,
    w_gu,
    w_down,
):
    seq_count = lax.axis_size("seq")
    wa_count = lax.axis_size("wa")
    tokens, width = x_in.shape
    rows = tokens // wa_count
    seq_here = lax.axis_index("seq")
    wa_here = lax.axis_index("wa")
    start_row = seq_here * tokens
    inner = w_zx.shape[3]
    heads = w_dt.shape[2]
    hidden = w_gu.shape[3]
    query_local = w_q.shape[2] // HEAD_SIZE
    group = QUERY_HEADS // KEY_VALUE_HEADS
    kv_head = wa_here * query_local // group
    me = wa_here.astype(jnp.int32).reshape(1)
    here = seq_here.astype(jnp.int32).reshape(1)

    seg_blocks = segment_ids.reshape(seq_count, tokens)
    seg_here = lax.dynamic_slice_in_dim(segment_ids, start_row, tokens)
    seg_padded = jnp.concatenate([jnp.full((KC - 1,), -1, jnp.int32), segment_ids])
    seg_edge = lax.dynamic_slice_in_dim(seg_padded, start_row, KC - 1)
    seg_full = jnp.concatenate([seg_edge, seg_here])
    steps = jnp.arange(seq_count, dtype=jnp.int32)
    segrel = jnp.where(
        (steps <= seq_here)[:, None], seg_blocks[(seq_here - steps) % seq_count], -1
    )
    seglater = jnp.where(
        (steps + seq_here < seq_count)[:, None], seg_blocks[(seq_here + steps) % seq_count], -1
    )
    blocks_used = jnp.stack(
        [
            1 + jnp.sum((segrel[1:, tokens - 1] == seg_here[0]).astype(jnp.int32)),
            1 + jnp.sum((seglater[1:, 0] == seg_here[tokens - 1]).astype(jnp.int32)),
        ]
    ).astype(jnp.int32)
    segrel = segrel[:, None, :]
    seglater = seglater[:, None, :]
    segc = seg_here[:, None]
    lane = iota((tokens, 128), 1)
    tok = jnp.zeros((tokens, 128), F32)
    conditions = [seg_full[j : j + tokens] == seg_here for j in range(KC)]
    conditions.append(seg_here == seg_edge[KC - 2])
    conditions.append(seg_here == seg_here[tokens - 1])
    for k, condition in enumerate(conditions):
        tok = jnp.where((lane == k) & condition[:, None], 1.0, tok)
    half = HEAD_SIZE // 2
    frequency = jnp.exp((lane % half).astype(F32) * (-math.log(theta) / half))
    angles = (start_row + iota((tokens, 128), 0)).astype(F32) * frequency
    cos_q = jnp.cos(angles)
    sin_q = jnp.where(lane % HEAD_SIZE < half, -1.0, 1.0) * jnp.sin(angles)
    cos_kv = jnp.where(lane < HEAD_SIZE, cos_q, 1.0)
    sin_kv = jnp.where(lane < HEAD_SIZE, sin_q, 0.0)

    wzx_all = w_zx.reshape(LAYER_COUNT, width, 2 * inner)
    wgu_all = w_gu.reshape(LAYER_COUNT, width, 2 * hidden)
    wdt_all = jnp.pad(w_dt, ((0, 0), (0, 0), (0, 128 - heads)))
    kvw_all = lax.dynamic_slice_in_dim(
        key_value_weight, kv_head * HEAD_SIZE, HEAD_SIZE, axis=3
    ).reshape(LAYER_COUNT, width, 2 * HEAD_SIZE)
    conv_all = jnp.pad(
        jnp.concatenate([conv_x, conv_bc], axis=2), ((0, 0), (0, 8 - (KC + 1)), (0, 0))
    )
    hp_all = jnp.pad(
        jnp.stack([dt_bias, a_log, d_skip], axis=1), ((0, 0), (0, 5), (0, 128 - heads))
    )

    def own_rows(array):
        return lax.dynamic_slice_in_dim(array, wa_here * rows, rows)

    h = own_rows(x_in)
    normed = norm_first(h, norm_gains[0, 0][None, :])
    saved = []
    for layer in range(LAYER_COUNT):
        wzx, wbc, wdt, wq = [(a, layer) for a in (wzx_all, w_bc, wdt_all, w_q)]
        kvw, conv_w, hp = [(a, layer) for a in (kvw_all, conv_all, hp_all)]
        wout, wao, wgu, wdown = [(a, layer) for a in (w_out, w_ao, wgu_all, w_down)]
        normed_parts = gather_wa(normed)
        edge = jnp.zeros((16, width), BF)
        for d, part in enumerate(normed_parts):
            edge = jnp.where((wa_here + wa_count - d) % wa_count == wa_count - 1, part[rows - 16 :], edge)
        edge = lax.ppermute(edge, "seq", [(i, i + 1) for i in range(seq_count - 1)])
        nat, gate, u, r_raw, kv, q_own = project(
            me, normed_parts, wzx, wbc, wdt, wq, kvw, cos_q, sin_q, cos_kv, sin_kv
        )
        every = gather_seq(kv)
        pad, act, hd, pack = mixer_front(
            edge, u, r_raw, wzx, wbc, conv_w, hp, tok
        )
        states = gather_seq(pack)
        y_local = mixer_within(act, hd, segc, segrel, hp, inner)
        o2, flat = attend(here, every, q_own, segc, segrel, blocks_used)
        state_in, y, gated, *parts = mixer_out(
            me, here, states, y_local, act, hd, tok, gate, flat, wout, wao, wa_count
        )
        mixed, normed_two = norm_step(scatter_wa(parts), h, norm_gains[layer, 1][None, :])
        n2, gu, act_ff, *parts = feed_forward(gather_wa(normed_two), wgu, wdown)
        saved.append(
            (h, nat, every, q_own, gate, pad, act, hd, o2, flat, state_in, y, gated,
             mixed, n2, gu, act_ff)
        )
        if layer + 1 < LAYER_COUNT:
            h, normed = norm_step(scatter_wa(parts), mixed, norm_gains[layer + 1, 0][None, :])

    last_parts = parts
    last_mixed = mixed

    grad = own_rows(d_out)
    grad_parts = [
        lax.dynamic_slice_in_dim(d_out, (wa_here + wa_count - d) % wa_count * rows, rows).astype(BF)
        for d in range(wa_count)
    ]
    sums = [None] * LAYER_COUNT
    small = [None] * LAYER_COUNT
    for layer in reversed(range(LAYER_COUNT)):
        wzx, wbc, wdt, wq = [(a, layer) for a in (wzx_all, w_bc, wdt_all, w_q)]
        kvw, conv_w, hp = [(a, layer) for a in (kvw_all, conv_all, hp_all)]
        wout, wao, wgu, wdown = [(a, layer) for a in (w_out, w_ao, wgu_all, w_down)]
        (h_in, nat, every, q_own, gate, pad, act, hd, o2, flat, state_in, y, gated,
         mixed, n2, gu, act_ff) = saved[layer]
        gb, dgu, *parts = feed_back(grad_parts, gu, wgu, wdown)
        parts = scatter_wa(parts)
        ff_pairs = [(gb, act_ff), (n2, dgu)]
        grad_ties = []
        if not layer:
            early = weight_grads(here, [(ff_pairs, False)], seq_count)[0]
            grad_ties = list(early)
        d_mixed, mixed_b, gain_two = norm_back(
            parts, mixed, norm_gains[layer, 1][None, :], grad, grad_ties
        )
        mixed_parts = gather_wa(mixed_b)
        mb, dy, dgate, pack, da, delta = mixer_grad_in(
            me, mixed_parts, wout, wao, gate, y, act, hd, tok, o2, q_own
        )
        states_back = gather_seq(pack)
        every_back = gather_seq(da)
        mix_pairs = [(mb, gated), (mb, flat), (nat, dgate)]
        if layer == LAYER_COUNT - 1:
            out_parts = scatter_wa(held_back(last_parts, [delta]))
            out_ties = out_parts[1:]
        if not layer:
            early = held_back(list(early), [joint, every_back])
            out_ties = list(early)
            sum_ff = scatter_rows(early)
        dq, dkv = attend_back(
            here, every, states_back, every_back, delta, o2, q_own, segc, segrel, seglater,
            blocks_used, cos_q, sin_q, cos_kv, sin_kv, inner, out_ties,
        )
        dmix, tail, edge_grad, ddt, gconv, ghead = mixer_grad(
            here, states_back, state_in, dy, pad, hd, tok, segc, segrel, hp, conv_w
        )
        next_edge = lax.ppermute(
            edge_grad, "seq", [(i + 1, i) for i in range(seq_count - 1)]
        )
        dx, dbc, *parts = grads_out(
            me, dgate, dmix, tail, next_edge, ddt, dq, dkv, wzx, wbc, wdt, wq, kvw, wa_count, []
        )
        parts = scatter_wa(parts)
        every_pairs = [(nat, dbc), (nat, dkv)]
        in_pairs = [(nat, dx), (nat, dq), (nat, ddt)]
        if layer:
            joint = weight_grads(
                here, [(ff_pairs + mix_pairs + every_pairs + in_pairs, False)], seq_count
            )[0]
            back_ties = list(joint)
            joint = scatter_rows(joint)
            cuts = [3 * hidden, 2 * inner + 128, 2 * NS + 128, inner + 256]
            ends = [sum(cuts[: k + 1]) for k in range(4)]
            sum_ff, sum_mix, sum_every, sum_in = [
                joint[:, end - size : end] for end, size in zip(ends, cuts)
            ]
            h = norm_step(out_parts, last_mixed, norm_gains[layer, 0][None, :], [parts[1]])[0]
        else:
            joint = weight_grads(
                here, [(every_pairs + mix_pairs + in_pairs, False)], seq_count
            )[0]
            back_ties = list(joint)
            joint = scatter_rows(joint)
            cuts = [2 * NS + 128, 2 * inner + 128, inner + 256]
            ends = [sum(cuts[: k + 1]) for k in range(3)]
            sum_every, sum_mix, sum_in = [
                joint[:, end - size : end] for end, size in zip(ends, cuts)
            ]
        grad, grad_b, gain_one = norm_back(
            parts, h_in, norm_gains[layer, 0][None, :], d_mixed, back_ties
        )
        grad_parts = gather_wa(grad_b)
        sums[layer] = (sum_ff, sum_mix, sum_in, sum_every)
        small[layer] = (gain_one, gain_two, gconv, ghead)
    x_parts = gather_wa(held_back([h.astype(BF)], [grad_parts[-1]])[0])
    shared_late = gather_wa(held_back([sums[1][3]], [x_parts[-1]])[0])
    x_out = all_rows(me, x_parts)
    d_x = all_rows(me, grad_parts)

    mix = inner + 2 * NS
    local = pack_small(
        [small[layer][k] for layer in range(LAYER_COUNT) for k in (0, 1)],
        [small[layer][2] for layer in range(LAYER_COUNT)],
        [small[layer][3] for layer in range(LAYER_COUNT)],
        inner,
        [grad_parts[-1]],
    )
    local = jnp.sum(gather_seq(local), axis=0)
    gain_rows = 2 * LAYER_COUNT * width // 128
    shared_rows = gain_rows + LAYER_COUNT * (KC + 1) * 2 * NS // 128
    shared = sum(gather_wa(local[:shared_rows]))
    gain_sum = shared[:gain_rows].reshape(LAYER_COUNT, 2, width)
    g_conv_bc = shared[gain_rows:].reshape(LAYER_COUNT, KC + 1, 2 * NS)
    local = local[shared_rows:]
    conv_rows = LAYER_COUNT * (KC + 1) * (inner // 128)
    g_conv_x = local[:conv_rows].reshape(LAYER_COUNT, KC + 1, inner)
    head_part = local[conv_rows:].reshape(LAYER_COUNT, 8, 128)

    every_parts = [
        jnp.stack(pair) for pair in zip(gather_wa(sums[0][3]), shared_late)
    ]
    g_bc = sum(part[:, :, : 2 * NS].astype(F32) for part in every_parts)
    kv_columns = []
    for head in range(KEY_VALUE_HEADS):
        total = 0.0
        for d, part in enumerate(every_parts):
            source = (wa_here + wa_count - d) % wa_count * query_local // group
            total = total + jnp.where(source == head, part[:, :, 2 * NS :].astype(F32), 0.0)
        kv_columns.append(total.reshape(total.shape[0], total.shape[1], 2, HEAD_SIZE))
    g_kv = jnp.concatenate(kv_columns, axis=3)

    block = sums[0][0].shape[0]

    def stacked(pick):
        return jnp.stack([pick(s).astype(F32) for s in sums])

    g_down = stacked(lambda s: s[0][:, :hidden].T)
    g_gu = stacked(lambda s: s[0][:, hidden:].reshape(block, 2, hidden))
    ends = inner + 128
    g_out = stacked(lambda s: s[1][:, :inner].T)
    g_ao = stacked(lambda s: s[1][:, inner:ends].T)
    g_zx = stacked(
        lambda s: jnp.stack(
            [s[1][:, ends : ends + inner].astype(F32), s[2][:, :inner].astype(F32)], axis=1
        )
    )
    g_q = stacked(lambda s: s[2][:, inner:ends])
    g_dt = stacked(lambda s: s[2][:, ends : ends + heads])
    return (
        x_out,
        d_x,
        gain_sum[:, 0],
        gain_sum[:, 1],
        g_zx,
        g_bc,
        g_dt,
        g_conv_x,
        g_conv_bc,
        head_part[:, 0, :heads],
        head_part[:, 1, :heads],
        head_part[:, 2, :heads],
        g_out,
        g_q,
        g_kv,
        g_ao,
        g_gu,
        g_down,
    )


def solution(mesh):
    return jax.shard_map(
        per_device,
        mesh=mesh,
        in_specs=(
            P("seq", None),
            P("seq", None),
            P(),
            P(),
            P(None, None, None, "wa"),
            P(),
            P(None, None, "wa"),
            P(None, None, "wa"),
            P(),
            P(None, "wa"),
            P(None, "wa"),
            P(None, "wa"),
            P(None, "wa", None),
            P(None, None, "wa"),
            P(),
            P(None, "wa", None),
            P(None, None, None, "wa"),
            P(None, "wa", None),
        ),
        out_specs=(
            P("seq", None),
            P("seq", None),
            P(),
            P(),
            P(None, "seq", None, "wa"),
            P(None, "seq", None),
            P(None, "seq", "wa"),
            P(None, None, "wa"),
            P(),
            P(None, "wa"),
            P(None, "wa"),
            P(None, "wa"),
            P(None, "wa", "seq"),
            P(None, "seq", "wa"),
            P(None, "seq", None, None),
            P(None, "wa", "seq"),
            P(None, "seq", None, "wa"),
            P(None, "wa", "seq"),
        ),
        check_vma=False,
    )
```

```python
import math

import jax
import jax.numpy as jnp
from jax import lax
from jax.experimental import pallas as pl
from jax.experimental.pallas import tpu as pltpu
from jax.sharding import PartitionSpec as P

MODEL_WIDTH = 1024
HEAD_SIZE = 64
NS = 128
KC = 4
QUERY_HEADS = 8
KEY_VALUE_HEADS = 2
LAYER_COUNT = 2
DIRECT_MOST = 8
VMEM_MIB = 48

eps = 1e-05
theta = 10000.0
neg_big = -1e30
score_scale = 1.0 / math.sqrt(HEAD_SIZE)

BF = jnp.bfloat16
F32 = jnp.float32
HI = lax.Precision.HIGHEST


def mm(a, b):
    return lax.dot_general(
        a.astype(BF), b.astype(BF), (((1,), (0,)), ((), ())), preferred_element_type=F32
    )


def mm_nt(a, b):
    return lax.dot_general(
        a.astype(BF), b.astype(BF), (((1,), (1,)), ((), ())), preferred_element_type=F32
    )


def mm_tn(a, b):
    return lax.dot_general(
        a.astype(BF), b.astype(BF), (((0,), (0,)), ((), ())), preferred_element_type=F32
    )


def mm_hi(a, b):
    return jnp.dot(a, b, precision=HI, preferred_element_type=F32)


def iota(shape, dim):
    return lax.broadcasted_iota(jnp.int32, shape, dim)


def sigmoid(v):
    return 1.0 / (1.0 + jnp.exp(-v))


def gather_seq(block):
    return lax.all_gather(block, "seq")


def scatter_rows(blocks):
    n = lax.axis_size("seq")
    if len(blocks) > 1:
        got = [
            lax.ppermute(blocks[d], "seq", [(i, (i + d) % n) for i in range(n)])
            for d in range(1, n)
        ]
        total = blocks[0].astype(F32)
        for part in got:
            total = total + part.astype(F32)
        return total
    return lax.psum_scatter(blocks[0], "seq", scatter_dimension=0, tiled=True)


def gather_wa(block):
    n = lax.axis_size("wa")
    return [block] + [
        lax.ppermute(block, "wa", [(i, (i + d) % n) for i in range(n)]) for d in range(1, n)
    ]


def scatter_wa(blocks):
    n = lax.axis_size("wa")
    return [blocks[0]] + [
        lax.ppermute(blocks[n - d], "wa", [(i, (i + d) % n) for i in range(n)])
        for d in range(1, n)
    ]


def arrive(*refs):
    pass


def kernel_call(name, body, outs, args, scratch=(), flops=0, ties=()):
    in_specs, arrays = [], []
    bytes_accessed = sum(math.prod(s) * jnp.dtype(k).itemsize for s, k in outs)
    for item in args:
        array, layer = item if isinstance(item, tuple) else (item, None)
        arrays.append(array)
        if layer is not None:
            rest = array.ndim - 1
            spec = pl.BlockSpec(
                (None,) + array.shape[1:], lambda i, layer=layer, rest=rest: (layer,) + (0,) * rest
            )
        elif array.ndim == 1:
            spec = pl.BlockSpec(memory_space=pltpu.SMEM)
        else:
            spec = pl.BlockSpec(array.shape, lambda i, rest=array.ndim: (0,) * rest)
        in_specs.append(spec)
        bytes_accessed += array.size * array.dtype.itemsize // (1 if layer is None else array.shape[0])
    count, gap = len(arrays), len(arrays) + len(ties)
    in_specs += [pl.BlockSpec(memory_space=pl.ANY)] * len(ties)

    def whole(*refs):
        body(*refs[:count], *refs[gap:])

    return pl.pallas_call(
        whole,
        grid=(1,),
        in_specs=in_specs,
        out_specs=[
            pl.BlockSpec(shape, lambda i, rest=len(shape): (0,) * rest) for shape, kind in outs
        ],
        out_shape=[jax.ShapeDtypeStruct(shape, kind) for shape, kind in outs],
        scratch_shapes=list(scratch),
        compiler_params=pltpu.CompilerParams(vmem_limit_bytes=VMEM_MIB * 1024 * 1024),
        cost_estimate=pl.CostEstimate(
            flops=flops, bytes_accessed=bytes_accessed, transcendentals=0
        ),
        name=name,
    )(*arrays, *ties)


def ordered(me_ref, parts, nat_ref):
    n = len(parts)
    rows = parts[0].shape[0]
    for d in range(n):
        at = pl.multiple_of(lax.rem(me_ref[0] + n - d, n) * rows, rows)
        nat_ref[pl.ds(at, rows), :] = parts[d][...]


def rotated(me_ref, nat_ref, blocks):
    n = len(blocks)
    rows = blocks[0].shape[0]
    for d in range(n):
        at = pl.multiple_of(lax.rem(me_ref[0] + n - d, n) * rows, rows)
        blocks[d][...] = nat_ref[pl.ds(at, rows), :].astype(blocks[d].dtype)


def halves_swapped(v):
    width = v.shape[1]
    half = HEAD_SIZE // 2
    first = iota(v.shape, 1) % HEAD_SIZE < half
    return jnp.where(first, pltpu.roll(v, width - half, 1), pltpu.roll(v, half, 1))


def expand(v, width):
    k = v.shape[1]
    pick = (iota((k, width), 1) // HEAD_SIZE == iota((k, width), 0)).astype(F32)
    return mm_hi(v, pick)


def head_sum(v):
    width = v.shape[1]
    pick = (iota((width, 128), 0) // HEAD_SIZE == iota((width, 128), 1)).astype(F32)
    return mm_hi(v, pick)


def decay_rows(block_decay):
    high = block_decay.astype(BF).astype(F32)
    low = block_decay - high
    row = iota((16, 128), 0)
    return jnp.where(row == 0, high, jnp.where(row == 1, low, 0.0)).astype(BF)


def fold_states(packs_ref, inner, here, later):
    arrive(packs_ref)
    heads = inner // HEAD_SIZE
    n = packs_ref.shape[0]

    def step(k, state):
        j = n - 1 - k if later else k
        tail = packs_ref[j, inner : inner + 16, :].astype(F32)
        decay = tail[0:1, :] + tail[1:2, :]
        full = jnp.concatenate(
            [jnp.broadcast_to(decay[:, h : h + 1], (HEAD_SIZE, NS)) for h in range(heads)], axis=0
        )
        return state * full + packs_ref[j, :inner, :].astype(F32)

    count = n - 1 - here if later else here
    return lax.fori_loop(0, count, step, jnp.zeros((inner, NS), F32))


def norm_first(hidden, gain):
    rows, width = hidden.shape

    def body(h_ref, g_ref, n_ref):
        h = h_ref[...]
        scale = lax.rsqrt(jnp.mean(h * h, axis=-1, keepdims=True) + eps)
        n_ref[...] = (h * scale * g_ref[...]).astype(BF)

    return kernel_call("norm_first", body, [((rows, width), BF)], [hidden, gain])[0]


def norm_step(parts, hidden, gain, ties=()):
    rows, width = hidden.shape
    n = len(parts)

    def body(*refs):
        h_ref, g_ref, out_ref, n_ref = refs[n:]
        total = refs[0][...]
        for part in refs[1:n]:
            total = total + part[...].astype(F32)
        h = h_ref[...] + total
        out_ref[...] = h
        scale = lax.rsqrt(jnp.mean(h * h, axis=-1, keepdims=True) + eps)
        n_ref[...] = (h * scale * g_ref[...]).astype(BF)

    return kernel_call(
        "norm_step",
        body,
        [((rows, width), F32), ((rows, width), BF)],
        [*parts, hidden, gain],
        ties=ties,
    )


def norm_back(parts, hidden, gain, grad, ties):
    rows, width = hidden.shape
    n = len(parts)

    def body(*refs):
        h_ref, g_ref, grad_ref, out_ref, b_ref, gain_ref = refs[n:]
        total = refs[0][...]
        for part in refs[1:n]:
            total = total + part[...].astype(F32)
        h = h_ref[...]
        scale = lax.rsqrt(jnp.mean(h * h, axis=-1, keepdims=True) + eps)
        unit = h * scale
        through = total * g_ref[...]
        out = grad_ref[...] + scale * (
            through - unit * jnp.mean(through * unit, axis=-1, keepdims=True)
        )
        out_ref[...] = out
        b_ref[...] = out.astype(BF)
        gain_ref[...] = jnp.sum(total * unit, axis=0, keepdims=True)

    return kernel_call(
        "norm_back",
        body,
        [((rows, width), F32), ((rows, width), BF), ((1, width), F32)],
        [*parts, hidden, gain, grad],
        ties=ties,
    )


def project(me, parts, wzx, wbc, wdt, wq, kvw, cos_q, sin_q, cos_kv, sin_kv):
    n = len(parts)
    rows, width = parts[0].shape
    tokens = n * rows
    inner = wzx[0].shape[2] // 2
    mix = inner + 2 * NS

    def body(*refs):
        me_ref = refs[0]
        (
            kvw_ref, wq_ref, wdt_ref, wbc_ref, wzx_ref, cq_ref, sq_ref, ck_ref, sk_ref,
            nat_ref, gate_ref, u_ref, r_ref, kv_ref, q_ref,
        ) = refs[1 + n :]
        ordered(me_ref, refs[1 : 1 + n], nat_ref)
        x = nat_ref[...]
        kv = mm(x, kvw_ref[...])
        kv_ref[...] = (kv * ck_ref[...] + halves_swapped(kv) * sk_ref[...]).astype(BF)
        q = mm(x, wq_ref[...])
        q_ref[...] = (q * cq_ref[...] + halves_swapped(q) * sq_ref[...]).astype(BF)
        r_ref[...] = mm(x, wdt_ref[...])
        u_ref[:, inner:] = mm(x, wbc_ref[...])
        gate_ref[...] = mm(x, wzx_ref[:, :inner]).astype(BF)
        u_ref[:, :inner] = mm(x, wzx_ref[:, inner:])

    return kernel_call(
        "project",
        body,
        [
            ((tokens, width), BF),
            ((tokens, inner), BF),
            ((tokens, mix), F32),
            ((tokens, 128), F32),
            ((tokens, 128), BF),
            ((tokens, 128), BF),
        ],
        [me, *parts, kvw, wq, wdt, wbc, wzx, cos_q, sin_q, cos_kv, sin_kv],
        flops=2 * tokens * width * 1408,
    )


def convolved(pad_ref, cw_ref, tk, tokens):
    mix = pad_ref.shape[1]
    conv = jnp.broadcast_to(cw_ref[KC : KC + 1, :], (tokens, mix))
    for j in range(KC):
        at = 16 - (KC - 1) + j
        conv = conv + cw_ref[j : j + 1, :] * pad_ref[at : at + tokens, :] * tk[:, j : j + 1]
    return conv


def mixer_front(edge, u, r_raw, wzx, wbc, conv_w, hp, tok):
    tokens, mix = u.shape
    inner = mix - 2 * NS

    def body(
        edge_ref, u_ref, r_ref, wzx_ref, wbc_ref, cw_ref, hp_ref, tok_ref,
        pad_ref, act_ref, hd_ref, pack_ref,
    ):
        e = edge_ref[...]
        pad_ref[:16, :inner] = mm(e, wzx_ref[:, inner:])
        pad_ref[:16, inner:] = mm(e, wbc_ref[...])
        pad_ref[16:, :] = u_ref[...]
        tk = tok_ref[...]
        conv = convolved(pad_ref, cw_ref, tk, tokens)
        act = conv * sigmoid(conv)
        act_ref[...] = act.astype(BF)
        r = r_ref[...] + hp_ref[0:1, :]
        dt = jnp.maximum(r, 0.0) + jnp.log1p(jnp.exp(-jnp.abs(r)))
        log_decay = -dt * jnp.exp(hp_ref[1:2, :])
        lower = (iota((tokens, tokens), 0) >= iota((tokens, tokens), 1)).astype(F32)
        cum = mm_hi(lower, log_decay)
        hd_ref[0] = r
        hd_ref[1] = dt
        hd_ref[2] = cum
        last = cum[tokens - 1 :, :]
        to_last = jnp.where(tk[:, 5:6] > 0.5, jnp.exp(last - cum), 0.0)
        scaled = act[:, :inner] * expand(dt * to_last, inner)
        pack_ref[:inner, :] = mm_tn(scaled, act[:, inner : inner + NS]).astype(BF)
        pack_ref[inner:, :] = decay_rows(jnp.exp(last) * tk[tokens - 1 :, 4:5])

    return kernel_call(
        "mixer_front",
        body,
        [
            ((tokens + 16, mix), F32),
            ((tokens, mix), BF),
            ((3, tokens, 128), F32),
            ((inner + 16, NS), BF),
        ],
        [edge, u, r_raw, wzx, wbc, conv_w, hp, tok],
        flops=2 * tokens * tokens * 512,
    )


def query_rows(q):
    lane = iota(q.shape, 1)
    wide = q.astype(F32)
    return jnp.concatenate(
        [
            jnp.where(lane < HEAD_SIZE, wide, 0.0),
            jnp.where(lane < HEAD_SIZE, pltpu.roll(wide, HEAD_SIZE, 1), 0.0),
        ],
        axis=0,
    ).astype(BF)


def value_rows(v):
    lane = iota(v.shape, 1)
    wide = v.astype(F32)
    return jnp.concatenate(
        [
            jnp.where(lane >= HEAD_SIZE, pltpu.roll(wide, HEAD_SIZE, 1), 0.0),
            jnp.where(lane >= HEAD_SIZE, wide, 0.0),
        ],
        axis=0,
    )


def allowed_pair(segc, segr, tokens, steps_back):
    heads = segc.shape[0] // tokens
    row = iota((heads * tokens, tokens), 0) % tokens
    column = iota((heads * tokens, tokens), 1)
    return (segc == segr) & (column - tokens * steps_back <= row)


def within_decay(cum, cum_t, h, allowed):
    return jnp.exp(jnp.where(allowed, cum[:, h : h + 1] - cum_t[h : h + 1, :], neg_big))


def mixer_within(act, hd, segc, segrel, hp, inner):
    tokens = act.shape[0]

    def body(act_ref, hd_ref, segc_ref, segr_ref, hp_ref, y_ref):
        lane = iota((tokens, 128), 1)
        act_all = act_ref[...].astype(F32)
        b_mat = act_all[:, inner : inner + NS]
        c_mat = act_all[:, inner + NS :]
        both = mm_nt(c_mat, b_mat)
        dt, cum = hd_ref[1], hd_ref[2]
        cum_t = cum.T
        allowed = allowed_pair(segc_ref[...], segr_ref[0], tokens, 0)
        scaled = act_all[:, :inner] * expand(dt, inner)
        skip = expand(hp_ref[...], inner)[2:3, :]
        for p in range(inner // 128):
            cols = slice(128 * p, 128 * (p + 1))
            pair = [
                mm(within_decay(cum, cum_t, 2 * p + k, allowed) * both, scaled[:, cols])
                for k in range(2)
            ]
            y_ref[:, cols] = (
                jnp.where(lane < HEAD_SIZE, pair[0], pair[1])
                + skip[:, cols] * act_all[:, cols]
            )

    return kernel_call(
        "mixer_within",
        body,
        [((tokens, inner), F32)],
        [act, hd, segc, segrel, hp],
        flops=2 * tokens * tokens * 128 * 8,
    )[0]


def attend(here, every, q_own, segc, segrel, blocks):
    n = every.shape[0]
    tokens = segc.shape[0]
    rows = 2 * tokens

    def body(*refs):
        here_ref, all_ref, q_ref, segc_ref, segr_ref, nb_ref, o2_ref, flat_ref = refs
        arrive(all_ref, segr_ref)
        here_at = here_ref[0]
        q = query_rows(q_ref[...])
        seg_own = segc_ref[...]
        seg_two = jnp.concatenate([seg_own] * (rows // tokens), axis=0)

        def step(d, carry):
            top, total, out = carry
            kv = all_ref[here_at - d]
            allowed = allowed_pair(seg_two, segr_ref[d], tokens, d)
            scores = jnp.where(allowed, mm_nt(q, kv) * score_scale, neg_big)
            new_top = jnp.maximum(top, jnp.max(scores, axis=1, keepdims=True))
            weights = jnp.where(allowed, jnp.exp(scores - new_top), 0.0)
            shrink = jnp.exp(top - new_top)
            return (
                new_top,
                total * shrink + jnp.sum(weights, axis=1, keepdims=True),
                out * shrink + mm(weights, kv),
            )

        top, total, out = lax.fori_loop(
            0,
            nb_ref[0],
            step,
            (
                jnp.full((rows, 1), neg_big, F32),
                jnp.zeros((rows, 1), F32),
                jnp.zeros((rows, 128), F32),
            ),
        )
        out = out / total
        o2_ref[...] = jnp.where(iota((rows, 128), 1) == 0, top + jnp.log(total), out)
        lane = iota((tokens, 128), 1)
        flat_ref[...] = jnp.where(
            lane < HEAD_SIZE, pltpu.roll(out[:tokens], HEAD_SIZE, 1), out[tokens:]
        ).astype(BF)

    return kernel_call(
        "attend",
        body,
        [
            ((rows, 128), F32),
            ((tokens, 128), BF),
        ],
        [here, every, q_own, segc, segrel, blocks],
        flops=2 * rows * tokens * 128 * 2 * n,
    )


def mixer_out(me, here, states, y_local, act, hd, tok, gate, flat, wout, wao, wa_count):
    tokens, inner = y_local.shape
    width = wout[0].shape[2]
    rows = tokens // wa_count

    def body(*refs):
        me_ref, here_ref, all_ref = refs[:3]
        y_ref, act_ref, hd_ref, tok_ref, gate_ref, flat_ref, wout_ref, wao_ref = refs[3:11]
        state_ref, yy_ref, gated_ref = refs[11:14]
        blocks = refs[14 : 14 + wa_count]
        full_ref = refs[-1]
        state = fold_states(all_ref, inner, here_ref[0], False)
        state_ref[...] = state
        decay_in = jnp.exp(hd_ref[2]) * tok_ref[:, 4:5]
        y = y_ref[...] + mm_nt(act_ref[:, inner + NS :], state) * expand(decay_in, inner)
        yy_ref[...] = y.astype(BF)
        gate_raw = gate_ref[...].astype(F32)
        gated = (y * gate_raw * sigmoid(gate_raw)).astype(BF)
        gated_ref[...] = gated
        full_ref[...] = mm(gated, wout_ref[...]) + mm(flat_ref[...], wao_ref[...])
        rotated(me_ref, full_ref, blocks)

    return kernel_call(
        "mixer_out",
        body,
        [((inner, NS), F32), ((tokens, inner), BF), ((tokens, inner), BF)]
        + [((rows, width), F32)]
        + [((rows, width), BF)] * (wa_count - 1),
        [me, here, states, y_local, act, hd, tok, gate, flat, wout, wao],
        scratch=[pltpu.VMEM((tokens, width), F32)],
        flops=2 * tokens * width * 512,
    )


def feed_forward(parts, wgu, wdown):
    n = len(parts)
    rows, width = parts[0].shape
    tokens = n * rows
    hidden = wdown[0].shape[1]

    def body(*refs):
        wgu_ref, wdown_ref, n_ref, gu_ref, act_ref = refs[n : n + 5]
        blocks = refs[n + 5 : n + 5 + n]
        for d in range(n):
            n_ref[d * rows : (d + 1) * rows, :] = refs[d][...]
        x = n_ref[...]
        gate = mm(x, wgu_ref[:, :hidden])
        up = mm(x, wgu_ref[:, hidden:])
        gu_ref[:, :hidden] = gate.astype(BF)
        gu_ref[:, hidden:] = up.astype(BF)
        act = (gate * sigmoid(gate) * up).astype(BF)
        act_ref[...] = act
        for d in range(n):
            blocks[d][...] = mm(act[d * rows : (d + 1) * rows], wdown_ref[...]).astype(
                blocks[d].dtype
            )

    return kernel_call(
        "feed_forward",
        body,
        [((tokens, width), BF), ((tokens, 2 * hidden), BF), ((tokens, hidden), BF)]
        + [((rows, width), F32)]
        + [((rows, width), BF)] * (n - 1),
        [*parts, wgu, wdown],
        flops=2 * tokens * width * 3 * hidden,
    )


def feed_back(parts, gu, wgu, wdown):
    n = len(parts)
    rows, width = parts[0].shape
    tokens = n * rows
    hidden = wdown[0].shape[1]

    def body(*refs):
        gu_ref, wgu_ref, wdown_ref, gb_ref, dgu_ref = refs[n : n + 5]
        blocks = refs[n + 5 : n + 5 + n]
        for d in range(n):
            gb_ref[d * rows : (d + 1) * rows, :] = refs[d][...]
        d_act = mm_nt(gb_ref[...], wdown_ref[...])
        gate = gu_ref[:, :hidden].astype(F32)
        up = gu_ref[:, hidden:].astype(F32)
        sg = sigmoid(gate)
        dgu_ref[:, :hidden] = (d_act * up * sg * (1.0 + gate * (1.0 - sg))).astype(BF)
        dgu_ref[:, hidden:] = (d_act * gate * sg).astype(BF)
        for d in range(n):
            blocks[d][...] = mm_nt(dgu_ref[d * rows : (d + 1) * rows, :], wgu_ref[...]).astype(
                blocks[d].dtype
            )

    return kernel_call(
        "feed_back",
        body,
        [((tokens, width), BF), ((tokens, 2 * hidden), BF)]
        + [((rows, width), F32)]
        + [((rows, width), BF)] * (n - 1),
        [*parts, gu, wgu, wdown],
        flops=2 * tokens * width * 3 * hidden,
    )


def weight_grads(here, groups, n, ties=()):
    width = groups[0][0][0][0].shape[1]
    flat = [a for pairs, _ in groups for pair in pairs for a in pair]
    plan, shapes = [], [((8, 128), F32)]
    for pairs, direct in groups:
        blocks = n if direct and n <= DIRECT_MOST else 1
        columns = sum(right.shape[1] for _, right in pairs)
        plan.append((len(pairs), blocks))
        shapes += [
            ((width // blocks, columns), F32 if blocks > 1 and d == 0 else BF)
            for d in range(blocks)
        ]

    def body(*refs):
        here_ref = refs[0]
        source, out = 1, 2 + len(flat)
        refs[1 + len(flat)][...] = jnp.zeros((8, 128), F32)
        for count, blocks in plan:
            for d in range(blocks):
                rows = width // blocks
                start = 0
                for k in range(count):
                    left, right = refs[source + 2 * k], refs[source + 2 * k + 1]
                    if blocks > 1:
                        at = pl.multiple_of(lax.rem(here_ref[0] + d, n) * rows, rows)
                        piece = left[:, pl.ds(at, rows)]
                    else:
                        piece = left[...]
                    wide = right.shape[1]
                    target = refs[out + d]
                    target[:, start : start + wide] = mm_tn(piece, right[...]).astype(target.dtype)
                    start += wide
            source += 2 * count
            out += blocks

    got = kernel_call(
        "weight_grads",
        body,
        shapes,
        [here, *flat],
        flops=2 * flat[0].shape[0] * width * sum(a.shape[1] for a in flat[1::2]),
        ties=ties,
    )
    token, got = got[0], got[1:]
    out = []
    for _, blocks in plan:
        out.append(got[:blocks])
        got = got[blocks:]
    return out, token


def mixer_grad_in(me, parts, wout, wao, gate, y, act, hd, tok, o2, q_own):
    n = len(parts)
    rows, width = parts[0].shape
    tokens, inner = y.shape
    early = 96

    def body(*refs):
        me_ref = refs[0]
        wout_ref, wao_ref, gate_ref, y_ref, act_ref, hd_ref, tok_ref, o2_ref = refs[1 + n : 9 + n]
        q_ref, nat_ref, dy_ref, dgate_ref, pack_ref, da_ref, delta_ref = refs[9 + n :]
        ordered(me_ref, refs[1 : 1 + n], nat_ref)
        mb = nat_ref[...]
        d_gated = mm_nt(mb, wout_ref[...])
        gate_raw = gate_ref[...].astype(F32)
        sg = sigmoid(gate_raw)
        dy = d_gated * gate_raw * sg
        dy_ref[...] = dy.astype(BF)
        dgate_ref[...] = (
            d_gated * y_ref[...].astype(F32) * sg * (1.0 + gate_raw * (1.0 - sg))
        ).astype(BF)
        cum = hd_ref[2]
        decay_in = jnp.exp(cum) * tok_ref[:, 4:5]
        pack_ref[:inner, :] = mm_tn(
            dy * expand(decay_in, inner), act_ref[:, inner + NS :]
        ).astype(BF)
        pack_ref[inner : inner + 16, :] = decay_rows(decay_in[tokens - 1 :, :])
        pack_ref[inner + 16 :, :] = q_ref[:early, :]
        da_ref[tokens + 16 :, :] = q_ref[early:, :]
        d_attn = mm_nt(mb, wao_ref[...])
        da_ref[:tokens, :] = d_attn.astype(BF)
        delta = jnp.sum(value_rows(d_attn) * o2_ref[...], axis=1, keepdims=True)
        delta_ref[...] = jnp.broadcast_to(delta, (2 * tokens, 128))
        lane = iota((tokens, 128), 1)
        table = jnp.zeros((tokens, 128), F32)
        columns = [
            o2_ref[:tokens, 0:1], o2_ref[tokens:, 0:1], delta[:tokens], delta[tokens:]
        ]
        for k in range(4):
            table = jnp.where((lane == k) | (lane == k + 4), columns[k], table)
        table = table.T[:8]
        high = table.astype(BF).astype(F32)
        table = jnp.where(iota(table.shape, 0) < 4, high, table - high)
        da_ref[tokens : tokens + 16, :] = jnp.concatenate(
            [table[:, 128 * k : 128 * (k + 1)] for k in range(tokens // 128)], axis=0
        ).astype(BF)

    return kernel_call(
        "mixer_grad_in",
        body,
        [
            ((tokens, width), BF),
            ((tokens, inner), BF),
            ((tokens, inner), BF),
            ((inner + 16 + early, NS), BF),
            ((tokens + 16 + tokens - early, 128), BF),
            ((2 * tokens, 128), F32),
        ],
        [me, *parts, wout, wao, gate, y, act, hd, tok, o2, q_own],
        flops=2 * tokens * width * 512,
    )


def attend_back(
    here, every, states_back, every_back, delta, o2, q_own, segc, segrel, seglater, blocks,
    cos_q, sin_q, cos_kv, sin_kv, inner, ties,
):
    n = every.shape[0]
    tokens = segc.shape[0]
    rows = 2 * tokens

    def body(
        here_ref, all_ref, state_ref, back_ref, delta_ref, lse_ref, q_ref, segc_ref, segr_ref, segl_ref, nb_ref,
        cq_ref, sq_ref, ck_ref, sk_ref, dq_ref, dkv_ref,
    ):
        arrive(all_ref, state_ref, back_ref, segr_ref, segl_ref)
        here_at = here_ref[0]
        q = query_rows(q_ref[...])
        da = value_rows(back_ref[here_at, :tokens, :]).astype(BF)
        lse_col = lse_ref[:, 0:1]
        delta_col = delta_ref[:, 0:1]
        seg_own = segc_ref[...]
        seg_two = jnp.concatenate([seg_own] * 2, axis=0)

        def step(d, dq):
            kv = all_ref[here_at - d]
            allowed = allowed_pair(seg_two, segr_ref[d], tokens, d)
            scores = mm_nt(q, kv) * score_scale
            probs = jnp.exp(jnp.where(allowed, scores - lse_col, neg_big))
            d_scores = probs * (mm_nt(da, kv) - delta_col)
            return dq + mm(d_scores, kv)

        dq = lax.fori_loop(0, nb_ref[0], step, jnp.zeros((rows, 128), F32)) * score_scale
        lane = iota((tokens, 128), 1)
        flat = jnp.where(lane < HEAD_SIZE, dq[:tokens], pltpu.roll(dq[tokens:], HEAD_SIZE, 1))
        dq_ref[...] = (flat * cq_ref[...] - halves_swapped(flat) * sq_ref[...]).astype(BF)
        kv_own = all_ref[here_at]

        def back_step(d, dkv):
            j = here_at + d
            q_there = query_rows(
                jnp.concatenate(
                    [state_ref[j, inner + 16 :, :], back_ref[j, tokens + 16 :, :]], axis=0
                )
            )
            da_there = value_rows(back_ref[j, :tokens, :]).astype(BF)
            table = back_ref[j, tokens : tokens + 16, :].astype(F32)
            row = iota((tokens, tokens), 0)
            column = iota((tokens, tokens), 1)
            allowed = (seg_own == segl_ref[d]) & (row <= column + tokens * d)
            d_key = jnp.zeros((tokens, 128), F32)
            d_value = jnp.zeros((tokens, 128), F32)
            for k in range(2):

                def line(r):
                    return jnp.concatenate(
                        [
                            table[8 * i + r : 8 * i + r + 1] + table[8 * i + r + 4 : 8 * i + r + 5]
                            for i in range(tokens // 128)
                        ],
                        axis=1,
                    )

                mine = slice(k * tokens, (k + 1) * tokens)
                scores = mm_nt(kv_own, q_there[mine]) * score_scale
                probs = jnp.exp(jnp.where(allowed, scores - line(k), neg_big))
                d_scores = probs * (mm_nt(kv_own, da_there[mine]) - line(2 + k))
                d_key = d_key + mm(d_scores, q_there[mine])
                d_value = d_value + mm(probs, da_there[mine])
            return dkv + (d_key * score_scale + d_value)

        dkv = lax.fori_loop(0, nb_ref[1], back_step, jnp.zeros((tokens, 128), F32))
        dkv_ref[...] = (dkv * ck_ref[...] - halves_swapped(dkv) * sk_ref[...]).astype(BF)

    return kernel_call(
        "attend_back",
        body,
        [((tokens, 128), BF), ((tokens, 128), BF)],
        [
            here, every, states_back, every_back, delta, o2, q_own, segc, segrel, seglater, blocks,
            cos_q, sin_q, cos_kv, sin_kv,
        ],
        flops=2 * rows * tokens * 128 * 7 * n,
        ties=ties,
    )


def mixer_grad(here, every_back, state_in, dy, pad, hd, tok, segc, segrel, hp, conv_w):
    tokens, inner = dy.shape
    mix = pad.shape[1]

    def body(*refs):
        (
            here_ref, back_ref, state_ref, dy_ref, pad_ref, hd_ref, tok_ref, segc_ref, segr_ref,
            hp_ref, cw_ref, dmix_ref, tail_ref, edge_ref, ddt_ref, gconv_ref, ghead_ref,
            dconv_ref, dpad_ref, dxs_ref, slope_ref,
        ) = refs
        later = fold_states(back_ref, inner, here_ref[0], True)
        state = state_ref[...]
        tk = tok_ref[...]
        conv = convolved(pad_ref, cw_ref, tk, tokens)
        sg = sigmoid(conv)
        slope_ref[...] = sg * (1.0 + conv * (1.0 - sg))
        act_all = conv * sg
        x = act_all[:, :inner]
        b_mat = act_all[:, inner : inner + NS]
        c_mat = act_all[:, inner + NS :]
        dy_all = dy_ref[...].astype(F32)
        r, dt, cum = hd_ref[0], hd_ref[1], hd_ref[2]
        cum_t = cum.T
        last = cum[tokens - 1 :, :]
        to_last = jnp.where(tk[:, 5:6] > 0.5, jnp.exp(last - cum), 0.0)
        decay_in = jnp.exp(cum) * tk[:, 4:5]
        dt_wide = expand(dt, inner)
        last_wide = expand(to_last, inner)
        in_wide = expand(decay_in, inner)
        xs = x * dt_wide
        allowed = allowed_pair(segc_ref[...], segr_ref[0], tokens, 0)
        both = mm_nt(c_mat, b_mat)
        lane = iota((tokens, 128), 1)
        lane_row = iota((128, tokens), 0)
        d_both = jnp.zeros((tokens, tokens), F32)
        d_cum = jnp.zeros((tokens, 128), F32)
        d_cum_t = jnp.zeros((128, tokens), F32)
        for p in range(inner // 128):
            cols = slice(128 * p, 128 * (p + 1))
            xs_pair = xs[:, cols].astype(BF)
            dy_pair = dy_all[:, cols]
            pieces = []
            for k in range(2):
                h = 2 * p + k
                decay = within_decay(cum, cum_t, h, allowed)
                weight = decay * both
                mine = (lane >= HEAD_SIZE) if k else (lane < HEAD_SIZE)
                d_weight = mm_nt(jnp.where(mine, dy_pair, 0.0), xs_pair)
                d_both = d_both + d_weight * decay
                flow = d_weight * weight
                d_cum = d_cum + jnp.where(lane == h, jnp.sum(flow, axis=1, keepdims=True), 0.0)
                d_cum_t = d_cum_t + jnp.where(
                    lane_row == h, jnp.sum(flow, axis=0, keepdims=True), 0.0
                )
                pieces.append(mm_tn(weight, dy_pair))
            dxs_ref[:, cols] = jnp.where(lane < HEAD_SIZE, pieces[0], pieces[1])
        from_state = mm_nt(b_mat, later)
        d_xs = dxs_ref[...] + from_state * last_wide
        dy_in = dy_all * in_wide
        inflow = mm_nt(c_mat, state)
        d_c = mm(d_both, b_mat) + mm(dy_in, state)
        d_b = mm_tn(d_both, c_mat) + mm(xs * last_wide, later)
        carried = head_sum(from_state * xs * last_wide)
        d_cum = d_cum - d_cum_t.T + head_sum(dy_in * inflow) - carried
        row_sum = jnp.sum(later * state, axis=1, keepdims=True)
        pick = (iota((inner, 128), 0) // HEAD_SIZE == iota((inner, 128), 1)).astype(F32)
        d_decay = jnp.sum(row_sum * pick, axis=0, keepdims=True)
        d_last = jnp.sum(carried, axis=0, keepdims=True) + decay_in[tokens - 1 :, :] * d_decay
        d_cum = d_cum + jnp.where(iota((tokens, 128), 0) == tokens - 1, d_last, 0.0)
        upper = (iota((tokens, tokens), 0) <= iota((tokens, tokens), 1)).astype(F32)
        d_log = mm_hi(upper, d_cum)
        rate = jnp.exp(hp_ref[1:2, :])
        d_dt = head_sum(d_xs * x) - rate * d_log
        d_r = d_dt * sigmoid(r)
        ddt_ref[...] = d_r.astype(BF)
        g_bias = jnp.sum(d_r, axis=0, keepdims=True)
        g_log = -jnp.sum(d_log * dt, axis=0, keepdims=True) * rate
        g_skip = jnp.sum(head_sum(dy_all * x), axis=0, keepdims=True)
        row8 = iota((8, 128), 0)
        ghead_ref[...] = jnp.where(
            row8 == 0, g_bias, jnp.where(row8 == 1, g_log, jnp.where(row8 == 2, g_skip, 0.0))
        )
        skip = expand(hp_ref[...], inner)[2:3, :]
        dconv_ref[:, :inner] = (dy_all * skip + d_xs * dt_wide) * slope_ref[:, :inner]
        dconv_ref[:, inner : inner + NS] = d_b * slope_ref[:, inner : inner + NS]
        dconv_ref[:, inner + NS :] = d_c * slope_ref[:, inner + NS :]
        dpad_ref[...] = jnp.zeros((tokens + 16, mix), F32)
        gconv_ref[...] = jnp.zeros((8, mix), F32)
        dconv = dconv_ref[...]
        gconv_ref[KC : KC + 1, :] = jnp.sum(dconv, axis=0, keepdims=True)
        for j in range(KC):
            at = 16 - (KC - 1) + j
            used = dconv * tk[:, j : j + 1]
            gconv_ref[j : j + 1, :] = jnp.sum(
                used * pad_ref[at : at + tokens, :], axis=0, keepdims=True
            )
            dpad_ref[at : at + tokens, :] = (
                dpad_ref[at : at + tokens, :] + used * cw_ref[j : j + 1, :]
            )
        dmix_ref[...] = dpad_ref[16:, :].astype(BF)
        tail_ref[...] = dpad_ref[tokens:, :]
        edge_ref[...] = dpad_ref[8:16, :]

    return kernel_call(
        "mixer_grad",
        body,
        [
            ((tokens, mix), BF),
            ((16, mix), F32),
            ((8, mix), F32),
            ((tokens, 128), BF),
            ((8, mix), F32),
            ((8, 128), F32),
        ],
        [here, every_back, state_in, dy, pad, hd, tok, segc, segrel, hp, conv_w],
        scratch=[
            pltpu.VMEM((tokens, mix), F32),
            pltpu.VMEM((tokens + 16, mix), F32),
            pltpu.VMEM((tokens, inner), F32),
            pltpu.VMEM((tokens, mix), F32),
        ],
        flops=2 * tokens * tokens * 128 * 24,
    )


def grads_out(
    me, dgate, dmix, tail, next_edge, ddt, dq, dkv, wzx, wbc, wdt, wq, kvw, wa_count, ties
):
    tokens, inner = dgate.shape
    mix = dmix.shape[1]
    width = wzx[0].shape[1]
    rows = tokens // wa_count

    def body(
        me_ref, dgate_ref, dmix_ref, tail_ref, edge_ref, ddt_ref, dq_ref, dkv_ref,
        wzx_ref, wbc_ref, wdt_ref, wq_ref, kvw_ref, dx_ref, dbc_ref, *rest,
    ):
        blocks, full_ref = rest[:-1], rest[-1]
        ends = tail_ref[...] + jnp.concatenate([jnp.zeros((8, mix), F32), edge_ref[...]], axis=0)
        for ref, cols in ((dx_ref, slice(0, inner)), (dbc_ref, slice(inner, mix))):
            ref[: tokens - 16, :] = dmix_ref[: tokens - 16, cols]
            ref[tokens - 16 :, :] = ends[:, cols].astype(BF)
        full_ref[...] = (
            mm_nt(ddt_ref[...], wdt_ref[...])
            + mm_nt(dq_ref[...], wq_ref[...])
            + mm_nt(dkv_ref[...], kvw_ref[...])
            + mm_nt(dbc_ref[...], wbc_ref[...])
            + mm_nt(dgate_ref[...], wzx_ref[:, :inner])
            + mm_nt(dx_ref[...], wzx_ref[:, inner:])
        )
        rotated(me_ref, full_ref, blocks)

    return kernel_call(
        "grads_out",
        body,
        [((tokens, inner), BF), ((tokens, 2 * NS), BF), ((rows, width), F32)]
        + [((rows, width), BF)] * (wa_count - 1),
        [me, dgate, dmix, tail, next_edge, ddt, dq, dkv, wzx, wbc, wdt, wq, kvw],
        scratch=[pltpu.VMEM((tokens, width), F32)],
        flops=2 * tokens * width * (mix + 768),
        ties=ties,
    )


def all_rows(me, parts):
    n = len(parts)
    rows, width = parts[0].shape

    def body(*refs):
        for d in range(n):
            at = pl.multiple_of(lax.rem(refs[0][0] + n - d, n) * rows, rows)
            refs[-1][pl.ds(at, rows), :] = refs[1 + d][...].astype(F32)

    return kernel_call("all_rows", body, [((n * rows, width), F32)], [me, *parts])[0]


def held_back(arrays, ties):
    count = len(arrays)

    def body(*refs):
        pass

    return pl.pallas_call(
        body,
        in_specs=[pl.BlockSpec(memory_space=pl.ANY)] * (count + len(ties)),
        out_specs=[pl.BlockSpec(memory_space=pl.ANY)] * count,
        out_shape=[jax.ShapeDtypeStruct(a.shape, a.dtype) for a in arrays],
        input_output_aliases={i: i for i in range(count)},
        name="held_back",
    )(*arrays, *ties)


def pack_small(gains, convs, heads, inner, ties):
    width = gains[0].shape[1]
    mix = convs[0].shape[1]
    pieces = [(g, 0, 0, width) for g in range(len(gains))]
    at = len(gains)
    pieces += [(at + k, j, inner, mix) for k in range(len(convs)) for j in range(KC + 1)]
    pieces += [(at + k, j, 0, inner) for k in range(len(convs)) for j in range(KC + 1)]
    at += len(convs)
    pieces += [(at + k, j, 0, 128) for k in range(len(heads)) for j in range(8)]
    total = sum((end - start) // 128 for _, _, start, end in pieces)

    def body(*refs):
        row = 0
        for source, line, start, end in pieces:
            for c in range(start, end, 128):
                refs[-1][row : row + 1, :] = refs[source][line : line + 1, c : c + 128]
                row += 1

    return kernel_call(
        "pack_small", body, [((total, 128), F32)], [*gains, *convs, *heads], ties=ties
    )[0]


def per_device(
    x_in,
    d_out,
    segment_ids,
    norm_gains,
    w_zx,
    w_bc,
    w_dt,
    conv_x,
    conv_bc,
    dt_bias,
    a_log,
    d_skip,
    w_out,
    w_q,
    key_value_weight,
    w_ao,
    w_gu,
    w_down,
):
    seq_count = lax.axis_size("seq")
    wa_count = lax.axis_size("wa")
    tokens, width = x_in.shape
    rows = tokens // wa_count
    seq_here = lax.axis_index("seq")
    wa_here = lax.axis_index("wa")
    start_row = seq_here * tokens
    inner = w_zx.shape[3]
    heads = w_dt.shape[2]
    hidden = w_gu.shape[3]
    query_local = w_q.shape[2] // HEAD_SIZE
    group = QUERY_HEADS // KEY_VALUE_HEADS
    kv_head = wa_here * query_local // group
    me = wa_here.astype(jnp.int32).reshape(1)
    here = seq_here.astype(jnp.int32).reshape(1)

    seg_blocks = segment_ids.reshape(seq_count, tokens)
    seg_here = lax.dynamic_slice_in_dim(segment_ids, start_row, tokens)
    seg_padded = jnp.concatenate([jnp.full((KC - 1,), -1, jnp.int32), segment_ids])
    seg_edge = lax.dynamic_slice_in_dim(seg_padded, start_row, KC - 1)
    seg_full = jnp.concatenate([seg_edge, seg_here])
    steps = jnp.arange(seq_count, dtype=jnp.int32)
    segrel = jnp.where(
        (steps <= seq_here)[:, None], seg_blocks[(seq_here - steps) % seq_count], -1
    )
    seglater = jnp.where(
        (steps + seq_here < seq_count)[:, None], seg_blocks[(seq_here + steps) % seq_count], -1
    )
    blocks_used = jnp.stack(
        [
            1 + jnp.sum((segrel[1:, tokens - 1] == seg_here[0]).astype(jnp.int32)),
            1 + jnp.sum((seglater[1:, 0] == seg_here[tokens - 1]).astype(jnp.int32)),
        ]
    ).astype(jnp.int32)
    segrel = segrel[:, None, :]
    seglater = seglater[:, None, :]
    segc = seg_here[:, None]
    lane = iota((tokens, 128), 1)
    tok = jnp.zeros((tokens, 128), F32)
    conditions = [seg_full[j : j + tokens] == seg_here for j in range(KC)]
    conditions.append(seg_here == seg_edge[KC - 2])
    conditions.append(seg_here == seg_here[tokens - 1])
    for k, condition in enumerate(conditions):
        tok = jnp.where((lane == k) & condition[:, None], 1.0, tok)
    half = HEAD_SIZE // 2
    frequency = jnp.exp((lane % half).astype(F32) * (-math.log(theta) / half))
    angles = (start_row + iota((tokens, 128), 0)).astype(F32) * frequency
    cos_q = jnp.cos(angles)
    sin_q = jnp.where(lane % HEAD_SIZE < half, -1.0, 1.0) * jnp.sin(angles)
    cos_kv = jnp.where(lane < HEAD_SIZE, cos_q, 1.0)
    sin_kv = jnp.where(lane < HEAD_SIZE, sin_q, 0.0)

    wzx_all = w_zx.reshape(LAYER_COUNT, width, 2 * inner)
    wgu_all = w_gu.reshape(LAYER_COUNT, width, 2 * hidden)
    wdt_all = jnp.pad(w_dt, ((0, 0), (0, 0), (0, 128 - heads)))
    kvw_all = lax.dynamic_slice_in_dim(
        key_value_weight, kv_head * HEAD_SIZE, HEAD_SIZE, axis=3
    ).reshape(LAYER_COUNT, width, 2 * HEAD_SIZE)
    conv_all = jnp.pad(
        jnp.concatenate([conv_x, conv_bc], axis=2), ((0, 0), (0, 8 - (KC + 1)), (0, 0))
    )
    hp_all = jnp.pad(
        jnp.stack([dt_bias, a_log, d_skip], axis=1), ((0, 0), (0, 5), (0, 128 - heads))
    )

    def own_rows(array):
        return lax.dynamic_slice_in_dim(array, wa_here * rows, rows)

    h = own_rows(x_in)
    normed = norm_first(h, norm_gains[0, 0][None, :])
    saved = []
    for layer in range(LAYER_COUNT):
        wzx, wbc, wdt, wq = [(a, layer) for a in (wzx_all, w_bc, wdt_all, w_q)]
        kvw, conv_w, hp = [(a, layer) for a in (kvw_all, conv_all, hp_all)]
        wout, wao, wgu, wdown = [(a, layer) for a in (w_out, w_ao, wgu_all, w_down)]
        normed_parts = gather_wa(normed)
        edge = jnp.zeros((16, width), BF)
        for d, part in enumerate(normed_parts):
            edge = jnp.where((wa_here + wa_count - d) % wa_count == wa_count - 1, part[rows - 16 :], edge)
        edge = lax.ppermute(edge, "seq", [(i, i + 1) for i in range(seq_count - 1)])
        nat, gate, u, r_raw, kv, q_own = project(
            me, normed_parts, wzx, wbc, wdt, wq, kvw, cos_q, sin_q, cos_kv, sin_kv
        )
        every = gather_seq(kv)
        pad, act, hd, pack = mixer_front(
            edge, u, r_raw, wzx, wbc, conv_w, hp, tok
        )
        states = gather_seq(pack)
        y_local = mixer_within(act, hd, segc, segrel, hp, inner)
        o2, flat = attend(here, every, q_own, segc, segrel, blocks_used)
        state_in, y, gated, *parts = mixer_out(
            me, here, states, y_local, act, hd, tok, gate, flat, wout, wao, wa_count
        )
        mixed, normed_two = norm_step(scatter_wa(parts), h, norm_gains[layer, 1][None, :])
        n2, gu, act_ff, *parts = feed_forward(gather_wa(normed_two), wgu, wdown)
        saved.append(
            (h, nat, every, q_own, gate, pad, act, hd, o2, flat, state_in, y, gated,
             mixed, n2, gu, act_ff)
        )
        if layer + 1 < LAYER_COUNT:
            h, normed = norm_step(scatter_wa(parts), mixed, norm_gains[layer + 1, 0][None, :])

    last_parts = parts
    last_mixed = mixed

    grad = own_rows(d_out)
    grad_parts = [
        lax.dynamic_slice_in_dim(d_out, (wa_here + wa_count - d) % wa_count * rows, rows).astype(BF)
        for d in range(wa_count)
    ]
    sums = [None] * LAYER_COUNT
    small = [None] * LAYER_COUNT
    for layer in reversed(range(LAYER_COUNT)):
        wzx, wbc, wdt, wq = [(a, layer) for a in (wzx_all, w_bc, wdt_all, w_q)]
        kvw, conv_w, hp = [(a, layer) for a in (kvw_all, conv_all, hp_all)]
        wout, wao, wgu, wdown = [(a, layer) for a in (w_out, w_ao, wgu_all, w_down)]
        (h_in, nat, every, q_own, gate, pad, act, hd, o2, flat, state_in, y, gated,
         mixed, n2, gu, act_ff) = saved[layer]
        gb, dgu, *parts = feed_back(grad_parts, gu, wgu, wdown)
        parts = scatter_wa(parts)
        ff_pairs = [(gb, act_ff), (n2, dgu)]
        grad_ties = []
        if not layer:
            (early,), token = weight_grads(here, [(ff_pairs, False)], seq_count)
            grad_ties = [token]
        d_mixed, mixed_b, gain_two = norm_back(
            parts, mixed, norm_gains[layer, 1][None, :], grad, grad_ties
        )
        mixed_parts = gather_wa(mixed_b)
        mb, dy, dgate, pack, da, delta = mixer_grad_in(
            me, mixed_parts, wout, wao, gate, y, act, hd, tok, o2, q_own
        )
        states_back = gather_seq(pack)
        every_back = gather_seq(da)
        mix_pairs = [(mb, gated), (mb, flat), (nat, dgate)]
        if layer == LAYER_COUNT - 1:
            out_parts = scatter_wa(held_back(last_parts, [delta]))
            out_ties = out_parts[1:]
        if not layer:
            early = held_back(list(early), [joint, every_back])
            out_ties = list(early)
            sum_ff = scatter_rows(early)
        dq, dkv = attend_back(
            here, every, states_back, every_back, delta, o2, q_own, segc, segrel, seglater,
            blocks_used, cos_q, sin_q, cos_kv, sin_kv, inner, out_ties,
        )
        dmix, tail, edge_grad, ddt, gconv, ghead = mixer_grad(
            here, states_back, state_in, dy, pad, hd, tok, segc, segrel, hp, conv_w
        )
        next_edge = lax.ppermute(
            edge_grad, "seq", [(i + 1, i) for i in range(seq_count - 1)]
        )
        dx, dbc, *parts = grads_out(
            me, dgate, dmix, tail, next_edge, ddt, dq, dkv, wzx, wbc, wdt, wq, kvw, wa_count, []
        )
        parts = scatter_wa(parts)
        every_pairs = [(nat, dbc), (nat, dkv)]
        in_pairs = [(nat, dx), (nat, dq), (nat, ddt)]
        if layer:
            (joint,), token = weight_grads(
                here, [(ff_pairs + mix_pairs + every_pairs + in_pairs, False)], seq_count
            )
            back_ties = [token]
            joint = scatter_rows(joint)
            cuts = [3 * hidden, 2 * inner + 128, 2 * NS + 128, inner + 256]
            ends = [sum(cuts[: k + 1]) for k in range(4)]
            sum_ff, sum_mix, sum_every, sum_in = [
                joint[:, end - size : end] for end, size in zip(ends, cuts)
            ]
            h = norm_step(out_parts, last_mixed, norm_gains[layer, 0][None, :], [parts[1]])[0]
        else:
            (joint,), token = weight_grads(
                here, [(every_pairs + mix_pairs + in_pairs, False)], seq_count
            )
            back_ties = [token]
            joint = scatter_rows(joint)
            cuts = [2 * NS + 128, 2 * inner + 128, inner + 256]
            ends = [sum(cuts[: k + 1]) for k in range(3)]
            sum_every, sum_mix, sum_in = [
                joint[:, end - size : end] for end, size in zip(ends, cuts)
            ]
        grad, grad_b, gain_one = norm_back(
            parts, h_in, norm_gains[layer, 0][None, :], d_mixed, back_ties
        )
        grad_parts = gather_wa(grad_b)
        sums[layer] = (sum_ff, sum_mix, sum_in, sum_every)
        small[layer] = (gain_one, gain_two, gconv, ghead)
    x_parts = gather_wa(held_back([h.astype(BF)], grad_parts[1:])[0])
    shared_late = gather_wa(held_back([sums[1][3]], x_parts[1:])[0])
    x_out = all_rows(me, x_parts)
    d_x = all_rows(me, grad_parts)

    mix = inner + 2 * NS
    local = pack_small(
        [small[layer][k] for layer in range(LAYER_COUNT) for k in (0, 1)],
        [small[layer][2] for layer in range(LAYER_COUNT)],
        [small[layer][3] for layer in range(LAYER_COUNT)],
        inner,
        grad_parts[1:],
    )
    local = jnp.sum(gather_seq(local), axis=0)
    gain_rows = 2 * LAYER_COUNT * width // 128
    shared_rows = gain_rows + LAYER_COUNT * (KC + 1) * 2 * NS // 128
    shared = sum(gather_wa(local[:shared_rows]))
    gain_sum = shared[:gain_rows].reshape(LAYER_COUNT, 2, width)
    g_conv_bc = shared[gain_rows:].reshape(LAYER_COUNT, KC + 1, 2 * NS)
    local = local[shared_rows:]
    conv_rows = LAYER_COUNT * (KC + 1) * (inner // 128)
    g_conv_x = local[:conv_rows].reshape(LAYER_COUNT, KC + 1, inner)
    head_part = local[conv_rows:].reshape(LAYER_COUNT, 8, 128)

    every_parts = [
        jnp.stack(pair) for pair in zip(gather_wa(sums[0][3]), shared_late)
    ]
    g_bc = sum(part[:, :, : 2 * NS].astype(F32) for part in every_parts)
    kv_columns = []
    for head in range(KEY_VALUE_HEADS):
        total = 0.0
        for d, part in enumerate(every_parts):
            source = (wa_here + wa_count - d) % wa_count * query_local // group
            total = total + jnp.where(source == head, part[:, :, 2 * NS :].astype(F32), 0.0)
        kv_columns.append(total.reshape(total.shape[0], total.shape[1], 2, HEAD_SIZE))
    g_kv = jnp.concatenate(kv_columns, axis=3)

    block = sums[0][0].shape[0]

    def stacked(pick):
        return jnp.stack([pick(s).astype(F32) for s in sums])

    g_down = stacked(lambda s: s[0][:, :hidden].T)
    g_gu = stacked(lambda s: s[0][:, hidden:].reshape(block, 2, hidden))
    ends = inner + 128
    g_out = stacked(lambda s: s[1][:, :inner].T)
    g_ao = stacked(lambda s: s[1][:, inner:ends].T)
    g_zx = stacked(
        lambda s: jnp.stack(
            [s[1][:, ends : ends + inner].astype(F32), s[2][:, :inner].astype(F32)], axis=1
        )
    )
    g_q = stacked(lambda s: s[2][:, inner:ends])
    g_dt = stacked(lambda s: s[2][:, ends : ends + heads])
    return (
        x_out,
        d_x,
        gain_sum[:, 0],
        gain_sum[:, 1],
        g_zx,
        g_bc,
        g_dt,
        g_conv_x,
        g_conv_bc,
        head_part[:, 0, :heads],
        head_part[:, 1, :heads],
        head_part[:, 2, :heads],
        g_out,
        g_q,
        g_kv,
        g_ao,
        g_gu,
        g_down,
    )


def solution(mesh):
    return jax.shard_map(
        per_device,
        mesh=mesh,
        in_specs=(
            P("seq", None),
            P("seq", None),
            P(),
            P(),
            P(None, None, None, "wa"),
            P(),
            P(None, None, "wa"),
            P(None, None, "wa"),
            P(),
            P(None, "wa"),
            P(None, "wa"),
            P(None, "wa"),
            P(None, "wa", None),
            P(None, None, "wa"),
            P(),
            P(None, "wa", None),
            P(None, None, None, "wa"),
            P(None, "wa", None),
        ),
        out_specs=(
            P("seq", None),
            P("seq", None),
            P(),
            P(),
            P(None, "seq", None, "wa"),
            P(None, "seq", None),
            P(None, "seq", "wa"),
            P(None, None, "wa"),
            P(),
            P(None, "wa"),
            P(None, "wa"),
            P(None, "wa"),
            P(None, "wa", "seq"),
            P(None, "seq", "wa"),
            P(None, "seq", None, None),
            P(None, "wa", "seq"),
            P(None, "seq", None, "wa"),
            P(None, "wa", "seq"),
        ),
        check_vma=False,
    )
```
